128 devices in a mesh: mem: 8 (over z_lo, x), tile: 16 (over y, z_hi, core).
Axes of the slice: x: 4, y: 4, z: 4 (z_hi: 2, z_lo: 2; z = z_hi * 2 + z_lo), core: 2. Of those that a mesh axis runs over, the one named last changes fastest.
Arguments:
- alpha: bfloat16 [80, 8, 512, 384], P('mem', None, 'tile'), may hold values from -6 to 6
- perturbation: bfloat16 [80, 8, 512, 384], P('mem', None, 'tile'), may hold values from -6 to 6
- cotangent: bfloat16 [8, 786432], P('mem', 'tile'), may hold values from -6 to 6
- decay_y: float32 [8, 512], P(None, 'tile'), may hold values from 0.4 to 1
- decay_x: float32 [8, 384], replicated, may hold values from 0.4 to 1
- group_members: int32 [8], replicated, may hold values from 2 to 10, as said below
- interp_weight: bfloat16 [16, 16, 128, 32, 128], P('tile'), may hold values from -0.5 to 0.5
- pair_count: int32 [16, 16], replicated, may hold values from 0 to 128, as said below
- src_index: int32 [16, 16, 128], replicated, may hold values from 0 to 383
- dst_index: int32 [16, 16, 128], replicated, may hold values from 0 to 383
Outputs:
- increment: float32 [8, 786432], P('mem', 'tile')
- alpha_grad: float32 [80, 8, 512, 384], P('mem', None, 'tile')
The draws below stay inside these ranges and needn't reach their ends.
Inputs may be any that keep to these rules, and one draw needn't show every extreme that they name: Slots 0 to group_members[g] - 1 of group g hold live members; some group holds 10. `pair_count`: one destination tile has 128 live slots from every source tile.
All inputs are finite; a program needn't handle non-finite values.
Results may differ from the reference program's by a relative error of at most 0.0029.
Values may be sent and summed in bfloat16 or wider, within the bound.
A program may use at most 128 MiB of HBM per device.

```python
import math
import jax
import jax.numpy as jnp
from jax import lax

MSLOT = 10
VERTICAL_LAYERS = 8
NXL = 384
BS = 32
BD = 128
CAP = 128
MEMBERS = 80
NY = 512
SBLK = 384
HCELL = 49152
DBLK = 384
NH = 786432
N_MEM = 8
N_TILE = 16


def decay_table(key, interval_extent, fast_share):
    derived_seeds = jax.random.split(key, 6)
    fast_levels = jax.random.uniform(derived_seeds[0], (VERTICAL_LAYERS, 1)) < fast_share
    slow_rate = jnp.exp(jax.random.uniform(derived_seeds[1], (VERTICAL_LAYERS, 1), minval=math.log(1.0 / 60.0), maxval=math.log(1.0 / 12.0)))
    quick_damping_speed = jnp.exp(jax.random.uniform(derived_seeds[2], (VERTICAL_LAYERS, 1), minval=math.log(1.0 / 40.0), maxval=math.log(1.0 / 20.0)))
    jitter = jnp.exp(jax.random.uniform(derived_seeds[3], (VERTICAL_LAYERS, interval_extent), minval=-0.7, maxval=0.7))
    damping_multipliers = jnp.where(fast_levels, quick_damping_speed, slow_rate) * jitter
    pulse_interval_flags = jax.random.uniform(derived_seeds[4], (VERTICAL_LAYERS, interval_extent)) < 3.0 / interval_extent
    pulse_keep_flags = jax.random.uniform(derived_seeds[5], (VERTICAL_LAYERS, interval_extent), minval=0.5, maxval=0.8)
    return ((1.0 - damping_multipliers) * jnp.where(pulse_interval_flags, pulse_keep_flags, 1.0)).astype(jnp.float32)


def draw_decay_y(key, part):
    key = jax.random.fold_in(key, 21)
    fast_share = 0.5
    return decay_table(key, NY, fast_share)


def draw_decay_x(key, part):
    key = jax.random.fold_in(key, 22)
    fast_share = 0.5
    return decay_table(key, NXL, fast_share)


def draw_group_members(key, part):
    key = jax.random.fold_in(key, 31)
    derived_seeds = jax.random.split(key, 2)
    raw_counts = jax.random.randint(derived_seeds[0], (N_MEM,), 2, MSLOT + 1)
    full_group = jax.random.randint(derived_seeds[1], (), 0, N_MEM)
    return jnp.where(jnp.arange(N_MEM) == full_group, MSLOT, raw_counts).astype(jnp.int32)


def draw_pair_count(key, part):
    key = jax.random.fold_in(key, 41)
    derived_seeds = jax.random.split(key, 3)
    level_pick = jax.random.randint(derived_seeds[0], (N_TILE, 1), 0, 3)
    row_limit = CAP // 4 * (level_pick + 2)
    raw_counts = jax.random.randint(derived_seeds[1], (N_TILE, N_TILE), 0, 1 << 20) % (row_limit + 1)
    full_row = jax.random.randint(derived_seeds[2], (), 0, N_TILE)
    return jnp.where(jnp.arange(N_TILE)[:, None] == full_row, CAP, raw_counts).astype(jnp.int32)


def draw_src_index(key, part):
    key = jax.random.fold_in(key, 51)
    return jax.random.randint(key, (N_TILE, N_TILE, CAP), 0, SBLK).astype(jnp.int32)


def draw_dst_index(key, part):
    key = jax.random.fold_in(key, 61)
    return jax.random.randint(key, (N_TILE, N_TILE, CAP), 0, DBLK).astype(jnp.int32)


def raised(array, own_key, source, target, parts, factor):
    def block_of(position):
        return (jnp.arange(array.shape[position]) // (array.shape[position] // parts)).reshape((-1,) + (1,) * (array.ndim - 1 - position))

    near = jax.random.permutation(own_key, parts)[block_of(target)]
    other_side = (block_of(target) + parts // 2) % parts
    return jnp.where((block_of(source) == near) | (block_of(source) == other_side), factor * array, array)


def steps_of(stream_key, shape, cuts, least, largest):
    gain = 1.0
    for position, blocks in cuts:
        heights = jax.random.uniform(jax.random.fold_in(jax.random.fold_in(stream_key, 6), position), (blocks,), jnp.float32, least / len(cuts), largest / len(cuts))
        gain = gain * jnp.repeat(jnp.exp(heights), shape[position] // blocks).reshape((-1,) + (1,) * (len(shape) - 1 - position))
    return gain


def gaussian(stream_key, extent, scale, most, shards=(), kind=jnp.bfloat16):
    values = scale * jax.random.normal(stream_key, extent, jnp.float32)
    if shards:
        values = values * steps_of(stream_key, extent, shards, -0.22, 0.18)
    return jnp.clip(values, -most, most).astype(kind)


def heavy_noise(key, dims, width, most, cuts, heavy, kind=jnp.bfloat16):
    array = width * jax.random.normal(key, dims, jnp.float32)
    if cuts:
        array = array * steps_of(key, dims, cuts, -0.22, 0.18)
    return jnp.clip(raised(array, jax.random.fold_in(key, 3), *heavy), -most, most).astype(kind)


def setup_inputs(seed: int = 0) -> dict:
    arg_keys = jax.random.split(jax.random.key(seed), 11)
    return {
        "alpha": gaussian(arg_keys[0], (MEMBERS, VERTICAL_LAYERS, NY, NXL), 1.0, 6.0, ((0, 8), (2, 16))),
        "perturbation": heavy_noise(arg_keys[1], (MEMBERS, VERTICAL_LAYERS, NY, NXL), 1.0, 6.0, ((0, 8), (2, 16)), (0, 1, 8, 2.0)),
        "cotangent": gaussian(arg_keys[2], (VERTICAL_LAYERS, NH), 1.0, 6.0, ((0, 8), (1, 16))),
        "decay_y": draw_decay_y(jax.random.fold_in(arg_keys[10], 71), 0),
        "decay_x": draw_decay_x(jax.random.fold_in(arg_keys[10], 71), 0),
        "group_members": draw_group_members(jax.random.fold_in(arg_keys[10], 71), 0),
        "interp_weight": gaussian(arg_keys[6], (N_TILE, N_TILE, CAP, BS, BD), (4 * BS) ** -0.5, 0.5, ((0, 16),)),
        "pair_count": draw_pair_count(jax.random.fold_in(arg_keys[10], 71), 0),
        "src_index": draw_src_index(jax.random.fold_in(arg_keys[10], 71), 0),
        "dst_index": draw_dst_index(jax.random.fold_in(arg_keys[10], 71), 0),
    }


def coefficient(decay):
    return ((1.0 - decay * decay) ** 3 / (1.0 + decay * decay)) ** 0.25

def recursive_filter(values, decay):
    scaling = coefficient(decay)

    def forward(carried, record):
        entry_value, decay_rate, weight = record
        carried = decay_rate * carried + weight * entry_value
        return (carried, carried)
    zero_state = jnp.zeros(values.shape[1:], jnp.float32)
    _, smooth = lax.scan(forward, zero_state, (values, decay, scaling))

    def backward(carried, record):
        entry_value, decay_rate = record
        running = entry_value + carried
        return (decay_rate * running, running)
    _, summed = lax.scan(backward, zero_state, (smooth, decay), reverse=True)
    return scaling * summed

def filter_rows(values, decay_y):
    turned = jnp.transpose(values, (1, 0, 2))
    result = recursive_filter(turned, jnp.transpose(decay_y)[:, :, None])
    return jnp.transpose(result, (1, 0, 2))

def filter_columns(values, decay_x):
    turned = jnp.transpose(values, (2, 0, 1))
    result = recursive_filter(turned, jnp.transpose(decay_x)[:, :, None])
    return jnp.transpose(result, (1, 2, 0))

def reference(alpha, perturbation, cotangent, decay_y, decay_x, group_members, interp_weight, pair_count, src_index, dst_index):
    slot_ids = jnp.arange(MSLOT, dtype=jnp.int32)
    live_slots = (slot_ids[None, :] < group_members[:, None]).reshape(-1).astype(jnp.float32)
    member_scale = 1.0 / jnp.sqrt(jnp.sum(group_members).astype(jnp.float32) - 1.0)

    def add_member(running, record):
        values, pert_field, live_flag = record
        smooth = filter_columns(filter_rows(values.astype(jnp.float32), decay_y), decay_x)
        return (running + live_flag * pert_field.astype(jnp.float32) * smooth, None)
    running, _ = lax.scan(add_member, jnp.zeros((VERTICAL_LAYERS, NY, NXL), jnp.float32), (alpha, perturbation, live_slots))
    low_values = (running * member_scale).astype(jnp.bfloat16).reshape(VERTICAL_LAYERS, N_TILE, SBLK, BS)
    cap_ids = jnp.arange(CAP, dtype=jnp.int32)
    tile_ids = jnp.arange(N_TILE, dtype=jnp.int32)

    def forward_tile(record):
        weights, counts, sources, targets = record
        slot_mask = (cap_ids[None, :] < counts[:, None]).astype(jnp.float32)
        picked = low_values[:, tile_ids[:, None], sources]
        contrib = jnp.einsum('lscb,scbe->scle', picked.astype(jnp.float32), weights.astype(jnp.float32))
        contrib = contrib * slot_mask[:, :, None, None]
        summed = jax.ops.segment_sum(contrib.reshape(N_TILE * CAP, VERTICAL_LAYERS, BD), targets.reshape(-1), num_segments=DBLK)
        return jnp.transpose(summed, (1, 0, 2)).reshape(VERTICAL_LAYERS, HCELL)
    pieces = lax.map(forward_tile, (interp_weight, pair_count, src_index, dst_index))
    increment = jnp.transpose(pieces, (1, 0, 2)).reshape(VERTICAL_LAYERS, NH)
    grad_tiles = jnp.transpose(cotangent.reshape(VERTICAL_LAYERS, N_TILE, DBLK, BD), (1, 0, 2, 3))

    def backward_tile(running, record):
        weights, counts, sources, targets, grad_tile = record
        slot_mask = (cap_ids[None, :] < counts[:, None]).astype(jnp.float32)
        picked = jnp.transpose(grad_tile, (1, 0, 2))[targets]
        contrib = jnp.einsum('scle,scbe->sclb', picked.astype(jnp.float32), weights.astype(jnp.float32))
        contrib = contrib * slot_mask[:, :, None, None]
        row_ids = (tile_ids[:, None] * SBLK + sources).reshape(-1)
        added = jax.ops.segment_sum(contrib.reshape(N_TILE * CAP, VERTICAL_LAYERS, BS), row_ids, num_segments=N_TILE * SBLK)
        return (running + added, None)
    back_low, _ = lax.scan(backward_tile, jnp.zeros((N_TILE * SBLK, VERTICAL_LAYERS, BS), jnp.float32), (interp_weight, pair_count, src_index, dst_index, grad_tiles))
    back_low = jnp.transpose(back_low, (1, 0, 2)).reshape(VERTICAL_LAYERS, NY, NXL)

    def member_grad(record):
        pert_field, live_flag = record
        smooth = filter_rows(filter_columns(pert_field.astype(jnp.float32) * back_low, decay_x), decay_y)
        return live_flag * member_scale * smooth
    alpha_grad = lax.map(member_grad, (perturbation, live_slots))
    return (increment, alpha_grad)
```

```python
import jax
import jax.numpy as jnp
from jax import lax
from jax.experimental import pallas as pl
from jax.experimental.pallas import tpu as pltpu
from jax.sharding import PartitionSpec as P

MESH = pl.DeviceIdType.MESH
F32 = jnp.float32
BF16 = jnp.bfloat16

LEVELS = 8
TILES = 16
ROWS = 32
COLS = 384
HALF = 5
PACK = HALF * ROWS
SLOTS = 128
BLK = 32
QROWS = ROWS * COLS // 128
DROWS = 384
GROUP = 4


def dot(a, b):
    return lax.dot_general(a, b, (((1,), (0,)), ((), ())), preferred_element_type=F32)


def dot_nt(a, b):
    return lax.dot_general(a, b, (((1,), (1,)), ((), ())), preferred_element_type=F32)


def split(x):
    high = x.astype(BF16)
    return high, (x - high.astype(F32)).astype(BF16)


def coefficient(a):
    t = 1.0 - a * a
    ratio = (t * t * t) / (1.0 + a * a)
    return jnp.where(ratio > 0.0, jnp.sqrt(jnp.sqrt(jnp.maximum(ratio, 1e-37))), 0.0)


def scans(a, pos, width, segment):
    logs = jnp.log(a)
    steps = [1 << b for b in range(16) if (1 << b) < segment]
    for k in steps:
        logs = logs + jnp.where(pos >= k, pltpu.roll(logs, k, 1), 0.0)
    rate = jnp.where(pos < segment - 1, pltpu.roll(a * a, width - 1, 1), 0.0)
    h = jnp.ones_like(a)
    for k in steps:
        h = h + rate * pltpu.roll(h, width - k, 1)
        rate = rate * pltpu.roll(rate, width - k, 1)
    return logs, h


def smooth(fields, carries, mt, pb, qb, kk, precise):
    p3 = jnp.concatenate([pb] * 3, axis=1)
    q3 = jnp.concatenate([qb] * 3, axis=1)
    rows = []
    for field, carry in zip(fields, carries):
        hi, *lo = field
        stack = jnp.concatenate([hi, hi, *lo], axis=0)
        y = dot(mt[:, 0 : stack.shape[0]], stack)
        for m in range(HALF):
            rows.append(
                y[ROWS * m : ROWS * m + ROWS]
                + p3 * carry[m : m + 1, :]
                + q3 * carry[8 + m : 9 + m, :]
            )
    y = jnp.concatenate(rows, axis=0)
    if not precise:
        yh = y.astype(BF16)
        return dot(jnp.concatenate([yh, yh], axis=1), kk)
    yh, yl = split(y)
    return dot(jnp.concatenate([yh, yh, yl], axis=1), jnp.concatenate([kk, kk[0:COLS]], axis=0))


def members(gm_ref):
    own = gm_ref[lax.axis_index("mem")]
    total = gm_ref[0]
    for i in range(1, LEVELS):
        total = total + gm_ref[i]
    scale = 1.0 / jnp.sqrt(jnp.full((1, COLS), total.astype(F32) - 1.0, F32))
    return scale, [jnp.where(m < own, 1.0, 0.0).astype(F32) for m in range(2 * HALF)]


def grad_kernel(
    gm_ref, pert_ref, back_ref, de_ref, mt_ref, pb_ref, qb_ref, kk_ref, inc_ref,
    inc_out, grad_ref,
):
    scale, live = members(gm_ref)
    fields = []
    for half in range(2):
        x = pert_ref[HALF * half : HALF * half + HALF, 0].astype(F32) * back_ref[...]
        fields.append(split(x.reshape(PACK, COLS)))
    y = smooth(
        fields, (de_ref[0], de_ref[1]), mt_ref[0], pb_ref[0], qb_ref[0], kk_ref[0], False
    )
    for m in range(2 * HALF):
        grad_ref[m, 0] = y[ROWS * m : ROWS * m + ROWS] * (scale * live[m])

    rows = DROWS // LEVELS
    first = pl.program_id(0) * rows
    x = inc_ref[pl.ds(pl.multiple_of(first, rows), rows), :]
    for r in range(rows):
        at = pl.multiple_of((first + r) * 128, 128)
        inc_out[0:1, pl.ds(at, 128)] = x[r : r + 1, :]


def kernel(
    alpha_hbm, pert_hbm, cot_hbm, dy_ref, dx_ref, gm_ref, w_hbm, pc_ref, src_hbm, dst_hbm,
    inc_hbm, back_hbm, de_hbm, mt_hbm, pb_hbm, qb_hbm, kk_hbm,
    alpha_v, pert_v, cot_raw, cot_v, w_v, src_v, dst_v,
    rep_v, yt, ytail, xt, mt, zf, zadd, pb, qb, kk,
    zs, zr, zo, de, zs2, zr2, zo2, de2,
    ss, sr, bq, back, ps, pr, lq, low, lows, inc_v, scol_v, dcol_v,
    in_sem, w_sem, out_sem, zs_s, zs_r, zo_s, zo_r, zs2_s, zs2_r, zo2_s, zo2_r,
    sp_s, sp_r, rs_s, rs_r, lo_s, lo_r, bk_s, bk_r,
):
    g = lax.axis_index("mem")
    t = lax.axis_index("tile")

    def tile_peer(k):
        return lax.rem(t + k, TILES)

    def tile_back(k):
        return lax.rem(t + TILES - k, TILES)

    def mem_peer(k):
        return lax.rem(g + k, LEVELS)

    def to_tile(src, dst, ssem, rsem, s):
        return pltpu.make_async_remote_copy(
            src_ref=src, dst_ref=dst, send_sem=ssem, recv_sem=rsem,
            device_id={"tile": s}, device_id_type=MESH,
        )

    def to_mem(src, dst, ssem, rsem, s):
        return pltpu.make_async_remote_copy(
            src_ref=src, dst_ref=dst, send_sem=ssem, recv_sem=rsem,
            device_id={"mem": s}, device_id_type=MESH,
        )

    loads = [
        pltpu.make_async_copy(alpha_hbm, alpha_v, in_sem.at[0]),
        pltpu.make_async_copy(cot_hbm, cot_raw, in_sem.at[1]),
        pltpu.make_async_copy(src_hbm.at[t], src_v, in_sem.at[2]),
        pltpu.make_async_copy(dst_hbm.at[t], dst_v, in_sem.at[3]),
        pltpu.make_async_copy(pert_hbm, pert_v, in_sem.at[4]),
    ]

    def wait_all(buf, sem, count):
        part = buf.at[pl.ds(0, count - 1)]
        pltpu.make_async_copy(part, part, sem).wait()

    def w_load(s):
        return pltpu.make_async_copy(w_hbm.at[0, s], w_v.at[s], w_sem.at[s])

    for c in loads[:4]:
        c.start()

    @pl.loop(1, TILES + 1)
    def _(k):
        w_load(tile_peer(k)).start()

    loads[4].start()

    barrier = pltpu.get_barrier_semaphore()

    @pl.loop(1, TILES)
    def _(k):
        pl.semaphore_signal(barrier, inc=1, device_id={"tile": tile_peer(k)}, device_id_type=MESH)

    @pl.loop(1, LEVELS)
    def _(k):
        pl.semaphore_signal(barrier, inc=1, device_id={"mem": mem_peer(k)}, device_id_type=MESH)

    scale, live = members(gm_ref)

    for k in range(16):
        rep_v[:, 32 * k : 32 * k + 32] = dy_ref[...]
    a = rep_v[...]
    pos = lax.broadcasted_iota(jnp.int32, (8, 512), 1) & 31
    logs, h = scans(a, pos, 512, ROWS)
    c = coefficient(a)
    ltot = jnp.broadcast_to(logs[:, 31:32], (8, 512))
    lane512 = lax.broadcasted_iota(jnp.int32, (8, 512), 1)
    hsum = jnp.sum(jnp.where(lane512 < 32, jnp.exp(2.0 * logs), 0.0), axis=1, keepdims=True)
    for f, x in enumerate(
        (logs, c, c * h, c * h * jnp.exp(logs), c * jnp.exp(ltot - logs))
    ):
        yt[:, f, :] = x
    yt[:, 5:8, :] = jnp.zeros((LEVELS, 3, 512), F32)
    ytail[:, 0, :] = jnp.broadcast_to(jnp.exp(ltot[:, 0:1]), (LEVELS, COLS))
    ytail[:, 1, :] = jnp.broadcast_to(hsum, (LEVELS, COLS))
    lane_y = lax.broadcasted_iota(jnp.int32, (ROWS, 512), 1)
    lower = lax.broadcasted_iota(jnp.int32, (ROWS, 512), 0) >= (lane_y & 31)
    zr_i = lax.broadcasted_iota(jnp.int32, (16, 256), 0)
    zc_i = lax.broadcasted_iota(jnp.int32, (16, 256), 1) >> 5
    row16 = lax.broadcasted_iota(jnp.int32, (16, COLS), 0)

    def columns(rows):
        width = rows.shape[1]
        return jnp.transpose(jnp.concatenate([rows, jnp.zeros((120, width), F32)], axis=0))

    @pl.loop(0, LEVELS)
    def _(l):
        rows = yt[l]
        cols = columns(rows[:, 0:128])[0:ROWS]

        def col(f):
            return cols[:, f : f + 1]

        e = jnp.exp(-jnp.abs(col(0) - rows[0:1]))
        m = e * jnp.where(lower, col(2) * rows[1:2], col(1) * rows[2:3])
        part = lane_y >> 5
        mh, ml = split(m)
        m = jnp.where((part >= HALF) & (part < 2 * HALF), ml.astype(F32), mh.astype(F32))
        part = jnp.where(part < 3 * HALF, part % HALF, -1)
        for i in range(HALF):
            mt[l, ROWS * i : ROWS * i + ROWS, :] = jnp.where(part == i, m, 0.0).astype(BF16)
        z = jnp.where(zr_i == zc_i, rows[4:5, 0:256], 0.0) + jnp.where(zr_i == zc_i + 8, rows[3:4, 0:256], 0.0)
        z = jnp.where(zc_i < HALF, z, 0.0)
        zh, zl = split(z)
        zf[l, 0:16, :] = zh[:, 0:PACK]
        zf[l, 16:32, :] = zl[:, 0:PACK]
        tail = ytail[l]
        zadd[l] = jnp.where(row16 == 5, tail[0:1], 0.0) + jnp.where(row16 == 6, tail[1:2], 0.0)
        pb[l] = jnp.broadcast_to(col(3), (ROWS, 128))
        qb[l] = jnp.broadcast_to(col(4), (ROWS, 128))

    low[:, QROWS:128, :] = jnp.zeros((TILES, 128 - QROWS, 128), BF16)

    loads[1].wait()

    @pl.loop(0, DROWS // 16)
    def _(i):
        rows = [
            cot_raw[:, pl.ds(pl.multiple_of(2048 * i + 128 * r, 128), 128)].astype(F32)
            for r in range(16)
        ]
        cot_v[pl.ds(pl.multiple_of(16 * i, 16), 16), :] = jnp.concatenate(rows, axis=0).astype(BF16)

    loads[0].wait()
    pl.semaphore_wait(barrier, TILES - 1 + LEVELS - 1)

    def alpha_of(l, half):
        return alpha_v[HALF * half : HALF * half + HALF, l].reshape(PACK, COLS)

    def source(l, hi, lo=None):
        r = dot(zf[l], hi)
        z = r[0:16] + r[16:32] + zadd[l]
        if lo is not None:
            z = z + dot(zf[l, 0:16, :], lo)
        return z

    def sources(field, zs, zr, s_s, s_r, first, last):
        @pl.loop(first, last)
        def _(k):
            found = []
            for i in range(2):
                l = lax.rem(t // 2 + 2 * k + i + 1, LEVELS)
                for half in range(2):
                    found.append((2 * l + half, source(l, *field(l, half))))
            for tt, z in found:
                zs[tt] = z
            for tt, _z in found:

                @pl.when(tt != t)
                def _():
                    to_tile(zs.at[tt], zr.at[t], s_s, s_r, tt).start()

        if last == LEVELS // 2:
            zr[t] = zs[t]

    sources(lambda l, half: (alpha_of(l, half),), zs, zr, zs_s, zs_r, 0, LEVELS // 2)

    def recursion(zr, zo, de, s_r, o_s, o_r):
        wait_all(zr, s_r, TILES)
        d = jnp.zeros((8, COLS), F32)
        downs = []
        for s in range(TILES):
            downs.append(d)
            zo[s, 0:8, :] = d
            d = zr[s, 5:6, :] * d + zr[s, 0:8, :]
        e = jnp.zeros((8, COLS), F32)
        for s in reversed(range(TILES)):
            zo[s, 8:16, :] = e
            e = zr[s, 5:6, :] * e + (zr[s, 8:16, :] + zr[s, 6:7, :] * downs[s])

        @pl.loop(1, TILES)
        def _(k):
            s = tile_peer(k)
            to_tile(zo.at[s], de.at[t], o_s, o_r, s).start()

        de[t] = zo[t]

    lane1 = lax.broadcasted_iota(jnp.int32, (1, 128), 1)
    lane = lax.broadcasted_iota(jnp.int32, (SLOTS, 128), 1)
    lgroup = lane >> 5
    slot_id = lax.broadcasted_iota(jnp.int32, (SLOTS, 128), 0)
    r16 = lax.broadcasted_iota(jnp.int32, (16, 128), 0) - (
        lax.broadcasted_iota(jnp.int32, (16, 128), 1) >> 5
    )
    sub96 = lax.broadcasted_iota(jnp.int32, (QROWS, 128), 0)
    sub384 = lax.broadcasted_iota(jnp.int32, (DROWS, 128), 0)

    def one_hot(condition):
        return jnp.where(condition, 1.0, 0.0).astype(BF16)

    def source_row(s):
        return jnp.where(lane1 < pc_ref[t, s], src_v[pl.ds(s, 1), :], -1)

    def target_row(s):
        return dst_v[pl.ds(s, 1), :]

    def spread_out(x):
        x = x + pltpu.roll(x, 64, 1)
        return x + pltpu.roll(x, 32, 1)

    def back_terms(tiles):
        srows = [source_row(s) for s in tiles]
        scols = [scol_v[s] for s in tiles]
        dcols = [dcol_v[s] for s in tiles]
        pick = jnp.concatenate(
            [
                jnp.concatenate([one_hot(lane + 128 * k == dcol) for k in range(3)], axis=1)
                for dcol in dcols
            ],
            axis=0,
        )
        grad = dot(pick, cot_v[...]).astype(BF16)
        results = []
        for n, s in enumerate(tiles):
            parts = []
            for i in range(8):
                w = w_v[s, 16 * i : 16 * i + 16].reshape(16 * BLK, 128)
                o = dot_nt(grad[SLOTS * n + 16 * i : SLOTS * n + 16 * i + 16], w)
                parts.append(
                    sum(
                        jnp.where(r16 == 4 * j, o[:, 128 * j : 128 * j + 128], 0.0)
                        for j in range(4)
                    )
                )
            terms = spread_out(jnp.concatenate(parts, axis=0))
            terms = jnp.where(lgroup == (scols[n] & 3), terms, 0.0)
            put = one_hot(sub96 == (srows[n] >> 2))
            both = dot(put, jnp.concatenate(split(terms), axis=1))
            results.append((both[:, 0:128] + both[:, 128:256]).astype(BF16))
        return results

    def forward_terms(tiles):
        puts, sums = [], []
        for s in tiles:
            scol = scol_v[s]
            picked = dot(one_hot(lane == (scol >> 2)), low[s])
            picked = spread_out(jnp.where(lgroup == (scol & 3), picked, 0.0))
            parts = []
            for i in range(8):
                x = picked[16 * i : 16 * i + 16]
                x = jnp.concatenate([jnp.where(r16 == 4 * j, x, 0.0) for j in range(4)], axis=1)
                w = w_v[s, 16 * i : 16 * i + 16].reshape(16 * BLK, 128)
                parts.append(dot(x.astype(BF16), w))
            sums.append(jnp.concatenate(split(jnp.concatenate(parts, axis=0)), axis=1))
            puts.append(one_hot(sub384 == target_row(s)))
        both = dot(jnp.concatenate(puts, axis=1), jnp.concatenate(sums, axis=0))
        return both[:, 0:128] + both[:, 128:256]

    loads[2].wait()
    loads[3].wait()
    turned = jnp.transpose(
        jnp.concatenate([src_v[...], dst_v[...], jnp.zeros((96, SLOTS), jnp.int32)], axis=0).astype(F32)
    ).astype(jnp.int32)
    for s in range(TILES):
        scol = jnp.broadcast_to(turned[:, s : s + 1], (SLOTS, 128))
        scol_v[s] = jnp.where(slot_id < pc_ref[t, s], scol, -1)
        dcol_v[s] = jnp.broadcast_to(turned[:, TILES + s : TILES + s + 1], (SLOTS, 128))

    def back_step(j):
        tiles = [tile_peer(GROUP * j + 1 + i) for i in range(GROUP)]
        for s in tiles:
            w_load(s).wait()
        results = back_terms(tiles)
        for s, r in zip(tiles, results):
            ss[s] = r
        for s in tiles:

            @pl.when(s != t)
            def _():
                to_tile(ss.at[s], sr.at[t], sp_s, sp_r, s).start()

    steps = TILES // GROUP

    @pl.loop(0, steps)
    def _(j):
        back_step(j)

        @pl.when(j == steps // 2 - 1)
        def _():
            recursion(zr, zo, de, zs_r, zo_s, zo_r)

    sr[t] = ss[t]

    ax = dx_ref[...]
    posx = lax.broadcasted_iota(jnp.int32, (8, COLS), 1)
    lx, hx = scans(ax, posx, COLS, COLS)
    cx = coefficient(ax)
    gx = cx * hx
    edge1 = jnp.broadcast_to(lx[:, 127:128], (8, COLS))
    edge2 = jnp.broadcast_to(lx[:, 255:256], (8, COLS))
    xt[:, 0, :] = lx
    xt[:, 1, :] = cx
    xt[:, 2, :] = gx
    xt[:, 3, :] = gx * jnp.exp(jnp.minimum(lx - jnp.where(posx < 256, edge1, edge2), 0.0))
    xt[:, 4, :] = cx * jnp.exp(jnp.minimum(edge1 - lx, 0.0))
    xt[:, 5, :] = cx * jnp.exp(jnp.minimum(edge2 - lx, 0.0))
    xt[:, 6:8, :] = jnp.zeros((LEVELS, 2, COLS), F32)
    lowx = lax.broadcasted_iota(jnp.int32, (128, 128), 0) >= (
        lax.broadcasted_iota(jnp.int32, (128, 128), 1)
    )

    @pl.loop(0, LEVELS)
    def _(l):
        rows = xt[l]
        cols = columns(rows)
        for ib in range(3):
            for jb in range(3):
                r = rows[:, 128 * jb : 128 * jb + 128]

                def xcol(f):
                    return cols[128 * ib : 128 * ib + 128, f : f + 1]

                if ib == jb:
                    e = jnp.exp(-jnp.abs(xcol(0) - r[0:1]))
                    m = e * jnp.where(lowx, xcol(2) * r[1:2], xcol(1) * r[2:3])
                elif ib > jb:
                    m = xcol(3) * r[3 + ib : 4 + ib]
                else:
                    m = xcol(3 + jb) * r[3:4]
                mh, ml = split(m)
                kk[l, 128 * ib : 128 * ib + 128, 128 * jb : 128 * jb + 128] = mh
                at = COLS + 128 * ib
                kk[l, at : at + 128, 128 * jb : 128 * jb + 128] = ml

    exports = [
        pltpu.make_async_copy(x, y, out_sem.at[i])
        for i, (x, y) in enumerate(
            [
                (mt, mt_hbm), (pb, pb_hbm), (qb, qb_hbm), (kk, kk_hbm),
                (back, back_hbm), (de2, de_hbm), (inc_v, inc_hbm),
            ]
        )
    ]
    for x in exports[:4]:
        x.start()

    wait_all(sr, sp_r, TILES)
    acc = sr[0].astype(F32)
    for s in range(1, TILES):
        acc = acc + sr[s].astype(F32)
    bq[...] = acc
    for j in range(3):
        back[g, :, 128 * j : 128 * j + 128] = bq[pl.ds(j, ROWS, stride=3), :]

    @pl.loop(1, LEVELS)
    def _(k):
        l = mem_peer(k)
        to_mem(back.at[g], back.at[g], bk_s, bk_r, l).start()

    loads[4].wait()
    wait_all(de, zo_r, TILES)

    def partial(l):
        y = smooth(
            [(alpha_of(l, half),) for half in range(2)], (de[2 * l], de[2 * l + 1]),
            mt[l], pb[l], qb[l], kk[l], True,
        )
        acc = jnp.zeros((ROWS, COLS), F32)
        for m in range(2 * HALF):
            acc = acc + (live[m] * pert_v[m, l].astype(F32)) * y[ROWS * m : ROWS * m + ROWS]
        return acc

    @pl.loop(1, LEVELS + 1)
    def _(k):
        l = mem_peer(k)
        ps[l] = partial(l)

        @pl.when(l != g)
        def _():
            to_mem(ps.at[l], pr.at[g], rs_s, rs_r, l).start()

    pr[g] = ps[g]

    wait_all(back, bk_r, LEVELS)
    exports[4].start()

    def weighted(l, half):
        x = pert_v[HALF * half : HALF * half + HALF, l].astype(F32) * back[l][None]
        return split(x.reshape(PACK, COLS))

    sources(weighted, zs2, zr2, zs2_s, zs2_r, 0, 2)

    wait_all(pr, rs_r, LEVELS)
    acc = pr[0]
    for s in range(1, LEVELS):
        acc = acc + pr[s]
    acc = acc * scale
    for j in range(3):
        lq[pl.ds(j, ROWS, stride=3), :] = acc[:, 128 * j : 128 * j + 128]
    lows[...] = lq[...].astype(BF16)

    @pl.loop(1, TILES)
    def _(k):
        s = tile_peer(k)
        to_tile(lows, low.at[t, pl.ds(0, QROWS), :], lo_s, lo_r.at[t], s).start()

    low[t, 0:QROWS, :] = lows[...]

    sources(weighted, zs2, zr2, zs2_s, zs2_r, 2, 4)

    inc_v[...] = jnp.zeros((DROWS, 128), F32)

    def forward_step(j):
        for i in range(GROUP):
            s = tile_back(GROUP * j + i)

            @pl.when(s != t)
            def _():
                to_tile(lows, low.at[s, pl.ds(0, QROWS), :], lo_s, lo_r.at[s], s).wait_recv()

        inc_v[...] += forward_terms([tile_back(GROUP * j + i) for i in range(GROUP)])

    @pl.loop(0, steps)
    def _(j):
        forward_step(j)

        @pl.when(j == steps // 2 - 1)
        def _():
            recursion(zr2, zo2, de2, zs2_r, zo2_s, zo2_r)

    wait_all(de2, zo2_r, TILES)
    exports[5].start()
    exports[6].start()

    wait_all(zs, zs_s, TILES)
    wait_all(zo, zo_s, TILES)
    wait_all(zs2, zs2_s, TILES)
    wait_all(zo2, zo2_s, TILES)
    wait_all(ss, sp_s, TILES)
    wait_all(sr, lo_s, TILES)
    wait_all(ps, rs_s, LEVELS)
    wait_all(back, bk_s, LEVELS)
    for x in exports:
        x.wait()


def shards(
    alpha, perturbation, cotangent, decay_y, decay_x, group_members, interp_weight,
    pair_count, src_index, dst_index,
):
    any_spec = pl.BlockSpec(memory_space=pl.ANY)
    vmem = pl.BlockSpec(memory_space=pltpu.VMEM)
    smem = pl.BlockSpec(memory_space=pltpu.SMEM)
    dma = pltpu.SemaphoreType.DMA
    V = pltpu.VMEM
    zbuf = V((TILES, 16, COLS), F32)
    scratch = [
        V((2 * HALF, LEVELS, ROWS, COLS), BF16),
        V((2 * HALF, LEVELS, ROWS, COLS), BF16),
        V((1, DROWS * 128), BF16),
        V((DROWS, 128), BF16),
        V((TILES, SLOTS, BLK, 128), BF16),
        V((TILES, SLOTS), jnp.int32),
        V((TILES, SLOTS), jnp.int32),
        V((8, 512), F32),
        V((LEVELS, 8, 512), F32),
        V((LEVELS, 2, COLS), F32),
        V((LEVELS, 8, COLS), F32),
        V((LEVELS, PACK, 512), BF16),
        V((LEVELS, 32, PACK), BF16),
        V((LEVELS, 16, COLS), F32),
        V((LEVELS, ROWS, 128), F32),
        V((LEVELS, ROWS, 128), F32),
        V((LEVELS, 2 * COLS, COLS), BF16),
        *[zbuf] * 8,
        V((TILES, QROWS, 128), BF16),
        V((TILES, QROWS, 128), BF16),
        V((QROWS, 128), F32),
        V((LEVELS, ROWS, COLS), F32),
        V((LEVELS, ROWS, COLS), F32),
        V((LEVELS, ROWS, COLS), F32),
        V((QROWS, 128), F32),
        V((TILES, 128, 128), BF16),
        V((QROWS, 128), BF16),
        V((DROWS, 128), F32),
        V((TILES, SLOTS, 128), jnp.int32),
        V((TILES, SLOTS, 128), jnp.int32),
        dma((5,)),
        dma((TILES,)),
        dma((7,)),
        *[dma] * 12,
        dma,
        dma((TILES,)),
        dma,
        dma,
    ]
    shape = jax.ShapeDtypeStruct
    inc, *rest = pl.pallas_call(
        kernel,
        out_shape=(
            shape((DROWS, 128), F32),
            shape((LEVELS, ROWS, COLS), F32),
            shape((TILES, 16, COLS), F32),
            shape((LEVELS, PACK, 512), BF16),
            shape((LEVELS, ROWS, 128), F32),
            shape((LEVELS, ROWS, 128), F32),
            shape((LEVELS, 2 * COLS, COLS), BF16),
        ),
        in_specs=[any_spec, any_spec, any_spec, vmem, vmem, smem, any_spec, smem, any_spec, any_spec],
        out_specs=(any_spec,) * 7,
        scratch_shapes=scratch,
        compiler_params=pltpu.CompilerParams(
            collective_id=0, has_side_effects=True, vmem_limit_bytes=60 * 1024 * 1024
        ),
        cost_estimate=pl.CostEstimate(
            flops=9_000_000_000, bytes_accessed=29_000_000, transcendentals=700_000
        ),
    )(
        alpha, perturbation, cotangent, decay_y, decay_x, group_members,
        interp_weight, pair_count, src_index, dst_index,
    )

    def level(*block):
        return pl.BlockSpec(block, lambda l: (l,) + (0,) * (len(block) - 1))

    member_block = pl.BlockSpec((2 * HALF, 1, ROWS, COLS), lambda l: (0, l, 0, 0))
    return pl.pallas_call(
        grad_kernel,
        grid=(LEVELS,),
        out_shape=(shape((1, DROWS * 128), F32), shape(alpha.shape, F32)),
        in_specs=[
            smem,
            member_block,
            level(1, ROWS, COLS),
            level(2, 16, COLS),
            level(1, PACK, 512),
            level(1, ROWS, 128),
            level(1, ROWS, 128),
            level(1, 2 * COLS, COLS),
            pl.BlockSpec((DROWS, 128), lambda l: (0, 0)),
        ],
        out_specs=(pl.BlockSpec((1, DROWS * 128), lambda l: (0, 0)), member_block),
        compiler_params=pltpu.CompilerParams(vmem_limit_bytes=60 * 1024 * 1024),
        cost_estimate=pl.CostEstimate(
            flops=3_500_000_000, bytes_accessed=13_000_000, transcendentals=0
        ),
    )(group_members, perturbation, *rest, inc)


def solution(mesh):
    in_specs = (
        P("mem", None, "tile", None),
        P("mem", None, "tile", None),
        P("mem", "tile"),
        P(None, "tile"),
        P(),
        P(),
        P("tile", None, None, None, None),
        P(),
        P(),
        P(),
    )
    out_specs = (P("mem", "tile"), P("mem", None, "tile", None))
    return jax.shard_map(shards, mesh=mesh, in_specs=in_specs, out_specs=out_specs, check_vma=False)
```

```python
import jax
import jax.numpy as jnp
from jax import lax
from jax.experimental import pallas as pl
from jax.experimental.pallas import tpu as pltpu
from jax.sharding import PartitionSpec as P

MESH = pl.DeviceIdType.MESH
F32 = jnp.float32
BF16 = jnp.bfloat16

LEVELS = 8
TILES = 16
ROWS = 32
COLS = 384
HALF = 5
PACK = HALF * ROWS
SLOTS = 128
BLK = 32
QROWS = ROWS * COLS // 128
DROWS = 384
GROUP = 4


def dot(a, b):
    return lax.dot_general(a, b, (((1,), (0,)), ((), ())), preferred_element_type=F32)


def dot_nt(a, b):
    return lax.dot_general(a, b, (((1,), (1,)), ((), ())), preferred_element_type=F32)


def split(x):
    high = x.astype(BF16)
    return high, (x - high.astype(F32)).astype(BF16)


def coefficient(a):
    t = 1.0 - a * a
    ratio = (t * t * t) / (1.0 + a * a)
    return jnp.where(ratio > 0.0, jnp.sqrt(jnp.sqrt(jnp.maximum(ratio, 1e-37))), 0.0)


def scans(a, pos, width, segment):
    logs = jnp.log(a)
    steps = [1 << b for b in range(16) if (1 << b) < segment]
    for k in steps:
        logs = logs + jnp.where(pos >= k, pltpu.roll(logs, k, 1), 0.0)
    rate = jnp.where(pos < segment - 1, pltpu.roll(a * a, width - 1, 1), 0.0)
    h = jnp.ones_like(a)
    for k in steps:
        h = h + rate * pltpu.roll(h, width - k, 1)
        rate = rate * pltpu.roll(rate, width - k, 1)
    return logs, h


def smooth(fields, carries, mt, pb, qb, kk, precise):
    p3 = jnp.concatenate([pb] * 3, axis=1)
    q3 = jnp.concatenate([qb] * 3, axis=1)
    rows = []
    for field, carry in zip(fields, carries):
        hi, *lo = field
        stack = jnp.concatenate([hi, hi, *lo], axis=0)
        y = dot(mt[:, 0 : stack.shape[0]], stack)
        for m in range(HALF):
            rows.append(
                y[ROWS * m : ROWS * m + ROWS]
                + p3 * carry[m : m + 1, :]
                + q3 * carry[8 + m : 9 + m, :]
            )
    y = jnp.concatenate(rows, axis=0)
    if not precise:
        yh = y.astype(BF16)
        return dot(jnp.concatenate([yh, yh], axis=1), kk)
    yh, yl = split(y)
    return dot(jnp.concatenate([yh, yh, yl], axis=1), jnp.concatenate([kk, kk[0:COLS]], axis=0))


def members(gm_ref):
    own = gm_ref[lax.axis_index("mem")]
    total = gm_ref[0]
    for i in range(1, LEVELS):
        total = total + gm_ref[i]
    scale = 1.0 / jnp.sqrt(jnp.full((1, COLS), total.astype(F32) - 1.0, F32))
    return scale, [jnp.where(m < own, 1.0, 0.0).astype(F32) for m in range(2 * HALF)]


def grad_kernel(
    gm_ref, pert_ref, back_ref, de_ref, mt_ref, pb_ref, qb_ref, kk_ref, inc_ref,
    inc_out, grad_ref,
):
    scale, live = members(gm_ref)
    fields = []
    for half in range(2):
        x = pert_ref[HALF * half : HALF * half + HALF, 0].astype(F32) * back_ref[...]
        fields.append(split(x.reshape(PACK, COLS)))
    y = smooth(
        fields, (de_ref[0], de_ref[1]), mt_ref[0], pb_ref[0], qb_ref[0], kk_ref[0], False
    )
    for m in range(2 * HALF):
        grad_ref[m, 0] = y[ROWS * m : ROWS * m + ROWS] * (scale * live[m])

    rows = DROWS // LEVELS
    first = pl.program_id(0) * rows
    x = inc_ref[pl.ds(pl.multiple_of(first, rows), rows), :]
    for r in range(rows):
        at = pl.multiple_of((first + r) * 128, 128)
        inc_out[0:1, pl.ds(at, 128)] = x[r : r + 1, :]


def kernel(
    alpha_hbm, pert_hbm, cot_hbm, dy_ref, dx_ref, gm_ref, w_hbm, pc_ref, src_hbm, dst_hbm,
    inc_hbm, back_hbm, de_hbm, mt_hbm, pb_hbm, qb_hbm, kk_hbm,
    alpha_v, pert_v, cot_raw, cot_v, w_v, src_v, dst_v,
    rep_v, yt, ytail, xt, mt, zf, zadd, pb, qb, kk,
    zs, zr, zo, de, zs2, zr2, zo2, de2,
    ss, sr, bq, back, ps, pr, lq, low, lows, inc_v, scol_v, dcol_v,
    in_sem, w_sem, out_sem, zs_s, zs_r, zo_s, zo_r, zs2_s, zs2_r, zo2_s, zo2_r,
    sp_s, sp_r, rs_s, rs_r, lo_s, lo_r, bk_s, bk_r,
):
    g = lax.axis_index("mem")
    t = lax.axis_index("tile")

    def tile_peer(k):
        return lax.rem(t + k, TILES)

    def tile_back(k):
        return lax.rem(t + TILES - k, TILES)

    def mem_peer(k):
        return lax.rem(g + k, LEVELS)

    def to_tile(src, dst, ssem, rsem, s):
        return pltpu.make_async_remote_copy(
            src_ref=src, dst_ref=dst, send_sem=ssem, recv_sem=rsem,
            device_id={"tile": s}, device_id_type=MESH,
        )

    def to_mem(src, dst, ssem, rsem, s):
        return pltpu.make_async_remote_copy(
            src_ref=src, dst_ref=dst, send_sem=ssem, recv_sem=rsem,
            device_id={"mem": s}, device_id_type=MESH,
        )

    loads = [
        pltpu.make_async_copy(alpha_hbm, alpha_v, in_sem.at[0]),
        pltpu.make_async_copy(cot_hbm, cot_raw, in_sem.at[1]),
        pltpu.make_async_copy(src_hbm.at[t], src_v, in_sem.at[2]),
        pltpu.make_async_copy(dst_hbm.at[t], dst_v, in_sem.at[3]),
        pltpu.make_async_copy(pert_hbm, pert_v, in_sem.at[4]),
    ]

    def wait_all(buf, sem, count):
        part = buf.at[pl.ds(0, count - 1)]
        pltpu.make_async_copy(part, part, sem).wait()

    def w_load(s):
        return pltpu.make_async_copy(w_hbm.at[0, s], w_v.at[s], w_sem.at[s])

    for c in loads[:4]:
        c.start()

    @pl.loop(1, TILES + 1)
    def _(k):
        w_load(tile_peer(k)).start()

    loads[4].start()

    barrier = pltpu.get_barrier_semaphore()

    @pl.loop(1, TILES)
    def _(k):
        pl.semaphore_signal(barrier, inc=1, device_id={"tile": tile_peer(k)}, device_id_type=MESH)

    @pl.loop(1, LEVELS)
    def _(k):
        pl.semaphore_signal(barrier, inc=1, device_id={"mem": mem_peer(k)}, device_id_type=MESH)

    scale, live = members(gm_ref)

    for k in range(16):
        rep_v[:, 32 * k : 32 * k + 32] = dy_ref[...]
    a = rep_v[...]
    pos = lax.broadcasted_iota(jnp.int32, (8, 512), 1) & 31
    logs, h = scans(a, pos, 512, ROWS)
    c = coefficient(a)
    ltot = jnp.broadcast_to(logs[:, 31:32], (8, 512))
    lane512 = lax.broadcasted_iota(jnp.int32, (8, 512), 1)
    hsum = jnp.sum(jnp.where(lane512 < 32, jnp.exp(2.0 * logs), 0.0), axis=1, keepdims=True)
    for f, x in enumerate(
        (logs, c, c * h, c * h * jnp.exp(logs), c * jnp.exp(ltot - logs))
    ):
        yt[:, f, :] = x
    yt[:, 5:8, :] = jnp.zeros((LEVELS, 3, 512), F32)
    ytail[:, 0, :] = jnp.broadcast_to(jnp.exp(ltot[:, 0:1]), (LEVELS, COLS))
    ytail[:, 1, :] = jnp.broadcast_to(hsum, (LEVELS, COLS))
    lane_y = lax.broadcasted_iota(jnp.int32, (ROWS, 512), 1)
    lower = lax.broadcasted_iota(jnp.int32, (ROWS, 512), 0) >= (lane_y & 31)
    zr_i = lax.broadcasted_iota(jnp.int32, (16, 256), 0)
    zc_i = lax.broadcasted_iota(jnp.int32, (16, 256), 1) >> 5
    row16 = lax.broadcasted_iota(jnp.int32, (16, COLS), 0)

    def columns(rows):
        width = rows.shape[1]
        return jnp.transpose(jnp.concatenate([rows, jnp.zeros((120, width), F32)], axis=0))

    @pl.loop(0, LEVELS)
    def _(l):
        rows = yt[l]
        cols = columns(rows[:, 0:128])[0:ROWS]

        def col(f):
            return cols[:, f : f + 1]

        e = jnp.exp(-jnp.abs(col(0) - rows[0:1]))
        m = e * jnp.where(lower, col(2) * rows[1:2], col(1) * rows[2:3])
        part = lane_y >> 5
        mh, ml = split(m)
        m = jnp.where((part >= HALF) & (part < 2 * HALF), ml.astype(F32), mh.astype(F32))
        part = jnp.where(part < 3 * HALF, part % HALF, -1)
        for i in range(HALF):
            mt[l, ROWS * i : ROWS * i + ROWS, :] = jnp.where(part == i, m, 0.0).astype(BF16)
        z = jnp.where(zr_i == zc_i, rows[4:5, 0:256], 0.0) + jnp.where(zr_i == zc_i + 8, rows[3:4, 0:256], 0.0)
        z = jnp.where(zc_i < HALF, z, 0.0)
        zh, zl = split(z)
        zf[l, 0:16, :] = zh[:, 0:PACK]
        zf[l, 16:32, :] = zl[:, 0:PACK]
        tail = ytail[l]
        zadd[l] = jnp.where(row16 == 5, tail[0:1], 0.0) + jnp.where(row16 == 6, tail[1:2], 0.0)
        pb[l] = jnp.broadcast_to(col(3), (ROWS, 128))
        qb[l] = jnp.broadcast_to(col(4), (ROWS, 128))

    low[:, QROWS:128, :] = jnp.zeros((TILES, 128 - QROWS, 128), BF16)

    loads[1].wait()

    @pl.loop(0, DROWS // 16)
    def _(i):
        rows = [
            cot_raw[:, pl.ds(pl.multiple_of(2048 * i + 128 * r, 128), 128)].astype(F32)
            for r in range(16)
        ]
        cot_v[pl.ds(pl.multiple_of(16 * i, 16), 16), :] = jnp.concatenate(rows, axis=0).astype(BF16)

    loads[0].wait()
    pl.semaphore_wait(barrier, TILES - 1 + LEVELS - 1)

    def alpha_of(l, half):
        return alpha_v[HALF * half : HALF * half + HALF, l].reshape(PACK, COLS)

    def source(l, hi, lo=None):
        r = dot(zf[l], hi)
        z = r[0:16] + r[16:32] + zadd[l]
        if lo is not None:
            z = z + dot(zf[l, 0:16, :], lo)
        return z

    def sources(field, zs, zr, s_s, s_r, first, last):
        @pl.loop(first, last)
        def _(k):
            found = []
            for i in range(2):
                l = lax.rem(t // 2 + 2 * k + i + 1, LEVELS)
                for half in range(2):
                    found.append((2 * l + half, source(l, *field(l, half))))
            for tt, z in found:
                zs[tt] = z
            for tt, _z in found:

                @pl.when(tt != t)
                def _():
                    to_tile(zs.at[tt], zr.at[t], s_s, s_r, tt).start()

        if last == LEVELS // 2:
            zr[t] = zs[t]

    sources(lambda l, half: (alpha_of(l, half),), zs, zr, zs_s, zs_r, 0, LEVELS // 2)

    def recursion(zr, zo, de, s_r, o_s, o_r):
        wait_all(zr, s_r, TILES)
        d = jnp.zeros((8, COLS), F32)
        downs = []
        for s in range(TILES):
            downs.append(d)
            zo[s, 0:8, :] = d
            d = zr[s, 5:6, :] * d + zr[s, 0:8, :]
        e = jnp.zeros((8, COLS), F32)
        for s in reversed(range(TILES)):
            zo[s, 8:16, :] = e
            e = zr[s, 5:6, :] * e + (zr[s, 8:16, :] + zr[s, 6:7, :] * downs[s])

        @pl.loop(1, TILES)
        def _(k):
            s = tile_peer(k)
            to_tile(zo.at[s], de.at[t], o_s, o_r, s).start()

        de[t] = zo[t]

    lane1 = lax.broadcasted_iota(jnp.int32, (1, 128), 1)
    lane = lax.broadcasted_iota(jnp.int32, (SLOTS, 128), 1)
    lgroup = lane >> 5
    slot_id = lax.broadcasted_iota(jnp.int32, (SLOTS, 128), 0)
    r16 = lax.broadcasted_iota(jnp.int32, (16, 128), 0) - (
        lax.broadcasted_iota(jnp.int32, (16, 128), 1) >> 5
    )
    sub96 = lax.broadcasted_iota(jnp.int32, (QROWS, 128), 0)
    sub384 = lax.broadcasted_iota(jnp.int32, (DROWS, 128), 0)

    def one_hot(condition):
        return jnp.where(condition, 1.0, 0.0).astype(BF16)

    def source_row(s):
        return jnp.where(lane1 < pc_ref[t, s], src_v[pl.ds(s, 1), :], -1)

    def target_row(s):
        return dst_v[pl.ds(s, 1), :]

    def spread_out(x):
        x = x + pltpu.roll(x, 64, 1)
        return x + pltpu.roll(x, 32, 1)

    def weight_pair(s, i):
        return jnp.concatenate(
            [
                w_v[s, 16 * (i + half) : 16 * (i + half) + 16].reshape(16 * BLK, 128)
                for half in range(2)
            ],
            axis=1,
        )

    def back_terms(tiles):
        srows = [source_row(s) for s in tiles]
        scols = [scol_v[s] for s in tiles]
        dcols = [dcol_v[s] for s in tiles]
        pick = jnp.concatenate(
            [
                jnp.concatenate([one_hot(lane + 128 * k == dcol) for k in range(3)], axis=1)
                for dcol in dcols
            ],
            axis=0,
        )
        grad = dot(pick, cot_v[...]).astype(BF16)
        results = []
        for n, s in enumerate(tiles):
            parts = []
            for i in range(0, 8, 2):
                first = SLOTS * n + 16 * i
                zero = jnp.zeros((16, 128), BF16)
                pair = jnp.concatenate(
                    [
                        jnp.concatenate([grad[first : first + 16], zero], axis=1),
                        jnp.concatenate([zero, grad[first + 16 : first + 32]], axis=1),
                    ],
                    axis=0,
                )
                o = dot_nt(pair, weight_pair(s, i))
                for half in range(2):
                    parts.append(
                        sum(
                            jnp.where(
                                r16 == 4 * j,
                                o[16 * half : 16 * half + 16, 128 * j : 128 * j + 128],
                                0.0,
                            )
                            for j in range(4)
                        )
                    )
            terms = spread_out(jnp.concatenate(parts, axis=0))
            terms = jnp.where(lgroup == (scols[n] & 3), terms, 0.0)
            put = one_hot(sub96 == (srows[n] >> 2))
            both = dot(put, jnp.concatenate(split(terms), axis=1))
            results.append((both[:, 0:128] + both[:, 128:256]).astype(BF16))
        return results

    def forward_terms(tiles):
        puts, sums = [], []
        for s in tiles:
            scol = scol_v[s]
            picked = dot(one_hot(lane == (scol >> 2)), low[s])
            picked = spread_out(jnp.where(lgroup == (scol & 3), picked, 0.0))
            parts = []
            for i in range(0, 8, 2):
                xs = []
                for half in range(2):
                    x = picked[16 * (i + half) : 16 * (i + half) + 16]
                    xs.append(
                        jnp.concatenate([jnp.where(r16 == 4 * j, x, 0.0) for j in range(4)], axis=1)
                    )
                both = dot(jnp.concatenate(xs, axis=0).astype(BF16), weight_pair(s, i))
                parts.append(both[0:16, 0:128])
                parts.append(both[16:32, 128:256])
            sums.append(jnp.concatenate(split(jnp.concatenate(parts, axis=0)), axis=1))
            puts.append(one_hot(sub384 == target_row(s)))
        both = dot(jnp.concatenate(puts, axis=1), jnp.concatenate(sums, axis=0))
        return both[:, 0:128] + both[:, 128:256]

    loads[2].wait()
    loads[3].wait()
    turned = jnp.transpose(
        jnp.concatenate([src_v[...], dst_v[...], jnp.zeros((96, SLOTS), jnp.int32)], axis=0).astype(F32)
    ).astype(jnp.int32)
    for s in range(TILES):
        scol = jnp.broadcast_to(turned[:, s : s + 1], (SLOTS, 128))
        scol_v[s] = jnp.where(slot_id < pc_ref[t, s], scol, -1)
        dcol_v[s] = jnp.broadcast_to(turned[:, TILES + s : TILES + s + 1], (SLOTS, 128))

    def back_step(j):
        tiles = [tile_peer(GROUP * j + 1 + i) for i in range(GROUP)]
        for s in tiles:
            w_load(s).wait()
        results = back_terms(tiles)
        for s, r in zip(tiles, results):
            ss[s] = r
        for s in tiles:

            @pl.when(s != t)
            def _():
                to_tile(ss.at[s], sr.at[t], sp_s, sp_r, s).start()

    steps = TILES // GROUP

    @pl.loop(0, steps)
    def _(j):
        back_step(j)

        @pl.when(j == steps // 2 - 1)
        def _():
            recursion(zr, zo, de, zs_r, zo_s, zo_r)

    sr[t] = ss[t]

    ax = dx_ref[...]
    posx = lax.broadcasted_iota(jnp.int32, (8, COLS), 1)
    lx, hx = scans(ax, posx, COLS, COLS)
    cx = coefficient(ax)
    gx = cx * hx
    edge1 = jnp.broadcast_to(lx[:, 127:128], (8, COLS))
    edge2 = jnp.broadcast_to(lx[:, 255:256], (8, COLS))
    xt[:, 0, :] = lx
    xt[:, 1, :] = cx
    xt[:, 2, :] = gx
    xt[:, 3, :] = gx * jnp.exp(jnp.minimum(lx - jnp.where(posx < 256, edge1, edge2), 0.0))
    xt[:, 4, :] = cx * jnp.exp(jnp.minimum(edge1 - lx, 0.0))
    xt[:, 5, :] = cx * jnp.exp(jnp.minimum(edge2 - lx, 0.0))
    xt[:, 6:8, :] = jnp.zeros((LEVELS, 2, COLS), F32)
    lowx = lax.broadcasted_iota(jnp.int32, (128, 128), 0) >= (
        lax.broadcasted_iota(jnp.int32, (128, 128), 1)
    )

    @pl.loop(0, LEVELS)
    def _(l):
        rows = xt[l]
        cols = columns(rows)
        for ib in range(3):
            for jb in range(3):
                r = rows[:, 128 * jb : 128 * jb + 128]

                def xcol(f):
                    return cols[128 * ib : 128 * ib + 128, f : f + 1]

                if ib == jb:
                    e = jnp.exp(-jnp.abs(xcol(0) - r[0:1]))
                    m = e * jnp.where(lowx, xcol(2) * r[1:2], xcol(1) * r[2:3])
                elif ib > jb:
                    m = xcol(3) * r[3 + ib : 4 + ib]
                else:
                    m = xcol(3 + jb) * r[3:4]
                mh, ml = split(m)
                kk[l, 128 * ib : 128 * ib + 128, 128 * jb : 128 * jb + 128] = mh
                at = COLS + 128 * ib
                kk[l, at : at + 128, 128 * jb : 128 * jb + 128] = ml

    exports = [
        pltpu.make_async_copy(x, y, out_sem.at[i])
        for i, (x, y) in enumerate(
            [
                (mt, mt_hbm), (pb, pb_hbm), (qb, qb_hbm), (kk, kk_hbm),
                (back, back_hbm), (de2, de_hbm), (inc_v, inc_hbm),
            ]
        )
    ]
    for x in exports[:4]:
        x.start()

    wait_all(sr, sp_r, TILES)
    acc = sr[0].astype(F32)
    for s in range(1, TILES):
        acc = acc + sr[s].astype(F32)
    bq[...] = acc
    for j in range(3):
        back[g, :, 128 * j : 128 * j + 128] = bq[pl.ds(j, ROWS, stride=3), :]

    @pl.loop(1, LEVELS)
    def _(k):
        l = mem_peer(k)
        to_mem(back.at[g], back.at[g], bk_s, bk_r, l).start()

    loads[4].wait()
    wait_all(de, zo_r, TILES)

    def partial(l):
        y = smooth(
            [(alpha_of(l, half),) for half in range(2)], (de[2 * l], de[2 * l + 1]),
            mt[l], pb[l], qb[l], kk[l], True,
        )
        acc = jnp.zeros((ROWS, COLS), F32)
        for m in range(2 * HALF):
            acc = acc + (live[m] * pert_v[m, l].astype(F32)) * y[ROWS * m : ROWS * m + ROWS]
        return acc

    @pl.loop(1, LEVELS + 1)
    def _(k):
        l = mem_peer(k)
        ps[l] = partial(l)

        @pl.when(l != g)
        def _():
            to_mem(ps.at[l], pr.at[g], rs_s, rs_r, l).start()

    pr[g] = ps[g]

    wait_all(back, bk_r, LEVELS)
    exports[4].start()

    def weighted(l, half):
        x = pert_v[HALF * half : HALF * half + HALF, l].astype(F32) * back[l][None]
        return split(x.reshape(PACK, COLS))

    sources(weighted, zs2, zr2, zs2_s, zs2_r, 0, 2)

    wait_all(pr, rs_r, LEVELS)
    acc = pr[0]
    for s in range(1, LEVELS):
        acc = acc + pr[s]
    acc = acc * scale
    for j in range(3):
        lq[pl.ds(j, ROWS, stride=3), :] = acc[:, 128 * j : 128 * j + 128]
    lows[...] = lq[...].astype(BF16)

    @pl.loop(1, TILES)
    def _(k):
        s = tile_peer(k)
        to_tile(lows, low.at[t, pl.ds(0, QROWS), :], lo_s, lo_r.at[t], s).start()

    low[t, 0:QROWS, :] = lows[...]

    sources(weighted, zs2, zr2, zs2_s, zs2_r, 2, 4)

    inc_v[...] = jnp.zeros((DROWS, 128), F32)

    def forward_step(j):
        for i in range(GROUP):
            s = tile_back(GROUP * j + i)

            @pl.when(s != t)
            def _():
                to_tile(lows, low.at[s, pl.ds(0, QROWS), :], lo_s, lo_r.at[s], s).wait_recv()

        inc_v[...] += forward_terms([tile_back(GROUP * j + i) for i in range(GROUP)])

    @pl.loop(0, steps)
    def _(j):
        forward_step(j)

        @pl.when(j == steps // 2 - 1)
        def _():
            recursion(zr2, zo2, de2, zs2_r, zo2_s, zo2_r)

    wait_all(de2, zo2_r, TILES)
    exports[5].start()
    exports[6].start()

    wait_all(zs, zs_s, TILES)
    wait_all(zo, zo_s, TILES)
    wait_all(zs2, zs2_s, TILES)
    wait_all(zo2, zo2_s, TILES)
    wait_all(ss, sp_s, TILES)
    wait_all(sr, lo_s, TILES)
    wait_all(ps, rs_s, LEVELS)
    wait_all(back, bk_s, LEVELS)
    for x in exports:
        x.wait()


def shards(
    alpha, perturbation, cotangent, decay_y, decay_x, group_members, interp_weight,
    pair_count, src_index, dst_index,
):
    any_spec = pl.BlockSpec(memory_space=pl.ANY)
    vmem = pl.BlockSpec(memory_space=pltpu.VMEM)
    smem = pl.BlockSpec(memory_space=pltpu.SMEM)
    dma = pltpu.SemaphoreType.DMA
    V = pltpu.VMEM
    zbuf = V((TILES, 16, COLS), F32)
    scratch = [
        V((2 * HALF, LEVELS, ROWS, COLS), BF16),
        V((2 * HALF, LEVELS, ROWS, COLS), BF16),
        V((1, DROWS * 128), BF16),
        V((DROWS, 128), BF16),
        V((TILES, SLOTS, BLK, 128), BF16),
        V((TILES, SLOTS), jnp.int32),
        V((TILES, SLOTS), jnp.int32),
        V((8, 512), F32),
        V((LEVELS, 8, 512), F32),
        V((LEVELS, 2, COLS), F32),
        V((LEVELS, 8, COLS), F32),
        V((LEVELS, PACK, 512), BF16),
        V((LEVELS, 32, PACK), BF16),
        V((LEVELS, 16, COLS), F32),
        V((LEVELS, ROWS, 128), F32),
        V((LEVELS, ROWS, 128), F32),
        V((LEVELS, 2 * COLS, COLS), BF16),
        *[zbuf] * 8,
        V((TILES, QROWS, 128), BF16),
        V((TILES, QROWS, 128), BF16),
        V((QROWS, 128), F32),
        V((LEVELS, ROWS, COLS), F32),
        V((LEVELS, ROWS, COLS), F32),
        V((LEVELS, ROWS, COLS), F32),
        V((QROWS, 128), F32),
        V((TILES, 128, 128), BF16),
        V((QROWS, 128), BF16),
        V((DROWS, 128), F32),
        V((TILES, SLOTS, 128), jnp.int32),
        V((TILES, SLOTS, 128), jnp.int32),
        dma((5,)),
        dma((TILES,)),
        dma((7,)),
        *[dma] * 12,
        dma,
        dma((TILES,)),
        dma,
        dma,
    ]
    shape = jax.ShapeDtypeStruct
    inc, *rest = pl.pallas_call(
        kernel,
        out_shape=(
            shape((DROWS, 128), F32),
            shape((LEVELS, ROWS, COLS), F32),
            shape((TILES, 16, COLS), F32),
            shape((LEVELS, PACK, 512), BF16),
            shape((LEVELS, ROWS, 128), F32),
            shape((LEVELS, ROWS, 128), F32),
            shape((LEVELS, 2 * COLS, COLS), BF16),
        ),
        in_specs=[any_spec, any_spec, any_spec, vmem, vmem, smem, any_spec, smem, any_spec, any_spec],
        out_specs=(any_spec,) * 7,
        scratch_shapes=scratch,
        compiler_params=pltpu.CompilerParams(
            collective_id=0, has_side_effects=True, vmem_limit_bytes=60 * 1024 * 1024
        ),
        cost_estimate=pl.CostEstimate(
            flops=9_000_000_000, bytes_accessed=29_000_000, transcendentals=700_000
        ),
    )(
        alpha, perturbation, cotangent, decay_y, decay_x, group_members,
        interp_weight, pair_count, src_index, dst_index,
    )

    def level(*block):
        return pl.BlockSpec(block, lambda l: (l,) + (0,) * (len(block) - 1))

    member_block = pl.BlockSpec((2 * HALF, 1, ROWS, COLS), lambda l: (0, l, 0, 0))
    return pl.pallas_call(
        grad_kernel,
        grid=(LEVELS,),
        out_shape=(shape((1, DROWS * 128), F32), shape(alpha.shape, F32)),
        in_specs=[
            smem,
            member_block,
            level(1, ROWS, COLS),
            level(2, 16, COLS),
            level(1, PACK, 512),
            level(1, ROWS, 128),
            level(1, ROWS, 128),
            level(1, 2 * COLS, COLS),
            pl.BlockSpec((DROWS, 128), lambda l: (0, 0)),
        ],
        out_specs=(pl.BlockSpec((1, DROWS * 128), lambda l: (0, 0)), member_block),
        compiler_params=pltpu.CompilerParams(vmem_limit_bytes=60 * 1024 * 1024),
        cost_estimate=pl.CostEstimate(
            flops=3_500_000_000, bytes_accessed=13_000_000, transcendentals=0
        ),
    )(group_members, perturbation, *rest, inc)


def solution(mesh):
    in_specs = (
        P("mem", None, "tile", None),
        P("mem", None, "tile", None),
        P("mem", "tile"),
        P(None, "tile"),
        P(),
        P(),
        P("tile", None, None, None, None),
        P(),
        P(),
        P(),
    )
    out_specs = (P("mem", "tile"), P("mem", None, "tile", None))
    return jax.shard_map(shards, mesh=mesh, in_specs=in_specs, out_specs=out_specs, check_vma=False)
```

```python
import jax
import jax.numpy as jnp
from jax import lax
from jax.experimental import pallas as pl
from jax.experimental.pallas import tpu as pltpu
from jax.sharding import PartitionSpec as P

MESH = pl.DeviceIdType.MESH
F32 = jnp.float32
BF16 = jnp.bfloat16

LEVELS = 8
TILES = 16
CHIPS = 8
ROWS = 32
COLS = 384
HALF = 5
PACK = HALF * ROWS
SLOTS = 128
BLK = 32
QROWS = ROWS * COLS // 128
DROWS = 384
GROUP = 2


def dot(a, b):
    return lax.dot_general(a, b, (((1,), (0,)), ((), ())), preferred_element_type=F32)


def dot_nt(a, b):
    return lax.dot_general(a, b, (((1,), (1,)), ((), ())), preferred_element_type=F32)


def split(x):
    high = x.astype(BF16)
    return high, (x - high.astype(F32)).astype(BF16)


def coefficient(a):
    t = 1.0 - a * a
    ratio = (t * t * t) / (1.0 + a * a)
    return jnp.where(ratio > 0.0, jnp.sqrt(jnp.sqrt(jnp.maximum(ratio, 1e-37))), 0.0)


def scans(a, pos, width, segment):
    logs = jnp.log(a)
    steps = [1 << b for b in range(16) if (1 << b) < segment]
    for k in steps:
        logs = logs + jnp.where(pos >= k, pltpu.roll(logs, k, 1), 0.0)
    rate = jnp.where(pos < segment - 1, pltpu.roll(a * a, width - 1, 1), 0.0)
    h = jnp.ones_like(a)
    for k in steps:
        h = h + rate * pltpu.roll(h, width - k, 1)
        rate = rate * pltpu.roll(rate, width - k, 1)
    return logs, h


def carry_row(carry, first):
    rows = [carry[first + HALF * j : first + HALF * j + 1, :] for j in range(3)]
    return jnp.concatenate(rows, axis=1)


def smooth(fields, carries, mt, pb, qb, upper, lower=None):
    p3 = jnp.concatenate([pb] * 3, axis=1)
    q3 = jnp.concatenate([qb] * 3, axis=1)
    rows = []
    for field, carry in zip(fields, carries):
        hi, *lo = field
        stack = jnp.concatenate([hi, hi, *lo], axis=0)
        y = dot(mt[:, 0 : stack.shape[0]], stack)
        for m in range(HALF):
            rows.append(
                y[ROWS * m : ROWS * m + ROWS]
                + p3 * carry_row(carry, m)
                + q3 * carry_row(carry, 16 + m)
            )
    yh, yl = split(jnp.concatenate(rows, axis=0))
    if lower is None:
        return dot(jnp.concatenate([yh, yl], axis=1), jnp.concatenate([upper] * 2, axis=0))
    return dot(
        jnp.concatenate([yh, yl, yh], axis=1), jnp.concatenate([upper, upper, lower], axis=0)
    )


def members(gm_ref):
    own = gm_ref[lax.axis_index("mem")]
    total = gm_ref[0]
    for i in range(1, LEVELS):
        total = total + gm_ref[i]
    scale = 1.0 / jnp.sqrt(jnp.full((1, COLS), total.astype(F32) - 1.0, F32))
    return scale, [jnp.where(m < own, 1.0, 0.0).astype(F32) for m in range(2 * HALF)]


def grad_kernel(
    gm_ref, pert_hbm, back_hbm, de_hbm, mt_hbm, pb_hbm, qb_hbm, kk_hbm, inc_ref,
    inc_out, grad_hbm,
    pert_v, back_v, de_v, mt_v, pb_v, qb_v, kk_v, out_v, in_sem, out_sem,
):
    def loads(l):
        pairs = [
            (pert_hbm.at[:, l], pert_v.at[:, l]),
            (back_hbm.at[l], back_v.at[l]),
            (de_hbm.at[:, l], de_v.at[:, l]),
            (mt_hbm.at[l], mt_v.at[l]),
            (pb_hbm.at[l], pb_v.at[l]),
            (qb_hbm.at[l], qb_v.at[l]),
            (kk_hbm.at[l], kk_v.at[l]),
        ]
        return [
            pltpu.make_async_copy(a, b, in_sem.at[i, l]) for i, (a, b) in enumerate(pairs)
        ]

    def store(l):
        return pltpu.make_async_copy(out_v.at[:, l], grad_hbm.at[:, l], out_sem.at[l])

    @pl.loop(0, LEVELS)
    def _(l):
        for x in loads(l):
            x.start()

    scale, live = members(gm_ref)

    @pl.loop(0, DROWS // 8)
    def _(i):
        x = inc_ref[pl.ds(pl.multiple_of(8 * i, 8), 8), :]
        for r in range(8):
            inc_out[0:1, pl.ds(pl.multiple_of(1024 * i + 128 * r, 128), 128)] = x[r : r + 1, :]

    @pl.loop(0, LEVELS)
    def _(l):
        for x in loads(l):
            x.wait()
        fields = []
        for half in range(2):
            x = pert_v[HALF * half : HALF * half + HALF, l].astype(F32) * back_v[l][None]
            fields.append(split(x.reshape(PACK, COLS)))
        y = smooth(fields, (de_v[0, l], de_v[1, l]), mt_v[l], pb_v[l], qb_v[l], kk_v[l])
        for m in range(2 * HALF):
            out_v[m, l] = y[ROWS * m : ROWS * m + ROWS] * (scale * live[m])
        store(l).start()

    @pl.loop(0, LEVELS)
    def _(l):
        store(l).wait()


def kernel(
    alpha_hbm, pert_hbm, cot_hbm, dy_ref, dx_ref, gm_ref, w_hbm, pc_ref, src_hbm, dst_hbm,
    inc_hbm, back_hbm, de_hbm, mt_hbm, pb_hbm, qb_hbm, kk_hbm,
    alpha_v, pert_v, cot_raw, cot_v, w_v, src_v, dst_v,
    rep_v, yt, ytail, xt, mt, zf, pb, qb, kk,
    za, zp, zc, zr, zo, dc, dp, de, za2, zp2, zc2, zr2, zo2, dc2, dp2, de2,
    sf, sp, ss, sr, bq, back, ps, pr, lq, low, lows, inc_v, scol_v, dcol_v,
    in_sem, w_sem, out_sem, z_sem, z2_sem,
    sp_s, sp_r, ss_s, ss_r, rs_s, rs_r, lo_s, lo_f, lo_r, bk_s, bk_r,
):
    g = lax.axis_index("mem")
    t = lax.axis_index("tile")

    chip = t // 2
    core = lax.rem(t, 2)
    partner = t + 1 - 2 * core

    def chip_peer(k):
        return lax.rem(chip + k, CHIPS)

    def chip_back(k):
        return lax.rem(chip + CHIPS - k, CHIPS)

    def tile_of(ch):
        return 2 * ch + core

    def mem_peer(k):
        return lax.rem(g + k, LEVELS)

    def to_tile(src, dst, ssem, rsem, s):
        return pltpu.make_async_remote_copy(
            src_ref=src, dst_ref=dst, send_sem=ssem, recv_sem=rsem,
            device_id={"tile": s}, device_id_type=MESH,
        )

    def to_mem(src, dst, ssem, rsem, s):
        return pltpu.make_async_remote_copy(
            src_ref=src, dst_ref=dst, send_sem=ssem, recv_sem=rsem,
            device_id={"mem": s}, device_id_type=MESH,
        )

    loads = [
        pltpu.make_async_copy(alpha_hbm, alpha_v, in_sem.at[0]),
        pltpu.make_async_copy(cot_hbm, cot_raw, in_sem.at[1]),
        pltpu.make_async_copy(src_hbm.at[t], src_v, in_sem.at[2]),
        pltpu.make_async_copy(dst_hbm.at[t], dst_v, in_sem.at[3]),
        pltpu.make_async_copy(pert_hbm, pert_v, in_sem.at[4]),
    ]

    def wait_all(buf, sem, count):
        part = buf.at[pl.ds(0, count - 1)]
        pltpu.make_async_copy(part, part, sem).wait()

    def w_load(s):
        return pltpu.make_async_copy(w_hbm.at[0, s], w_v.at[s], w_sem.at[s])

    for c in loads:
        c.start()

    @pl.loop(0, TILES)
    def _(i):
        late = i // CHIPS
        w_load(2 * chip_peer(i - CHIPS * late + 1) + 1 - core + late * (2 * core - 1)).start()

    barrier = pltpu.get_barrier_semaphore()

    pl.semaphore_signal(barrier, inc=1, device_id={"tile": partner}, device_id_type=MESH)

    @pl.loop(1, CHIPS)
    def _(k):
        pl.semaphore_signal(
            barrier, inc=1, device_id={"tile": tile_of(chip_peer(k))}, device_id_type=MESH
        )

    @pl.loop(1, LEVELS)
    def _(k):
        pl.semaphore_signal(barrier, inc=1, device_id={"mem": mem_peer(k)}, device_id_type=MESH)

    scale, live = members(gm_ref)

    for k in range(16):
        rep_v[:, 32 * k : 32 * k + 32] = dy_ref[...]
    a = rep_v[...]
    pos = lax.broadcasted_iota(jnp.int32, (8, 512), 1) & 31
    logs, h = scans(a, pos, 512, ROWS)
    c = coefficient(a)
    ltot = jnp.broadcast_to(logs[:, 31:32], (8, 512))
    lane512 = lax.broadcasted_iota(jnp.int32, (8, 512), 1)
    hsum = jnp.sum(jnp.where(lane512 < 32, jnp.exp(2.0 * logs), 0.0), axis=1, keepdims=True)
    for f, x in enumerate(
        (logs, c, c * h, c * h * jnp.exp(logs), c * jnp.exp(ltot - logs))
    ):
        yt[:, f, :] = x
    yt[:, 5:8, :] = jnp.zeros((LEVELS, 3, 512), F32)
    ytail[:, 0, :] = jnp.broadcast_to(jnp.exp(ltot[:, 0:1]), (LEVELS, COLS))
    ytail[:, 1, :] = jnp.broadcast_to(hsum, (LEVELS, COLS))
    lane_y = lax.broadcasted_iota(jnp.int32, (ROWS, 512), 1)
    lower = lax.broadcasted_iota(jnp.int32, (ROWS, 512), 0) >= (lane_y & 31)
    zr_i = lax.broadcasted_iota(jnp.int32, (16, 256), 0)
    zc_i = lax.broadcasted_iota(jnp.int32, (16, 256), 1) >> 5

    def columns(rows):
        width = rows.shape[1]
        return jnp.transpose(jnp.concatenate([rows, jnp.zeros((120, width), F32)], axis=0))

    @pl.loop(0, LEVELS)
    def _(l):
        rows = yt[l]
        cols = columns(rows[:, 0:128])[0:ROWS]

        def col(f):
            return cols[:, f : f + 1]

        e = jnp.exp(-jnp.abs(col(0) - rows[0:1]))
        m = e * jnp.where(lower, col(2) * rows[1:2], col(1) * rows[2:3])
        part = lane_y >> 5
        mh, ml = split(m)
        m = jnp.where((part >= HALF) & (part < 2 * HALF), ml.astype(F32), mh.astype(F32))
        part = jnp.where(part < 3 * HALF, part % HALF, -1)
        for i in range(HALF):
            mt[l, ROWS * i : ROWS * i + ROWS, :] = jnp.where(part == i, m, 0.0).astype(BF16)
        z = jnp.where(zr_i == zc_i, rows[4:5, 0:256], 0.0) + jnp.where(zr_i == zc_i + 8, rows[3:4, 0:256], 0.0)
        z = jnp.where(zc_i < HALF, z, 0.0)
        zh, zl = split(z)
        zf[l, 0:16, :] = zh[:, 0:PACK]
        zf[l, 16:32, :] = zl[:, 0:PACK]
        pb[l] = jnp.broadcast_to(col(3), (ROWS, 128))
        qb[l] = jnp.broadcast_to(col(4), (ROWS, 128))

    low[:, QROWS:128, :] = jnp.zeros((TILES, 128 - QROWS, 128), BF16)

    loads[1].wait()

    @pl.loop(0, DROWS // 16)
    def _(i):
        rows = [
            cot_raw[:, pl.ds(pl.multiple_of(2048 * i + 128 * r, 128), 128)].astype(F32)
            for r in range(16)
        ]
        cot_v[pl.ds(pl.multiple_of(16 * i, 16), 16), :] = jnp.concatenate(rows, axis=0).astype(BF16)

    loads[0].wait()
    pl.semaphore_wait(barrier, 1 + CHIPS - 1 + LEVELS - 1)

    def alpha_of(l, half):
        return alpha_v[HALF * half : HALF * half + HALF, l].reshape(PACK, COLS)

    def source(l, hi, lo=None):
        r = dot(zf[l], hi)
        z = r[0:16] + r[16:32]
        if lo is not None:
            z = z + dot(zf[l, 0:16, :], lo)
        return z

    def sources(field, za, first, last):
        @pl.loop(first, last)
        def _(k):
            found = []
            for i in range(2):
                l = 2 * k + i
                for half in range(2):
                    found.append((half, l, source(l, *field(l, half))))
            for half, l, z in found:
                for j in range(3):
                    part = z[:, 128 * j : 128 * j + 128]
                    za[half, l, HALF * j : HALF * j + HALF, :] = part[0:HALF]
                    za[half, l, 16 + HALF * j : 16 + HALF * j + HALF, :] = part[8 : 8 + HALF]
                za[half, l, 15:16, :] = ytail[l, 0:1, 0:128]
                za[half, l, 31:32, :] = ytail[l, 1:2, 0:128]

    def to_partner(za, zp, sem):
        other = za.at[1 - core]
        return to_tile(other, zp, sem.at[0], sem.at[1], partner)

    row16 = lax.broadcasted_iota(jnp.int32, (16, 128), 0)

    def tile_maps(za, zp, l):
        own, theirs = za[core, l], zp[l]
        first = jnp.where(core == 0, own, theirs)
        second = jnp.where(core == 0, theirs, own)
        return [(x[0:16], x[16:32], x[15:16], x[31:32]) for x in (first, second)]

    def compose(za, zp, zc, zr, sem):
        to_partner(za, zp, sem).wait_recv()

        @pl.loop(1, CHIPS + 1)
        def _(k):
            l = chip_peer(k)
            (s1, r1, p1, h1), (s2, r2, p2, h2) = tile_maps(za, zp, l)
            zc[l, 0:16, :] = jnp.where(row16 == 15, p1 * p2, p2 * s1 + s2)
            zc[l, 16:32, :] = jnp.where(
                row16 == 15, h1 + p1 * p1 * h2, r1 + p1 * (r2 + h2 * s1)
            )

            @pl.when(l != chip)
            def _():
                to_tile(zc.at[l], zr.at[chip], sem.at[2], sem.at[3], tile_of(l)).start()

        zr[chip] = zc[chip]

    def recursion(zr, zo, dc, sem):
        wait_all(zr, sem.at[3], CHIPS)
        d = jnp.zeros((16, 128), F32)
        downs = []
        for s in range(CHIPS):
            downs.append(d)
            zo[s, 0:16, :] = d
            d = zr[s, 15:16, :] * d + zr[s, 0:16, :]
        e = jnp.zeros((16, 128), F32)
        for s in reversed(range(CHIPS)):
            zo[s, 16:32, :] = e
            e = zr[s, 15:16, :] * e + (zr[s, 16:32, :] + zr[s, 31:32, :] * downs[s])

        @pl.loop(1, CHIPS)
        def _(k):
            s = chip_peer(k)
            to_tile(zo.at[s], dc.at[chip], sem.at[4], sem.at[5], tile_of(s)).start()

        dc[chip] = zo[chip]

    def hand_on(dp, de, sem):
        return to_tile(dp, de.at[core], sem.at[6], sem.at[7], partner)

    def divide(za, zp, dc, dp, de, sem):
        wait_all(dc, sem.at[5], CHIPS)

        @pl.loop(0, CHIPS)
        def _(l):
            (s1, _r1, p1, _h1), (_s2, r2, p2, h2) = tile_maps(za, zp, l)
            d1, e2 = dc[l, 0:16, :], dc[l, 16:32, :]
            d2 = p1 * d1 + s1
            e1 = p2 * e2 + (r2 + h2 * d2)
            de[core, l, 0:16, :] = jnp.where(core == 0, d1, d2)
            de[core, l, 16:32, :] = jnp.where(core == 0, e1, e2)
            dp[l, 0:16, :] = jnp.where(core == 0, d2, d1)
            dp[l, 16:32, :] = jnp.where(core == 0, e2, e1)

        hand_on(dp, de, sem).start()

    def carries_sent(za, zp, zc, zo, dp, de, sem):
        to_partner(za, zp, sem).wait_send()
        wait_all(zc, sem.at[2], CHIPS)
        wait_all(zo, sem.at[4], CHIPS)
        hand_on(dp, de, sem).wait_send()

    sources(lambda l, half: (alpha_of(l, half),), za, 0, LEVELS // 2)
    to_partner(za, zp, z_sem).start()

    lane1 = lax.broadcasted_iota(jnp.int32, (1, 128), 1)
    lane = lax.broadcasted_iota(jnp.int32, (SLOTS, 128), 1)
    lgroup = lane >> 5
    slot_id = lax.broadcasted_iota(jnp.int32, (SLOTS, 128), 0)
    r16 = lax.broadcasted_iota(jnp.int32, (16, 128), 0) - (
        lax.broadcasted_iota(jnp.int32, (16, 128), 1) >> 5
    )
    sub96 = lax.broadcasted_iota(jnp.int32, (QROWS, 128), 0)
    sub384 = lax.broadcasted_iota(jnp.int32, (DROWS, 128), 0)

    def one_hot(condition):
        return jnp.where(condition, 1.0, 0.0).astype(BF16)

    def source_row(s):
        return jnp.where(lane1 < pc_ref[t, s], src_v[pl.ds(s, 1), :], -1)

    def target_row(s):
        return dst_v[pl.ds(s, 1), :]

    def spread_out(x):
        x = x + pltpu.roll(x, 64, 1)
        return x + pltpu.roll(x, 32, 1)

    def weight_pair(s, i):
        return jnp.concatenate(
            [
                w_v[s, 16 * (i + half) : 16 * (i + half) + 16].reshape(16 * BLK, 128)
                for half in range(2)
            ],
            axis=1,
        )

    def back_terms(tiles):
        srows = [source_row(s) for s in tiles]
        scols = [scol_v[s] for s in tiles]
        dcols = [dcol_v[s] for s in tiles]
        pick = jnp.concatenate(
            [
                jnp.concatenate([one_hot(lane + 128 * k == dcol) for k in range(3)], axis=1)
                for dcol in dcols
            ],
            axis=0,
        )
        grad = dot(pick, cot_v[...]).astype(BF16)
        results = []
        for n, s in enumerate(tiles):
            parts = []
            for i in range(0, 8, 2):
                first = SLOTS * n + 16 * i
                zero = jnp.zeros((16, 128), BF16)
                pair = jnp.concatenate(
                    [
                        jnp.concatenate([grad[first : first + 16], zero], axis=1),
                        jnp.concatenate([zero, grad[first + 16 : first + 32]], axis=1),
                    ],
                    axis=0,
                )
                o = dot_nt(pair, weight_pair(s, i))
                for half in range(2):
                    parts.append(
                        sum(
                            jnp.where(
                                r16 == 4 * j,
                                o[16 * half : 16 * half + 16, 128 * j : 128 * j + 128],
                                0.0,
                            )
                            for j in range(4)
                        )
                    )
            terms = spread_out(jnp.concatenate(parts, axis=0))
            terms = jnp.where(lgroup == (scols[n] & 3), terms, 0.0)
            put = one_hot(sub96 == (srows[n] >> 2))
            both = dot(put, jnp.concatenate(split(terms), axis=1))
            results.append(both[:, 0:128] + both[:, 128:256])
        return results

    def forward_terms(tiles):
        puts, sums = [], []
        for s in tiles:
            scol = scol_v[s]
            picked = dot(one_hot(lane == (scol >> 2)), low[s])
            picked = spread_out(jnp.where(lgroup == (scol & 3), picked, 0.0))
            parts = []
            for i in range(0, 8, 2):
                xs = []
                for half in range(2):
                    x = picked[16 * (i + half) : 16 * (i + half) + 16]
                    xs.append(
                        jnp.concatenate([jnp.where(r16 == 4 * j, x, 0.0) for j in range(4)], axis=1)
                    )
                both = dot(jnp.concatenate(xs, axis=0).astype(BF16), weight_pair(s, i))
                parts.append(both[0:16, 0:128])
                parts.append(both[16:32, 128:256])
            sums.append(jnp.concatenate(split(jnp.concatenate(parts, axis=0)), axis=1))
            puts.append(one_hot(sub384 == target_row(s)))
        both = dot(jnp.concatenate(puts, axis=1), jnp.concatenate(sums, axis=0))
        return both[:, 0:128] + both[:, 128:256]

    loads[2].wait()
    loads[3].wait()
    turned = jnp.transpose(
        jnp.concatenate([src_v[...], dst_v[...], jnp.zeros((96, SLOTS), jnp.int32)], axis=0).astype(F32)
    ).astype(jnp.int32)
    for s in range(TILES):
        scol = jnp.broadcast_to(turned[:, s : s + 1], (SLOTS, 128))
        scol_v[s] = jnp.where(slot_id < pc_ref[t, s], scol, -1)
        dcol_v[s] = jnp.broadcast_to(turned[:, TILES + s : TILES + s + 1], (SLOTS, 128))

    def off_chip(ch):
        return to_tile(ss.at[ch], sr.at[chip], ss_s, ss_r, tile_of(ch))

    def core_pair(ch):
        return to_tile(sf.at[0, ch], sp.at[ch], sp_s, sp_r.at[ch], partner)

    steps = TILES // GROUP

    @pl.loop(0, steps)
    def _(j):
        late = j // (steps // 2)
        chips = [chip_peer(GROUP * (j - steps // 2 * late) + 1 + i) for i in range(GROUP)]
        tiles = [2 * ch + 1 - core + late * (2 * core - 1) for ch in chips]
        for s in tiles:
            w_load(s).wait()
        for ch, r in zip(chips, back_terms(tiles)):
            sf[late, ch] = r

        @pl.when(late == 0)
        def _():
            for ch in chips:
                core_pair(ch).start()

        @pl.when(late == 1)
        def _():
            for ch in chips:
                core_pair(ch).wait_recv()
                ss[ch] = (sf[1, ch] + sp[ch]).astype(BF16)

                @pl.when(ch != chip)
                def _():
                    off_chip(ch).start()

        @pl.when(j == steps // 4 - 1)
        def _():
            compose(za, zp, zc, zr, z_sem)

        @pl.when(j == steps // 2 - 1)
        def _():
            recursion(zr, zo, dc, z_sem)

        @pl.when(j == steps - 1)
        def _():
            divide(za, zp, dc, dp, de, z_sem)

    sr[chip] = ss[chip]

    ax = dx_ref[...]
    posx = lax.broadcasted_iota(jnp.int32, (8, COLS), 1)
    lx, hx = scans(ax, posx, COLS, COLS)
    cx = coefficient(ax)
    gx = cx * hx
    edge1 = jnp.broadcast_to(lx[:, 127:128], (8, COLS))
    edge2 = jnp.broadcast_to(lx[:, 255:256], (8, COLS))
    xt[:, 0, :] = lx
    xt[:, 1, :] = cx
    xt[:, 2, :] = gx
    xt[:, 3, :] = gx * jnp.exp(jnp.minimum(lx - jnp.where(posx < 256, edge1, edge2), 0.0))
    xt[:, 4, :] = cx * jnp.exp(jnp.minimum(edge1 - lx, 0.0))
    xt[:, 5, :] = cx * jnp.exp(jnp.minimum(edge2 - lx, 0.0))
    xt[:, 6:8, :] = jnp.zeros((LEVELS, 2, COLS), F32)
    lowx = lax.broadcasted_iota(jnp.int32, (128, 128), 0) >= (
        lax.broadcasted_iota(jnp.int32, (128, 128), 1)
    )

    @pl.loop(0, LEVELS)
    def _(l):
        rows = xt[l]
        cols = columns(rows)
        for ib in range(3):
            for jb in range(3):
                r = rows[:, 128 * jb : 128 * jb + 128]

                def xcol(f):
                    return cols[128 * ib : 128 * ib + 128, f : f + 1]

                if ib == jb:
                    e = jnp.exp(-jnp.abs(xcol(0) - r[0:1]))
                    m = e * jnp.where(lowx, xcol(2) * r[1:2], xcol(1) * r[2:3])
                elif ib > jb:
                    m = xcol(3) * r[3 + ib : 4 + ib]
                else:
                    m = xcol(3 + jb) * r[3:4]
                mh, ml = split(m)
                kk[l, 128 * ib : 128 * ib + 128, 128 * jb : 128 * jb + 128] = mh
                at = COLS + 128 * ib
                kk[l, at : at + 128, 128 * jb : 128 * jb + 128] = ml

    exports = [
        pltpu.make_async_copy(x, y, out_sem.at[i])
        for i, (x, y) in enumerate(
            [
                (mt, mt_hbm), (pb, pb_hbm), (qb, qb_hbm), (kk.at[:, pl.ds(0, COLS), :], kk_hbm),
                (back, back_hbm), (de2, de_hbm), (inc_v, inc_hbm),
            ]
        )
    ]
    for x in exports[:4]:
        x.start()

    wait_all(sr, ss_r, CHIPS)
    acc = sr[0].astype(F32)
    for s in range(1, CHIPS):
        acc = acc + sr[s].astype(F32)
    bq[...] = acc
    for j in range(3):
        back[g, :, 128 * j : 128 * j + 128] = bq[pl.ds(j, ROWS, stride=3), :]

    @pl.loop(1, LEVELS)
    def _(k):
        l = mem_peer(k)
        to_mem(back.at[g], back.at[g], bk_s, bk_r, l).start()

    loads[4].wait()
    hand_on(dp, de, z_sem).wait_recv()

    def partial(l):
        y = smooth(
            [(alpha_of(l, half),) for half in range(2)], (de[0, l], de[1, l]),
            mt[l], pb[l], qb[l], kk[l, 0:COLS], kk[l, COLS : 2 * COLS],
        )
        acc = jnp.zeros((ROWS, COLS), F32)
        for m in range(2 * HALF):
            acc = acc + (live[m] * pert_v[m, l].astype(F32)) * y[ROWS * m : ROWS * m + ROWS]
        return acc

    @pl.loop(1, LEVELS + 1)
    def _(k):
        l = mem_peer(k)
        ps[l] = partial(l)

        @pl.when(l != g)
        def _():
            to_mem(ps.at[l], pr.at[g], rs_s, rs_r, l).start()

    pr[g] = ps[g]

    wait_all(back, bk_r, LEVELS)
    exports[4].start()

    def weighted(l, half):
        x = pert_v[HALF * half : HALF * half + HALF, l].astype(F32) * back[l][None]
        return split(x.reshape(PACK, COLS))

    sources(weighted, za2, 0, 2)

    wait_all(pr, rs_r, LEVELS)
    acc = pr[0]
    for s in range(1, LEVELS):
        acc = acc + pr[s]
    acc = acc * scale
    for j in range(3):
        lq[pl.ds(j, ROWS, stride=3), :] = acc[:, 128 * j : 128 * j + 128]
    lows[...] = lq[...].astype(BF16)

    def low_rows(s):
        return low.at[s, pl.ds(0, QROWS), :]

    def low_to(s):
        return to_tile(lows, low_rows(t), lo_s, lo_r.at[t], s)

    def low_on(s):
        return to_tile(low_rows(s), low_rows(s), lo_f, lo_r.at[s], partner)

    @pl.loop(1, CHIPS)
    def _(k):
        low_to(tile_of(chip_peer(k))).start()

    low_to(partner).start()

    low[t, 0:QROWS, :] = lows[...]

    sources(weighted, za2, 2, 4)
    to_partner(za2, zp2, z2_sem).start()

    inc_v[...] = jnp.zeros((DROWS, 128), F32)

    @pl.loop(0, steps)
    def _(j):
        late = j // (steps // 2)
        chips = [chip_back(GROUP * (j - steps // 2 * late) + i) for i in range(GROUP)]
        tiles = [2 * ch + core + late * (1 - 2 * core) for ch in chips]
        for ch, s in zip(chips, tiles):

            @pl.when((late == 1) | (ch != chip))
            def _():
                low_on(s).wait_recv()

            @pl.when((late == 0) & (ch != chip))
            def _():
                low_on(s).start()

        inc_v[...] += forward_terms(tiles)

        @pl.when(j == steps // 4 - 1)
        def _():
            compose(za2, zp2, zc2, zr2, z2_sem)

        @pl.when(j == steps // 2 - 1)
        def _():
            recursion(zr2, zo2, dc2, z2_sem)

        @pl.when(j == 3 * steps // 4 - 1)
        def _():
            divide(za2, zp2, dc2, dp2, de2, z2_sem)

    hand_on(dp2, de2, z2_sem).wait_recv()
    exports[5].start()
    exports[6].start()

    carries_sent(za, zp, zc, zo, dp, de, z_sem)
    carries_sent(za2, zp2, zc2, zo2, dp2, de2, z2_sem)
    pltpu.make_async_copy(sp, sp, sp_s).wait()
    wait_all(ss, ss_s, CHIPS)
    pltpu.make_async_copy(sr, sr, lo_s).wait()
    wait_all(sr, lo_f, CHIPS)
    wait_all(ps, rs_s, LEVELS)
    wait_all(back, bk_s, LEVELS)
    for x in exports:
        x.wait()


def shards(
    alpha, perturbation, cotangent, decay_y, decay_x, group_members, interp_weight,
    pair_count, src_index, dst_index,
):
    any_spec = pl.BlockSpec(memory_space=pl.ANY)
    vmem = pl.BlockSpec(memory_space=pltpu.VMEM)
    smem = pl.BlockSpec(memory_space=pltpu.SMEM)
    dma = pltpu.SemaphoreType.DMA
    V = pltpu.VMEM
    zbuf = V((CHIPS, 32, 128), F32)
    zpair = V((2, CHIPS, 32, 128), F32)
    zall = [zpair, *[zbuf] * 6, zpair]
    scratch = [
        V((2 * HALF, LEVELS, ROWS, COLS), BF16),
        V((2 * HALF, LEVELS, ROWS, COLS), BF16),
        V((1, DROWS * 128), BF16),
        V((DROWS, 128), BF16),
        V((TILES, SLOTS, BLK, 128), BF16),
        V((TILES, SLOTS), jnp.int32),
        V((TILES, SLOTS), jnp.int32),
        V((8, 512), F32),
        V((LEVELS, 8, 512), F32),
        V((LEVELS, 2, COLS), F32),
        V((LEVELS, 8, COLS), F32),
        V((LEVELS, PACK, 512), BF16),
        V((LEVELS, 32, PACK), BF16),
        V((LEVELS, ROWS, 128), F32),
        V((LEVELS, ROWS, 128), F32),
        V((LEVELS, 2 * COLS, COLS), BF16),
        *zall,
        *zall,
        V((2, CHIPS, QROWS, 128), F32),
        V((CHIPS, QROWS, 128), F32),
        V((CHIPS, QROWS, 128), BF16),
        V((CHIPS, QROWS, 128), BF16),
        V((QROWS, 128), F32),
        V((LEVELS, ROWS, COLS), F32),
        V((LEVELS, ROWS, COLS), F32),
        V((LEVELS, ROWS, COLS), F32),
        V((QROWS, 128), F32),
        V((TILES, 128, 128), BF16),
        V((QROWS, 128), BF16),
        V((DROWS, 128), F32),
        V((TILES, SLOTS, 128), jnp.int32),
        V((TILES, SLOTS, 128), jnp.int32),
        dma((5,)),
        dma((TILES,)),
        dma((7,)),
        dma((8,)),
        dma((8,)),
        dma,
        dma((CHIPS,)),
        *[dma] * 6,
        dma((TILES,)),
        dma,
        dma,
    ]
    shape = jax.ShapeDtypeStruct
    inc, *rest = pl.pallas_call(
        kernel,
        out_shape=(
            shape((DROWS, 128), F32),
            shape((LEVELS, ROWS, COLS), F32),
            shape((2, CHIPS, 32, 128), F32),
            shape((LEVELS, PACK, 512), BF16),
            shape((LEVELS, ROWS, 128), F32),
            shape((LEVELS, ROWS, 128), F32),
            shape((LEVELS, COLS, COLS), BF16),
        ),
        in_specs=[any_spec, any_spec, any_spec, vmem, vmem, smem, any_spec, smem, any_spec, any_spec],
        out_specs=(any_spec,) * 7,
        scratch_shapes=scratch,
        compiler_params=pltpu.CompilerParams(
            collective_id=0, has_side_effects=True, vmem_limit_bytes=60 * 1024 * 1024
        ),
        cost_estimate=pl.CostEstimate(
            flops=9_000_000_000, bytes_accessed=29_000_000, transcendentals=700_000
        ),
    )(
        alpha, perturbation, cotangent, decay_y, decay_x, group_members,
        interp_weight, pair_count, src_index, dst_index,
    )

    members_shape = (2 * HALF, LEVELS, ROWS, COLS)
    return pl.pallas_call(
        grad_kernel,
        out_shape=(shape((1, DROWS * 128), F32), shape(alpha.shape, F32)),
        in_specs=[smem, *[any_spec] * 7, vmem],
        out_specs=(vmem, any_spec),
        scratch_shapes=[
            V(members_shape, BF16),
            V((LEVELS, ROWS, COLS), F32),
            V((2, CHIPS, 32, 128), F32),
            V((LEVELS, PACK, 512), BF16),
            V((LEVELS, ROWS, 128), F32),
            V((LEVELS, ROWS, 128), F32),
            V((LEVELS, COLS, COLS), BF16),
            V(members_shape, F32),
            dma((7, LEVELS)),
            dma((LEVELS,)),
        ],
        compiler_params=pltpu.CompilerParams(vmem_limit_bytes=60 * 1024 * 1024),
        cost_estimate=pl.CostEstimate(
            flops=3_500_000_000, bytes_accessed=11_000_000, transcendentals=0
        ),
    )(group_members, perturbation, *rest, inc)


def solution(mesh):
    in_specs = (
        P("mem", None, "tile", None),
        P("mem", None, "tile", None),
        P("mem", "tile"),
        P(None, "tile"),
        P(),
        P(),
        P("tile", None, None, None, None),
        P(),
        P(),
        P(),
    )
    out_specs = (P("mem", "tile"), P("mem", None, "tile", None))
    return jax.shard_map(shards, mesh=mesh, in_specs=in_specs, out_specs=out_specs, check_vma=False)
```

```python
import jax
import jax.numpy as jnp
from jax import lax
from jax.experimental import pallas as pl
from jax.experimental.pallas import tpu as pltpu
from jax.sharding import PartitionSpec as P

MESH = pl.DeviceIdType.MESH
F32 = jnp.float32
BF16 = jnp.bfloat16

LEVELS = 8
TILES = 16
CHIPS = 8
ROWS = 32
COLS = 384
HALF = 5
PACK = HALF * ROWS
SLOTS = 128
BLK = 32
QROWS = ROWS * COLS // 128
DROWS = 384
GROUP = 2


def dot(a, b):
    return lax.dot_general(a, b, (((1,), (0,)), ((), ())), preferred_element_type=F32)


def dot_nt(a, b):
    return lax.dot_general(a, b, (((1,), (1,)), ((), ())), preferred_element_type=F32)


def split(x):
    high = x.astype(BF16)
    return high, (x - high.astype(F32)).astype(BF16)


def coefficient(a):
    t = 1.0 - a * a
    ratio = (t * t * t) / (1.0 + a * a)
    return jnp.where(ratio > 0.0, jnp.sqrt(jnp.sqrt(jnp.maximum(ratio, 1e-37))), 0.0)


def scans(a, pos, width, segment):
    logs = jnp.log(a)
    steps = [1 << b for b in range(16) if (1 << b) < segment]
    for k in steps:
        logs = logs + jnp.where(pos >= k, pltpu.roll(logs, k, 1), 0.0)
    rate = jnp.where(pos < segment - 1, pltpu.roll(a * a, width - 1, 1), 0.0)
    h = jnp.ones_like(a)
    for k in steps:
        h = h + rate * pltpu.roll(h, width - k, 1)
        rate = rate * pltpu.roll(rate, width - k, 1)
    return logs, h


def carry_row(carry, first):
    rows = [carry[first + HALF * j : first + HALF * j + 1, :] for j in range(3)]
    return jnp.concatenate(rows, axis=1)


def smooth(fields, carries, mt, pb, qb, upper, lower=None):
    p3 = jnp.concatenate([pb] * 3, axis=1)
    q3 = jnp.concatenate([qb] * 3, axis=1)
    rows = []
    for field, carry in zip(fields, carries):
        hi, *lo = field
        stack = jnp.concatenate([hi, hi, *lo], axis=0)
        y = dot(mt[:, 0 : stack.shape[0]], stack)
        for m in range(HALF):
            rows.append(
                y[ROWS * m : ROWS * m + ROWS]
                + p3 * carry_row(carry, m)
                + q3 * carry_row(carry, 16 + m)
            )
    yh, yl = split(jnp.concatenate(rows, axis=0))
    if lower is None:
        return dot(jnp.concatenate([yh, yl], axis=1), jnp.concatenate([upper] * 2, axis=0))
    return dot(
        jnp.concatenate([yh, yl, yh], axis=1), jnp.concatenate([upper, upper, lower], axis=0)
    )


def members(gm_ref):
    own = gm_ref[lax.axis_index("mem")]
    total = gm_ref[0]
    for i in range(1, LEVELS):
        total = total + gm_ref[i]
    scale = 1.0 / jnp.sqrt(jnp.full((1, COLS), total.astype(F32) - 1.0, F32))
    return scale, [jnp.where(m < own, 1.0, 0.0).astype(F32) for m in range(2 * HALF)]


def grad_kernel(
    gm_ref, pert_hbm, back_hbm, de_hbm, mt_hbm, pb_hbm, qb_hbm, kk_hbm, inc_ref,
    inc_out, grad_hbm,
    pert_v, back_v, de_v, mt_v, pb_v, qb_v, kk_v, out_v, in_sem, out_sem,
):
    def loads(l):
        pairs = [
            (pert_hbm.at[:, l], pert_v.at[:, l]),
            (back_hbm.at[l], back_v.at[l]),
            (de_hbm.at[:, l], de_v.at[:, l]),
            (mt_hbm.at[l], mt_v.at[l]),
            (pb_hbm.at[l], pb_v.at[l]),
            (qb_hbm.at[l], qb_v.at[l]),
            (kk_hbm.at[l], kk_v.at[l]),
        ]
        return [
            pltpu.make_async_copy(a, b, in_sem.at[i, l]) for i, (a, b) in enumerate(pairs)
        ]

    def store(l):
        return pltpu.make_async_copy(out_v.at[:, l], grad_hbm.at[:, l], out_sem.at[l])

    @pl.loop(0, LEVELS)
    def _(l):
        for x in loads(l):
            x.start()

    scale, live = members(gm_ref)

    @pl.loop(0, DROWS // 8)
    def _(i):
        x = inc_ref[pl.ds(pl.multiple_of(8 * i, 8), 8), :]
        for r in range(8):
            inc_out[0:1, pl.ds(pl.multiple_of(1024 * i + 128 * r, 128), 128)] = x[r : r + 1, :]

    @pl.loop(0, LEVELS)
    def _(l):
        for x in loads(l):
            x.wait()
        fields = []
        for half in range(2):
            x = pert_v[HALF * half : HALF * half + HALF, l].astype(F32) * back_v[l].astype(F32)[None]
            fields.append(split(x.reshape(PACK, COLS)))
        y = smooth(fields, (de_v[0, l], de_v[1, l]), mt_v[l], pb_v[l], qb_v[l], kk_v[l])
        for m in range(2 * HALF):
            out_v[m, l] = y[ROWS * m : ROWS * m + ROWS] * (scale * live[m])
        store(l).start()

    @pl.loop(0, LEVELS)
    def _(l):
        store(l).wait()


def kernel(
    alpha_hbm, pert_hbm, cot_hbm, dy_ref, dx_ref, gm_ref, w_hbm, pc_ref, src_hbm, dst_hbm,
    inc_hbm, back_hbm, de_hbm, mt_hbm, pb_hbm, qb_hbm, kk_hbm,
    alpha_v, pert_v, cot_raw, cot_v, w_v, src_v, dst_v,
    rep_v, yt, ytail, xt, mt, zf, pb, qb, kk,
    za, zp, zc, zr, zo, dc, dp, de, za2, zp2, zc2, zr2, zo2, dc2, dp2, de2,
    sf, sp, ss, sr, bq, back, ps, pr, lq, low, lows, inc_v, scol_v, dcol_v,
    in_sem, w_sem, out_sem, z_sem, z2_sem,
    sp_s, sp_r, ss_s, ss_r, rs_s, rs_r, lo_s, lo_f, lo_r, bk_s, bk_r,
):
    g = lax.axis_index("mem")
    t = lax.axis_index("tile")

    chip = t // 2
    core = lax.rem(t, 2)
    partner = t + 1 - 2 * core

    def chip_peer(k):
        return lax.rem(chip + k, CHIPS)

    def chip_back(k):
        return lax.rem(chip + CHIPS - k, CHIPS)

    def tile_of(ch):
        return 2 * ch + core

    def mem_peer(k):
        return lax.rem(g + k, LEVELS)

    def to_tile(src, dst, ssem, rsem, s):
        return pltpu.make_async_remote_copy(
            src_ref=src, dst_ref=dst, send_sem=ssem, recv_sem=rsem,
            device_id={"tile": s}, device_id_type=MESH,
        )

    def to_mem(src, dst, ssem, rsem, s):
        return pltpu.make_async_remote_copy(
            src_ref=src, dst_ref=dst, send_sem=ssem, recv_sem=rsem,
            device_id={"mem": s}, device_id_type=MESH,
        )

    loads = [
        pltpu.make_async_copy(alpha_hbm, alpha_v, in_sem.at[0]),
        pltpu.make_async_copy(cot_hbm, cot_raw, in_sem.at[1]),
        pltpu.make_async_copy(src_hbm.at[t], src_v, in_sem.at[2]),
        pltpu.make_async_copy(dst_hbm.at[t], dst_v, in_sem.at[3]),
        pltpu.make_async_copy(pert_hbm, pert_v, in_sem.at[4]),
    ]

    def wait_all(buf, sem, count):
        part = buf.at[pl.ds(0, count - 1)]
        pltpu.make_async_copy(part, part, sem).wait()

    def w_load(s):
        return pltpu.make_async_copy(w_hbm.at[0, s], w_v.at[s], w_sem.at[s])

    for c in loads:
        c.start()

    @pl.loop(0, TILES)
    def _(i):
        late = i // CHIPS
        w_load(2 * chip_peer(i - CHIPS * late + 1) + 1 - core + late * (2 * core - 1)).start()

    barrier = pltpu.get_barrier_semaphore()

    pl.semaphore_signal(barrier, inc=1, device_id={"tile": partner}, device_id_type=MESH)

    @pl.loop(1, CHIPS)
    def _(k):
        pl.semaphore_signal(
            barrier, inc=1, device_id={"tile": tile_of(chip_peer(k))}, device_id_type=MESH
        )

    @pl.loop(1, LEVELS)
    def _(k):
        pl.semaphore_signal(barrier, inc=1, device_id={"mem": mem_peer(k)}, device_id_type=MESH)

    scale, live = members(gm_ref)

    for k in range(16):
        rep_v[:, 32 * k : 32 * k + 32] = dy_ref[...]
    a = rep_v[...]
    pos = lax.broadcasted_iota(jnp.int32, (8, 512), 1) & 31
    logs, h = scans(a, pos, 512, ROWS)
    c = coefficient(a)
    ltot = jnp.broadcast_to(logs[:, 31:32], (8, 512))
    lane512 = lax.broadcasted_iota(jnp.int32, (8, 512), 1)
    hsum = jnp.sum(jnp.where(lane512 < 32, jnp.exp(2.0 * logs), 0.0), axis=1, keepdims=True)
    for f, x in enumerate(
        (logs, c, c * h, c * h * jnp.exp(logs), c * jnp.exp(ltot - logs))
    ):
        yt[:, f, :] = x
    yt[:, 5:8, :] = jnp.zeros((LEVELS, 3, 512), F32)
    ytail[:, 0, :] = jnp.broadcast_to(jnp.exp(ltot[:, 0:1]), (LEVELS, COLS))
    ytail[:, 1, :] = jnp.broadcast_to(hsum, (LEVELS, COLS))
    lane_y = lax.broadcasted_iota(jnp.int32, (ROWS, 512), 1)
    lower = lax.broadcasted_iota(jnp.int32, (ROWS, 512), 0) >= (lane_y & 31)
    zr_i = lax.broadcasted_iota(jnp.int32, (16, 256), 0)
    zc_i = lax.broadcasted_iota(jnp.int32, (16, 256), 1) >> 5

    def columns(rows):
        width = rows.shape[1]
        return jnp.transpose(jnp.concatenate([rows, jnp.zeros((120, width), F32)], axis=0))

    @pl.loop(0, LEVELS)
    def _(l):
        rows = yt[l]
        cols = columns(rows[:, 0:128])[0:ROWS]

        def col(f):
            return cols[:, f : f + 1]

        e = jnp.exp(-jnp.abs(col(0) - rows[0:1]))
        m = e * jnp.where(lower, col(2) * rows[1:2], col(1) * rows[2:3])
        part = lane_y >> 5
        mh, ml = split(m)
        m = jnp.where((part >= HALF) & (part < 2 * HALF), ml.astype(F32), mh.astype(F32))
        part = jnp.where(part < 3 * HALF, part % HALF, -1)
        for i in range(HALF):
            mt[l, ROWS * i : ROWS * i + ROWS, :] = jnp.where(part == i, m, 0.0).astype(BF16)
        z = jnp.where(zr_i == zc_i, rows[4:5, 0:256], 0.0) + jnp.where(zr_i == zc_i + 8, rows[3:4, 0:256], 0.0)
        z = jnp.where(zc_i < HALF, z, 0.0)
        zh, zl = split(z)
        zf[l, 0:16, :] = zh[:, 0:PACK]
        zf[l, 16:32, :] = zl[:, 0:PACK]
        pb[l] = jnp.broadcast_to(col(3), (ROWS, 128))
        qb[l] = jnp.broadcast_to(col(4), (ROWS, 128))

    low[:, QROWS:128, :] = jnp.zeros((TILES, 128 - QROWS, 128), BF16)

    loads[1].wait()

    @pl.loop(0, DROWS // 16)
    def _(i):
        rows = [
            cot_raw[:, pl.ds(pl.multiple_of(2048 * i + 128 * r, 128), 128)].astype(F32)
            for r in range(16)
        ]
        cot_v[pl.ds(pl.multiple_of(16 * i, 16), 16), :] = jnp.concatenate(rows, axis=0).astype(BF16)

    loads[0].wait()
    pl.semaphore_wait(barrier, 1 + CHIPS - 1 + LEVELS - 1)

    def alpha_of(l, half):
        return alpha_v[HALF * half : HALF * half + HALF, l].reshape(PACK, COLS)

    def source(l, hi, lo=None):
        r = dot(zf[l], hi)
        z = r[0:16] + r[16:32]
        if lo is not None:
            z = z + dot(zf[l, 0:16, :], lo)
        return z

    def sources(field, za, first, last):
        @pl.loop(first, last)
        def _(k):
            found = []
            for i in range(2):
                l = 2 * k + i
                for half in range(2):
                    found.append((half, l, source(l, *field(l, half))))
            for half, l, z in found:
                for j in range(3):
                    part = z[:, 128 * j : 128 * j + 128]
                    za[half, l, HALF * j : HALF * j + HALF, :] = part[0:HALF]
                    za[half, l, 16 + HALF * j : 16 + HALF * j + HALF, :] = part[8 : 8 + HALF]
                za[half, l, 15:16, :] = ytail[l, 0:1, 0:128]
                za[half, l, 31:32, :] = ytail[l, 1:2, 0:128]

    def to_partner(za, zp, sem):
        other = za.at[1 - core]
        return to_tile(other, zp, sem.at[0], sem.at[1], partner)

    row16 = lax.broadcasted_iota(jnp.int32, (16, 128), 0)

    def tile_maps(za, zp, l):
        own, theirs = za[core, l], zp[l]
        first = jnp.where(core == 0, own, theirs)
        second = jnp.where(core == 0, theirs, own)
        return [(x[0:16], x[16:32], x[15:16], x[31:32]) for x in (first, second)]

    def compose(za, zp, zc, zr, sem):
        to_partner(za, zp, sem).wait_recv()

        @pl.loop(1, CHIPS + 1)
        def _(k):
            l = chip_peer(k)
            (s1, r1, p1, h1), (s2, r2, p2, h2) = tile_maps(za, zp, l)
            zc[l, 0:16, :] = jnp.where(row16 == 15, p1 * p2, p2 * s1 + s2)
            zc[l, 16:32, :] = jnp.where(
                row16 == 15, h1 + p1 * p1 * h2, r1 + p1 * (r2 + h2 * s1)
            )

            @pl.when(l != chip)
            def _():
                to_tile(zc.at[l], zr.at[chip], sem.at[2], sem.at[3], tile_of(l)).start()

        zr[chip] = zc[chip]

    def recursion(zr, zo, dc, sem):
        wait_all(zr, sem.at[3], CHIPS)
        d = jnp.zeros((16, 128), F32)
        downs = []
        for s in range(CHIPS):
            downs.append(d)
            zo[s, 0:16, :] = d
            d = zr[s, 15:16, :] * d + zr[s, 0:16, :]
        e = jnp.zeros((16, 128), F32)
        for s in reversed(range(CHIPS)):
            zo[s, 16:32, :] = e
            e = zr[s, 15:16, :] * e + (zr[s, 16:32, :] + zr[s, 31:32, :] * downs[s])

        @pl.loop(1, CHIPS)
        def _(k):
            s = chip_peer(k)
            to_tile(zo.at[s], dc.at[chip], sem.at[4], sem.at[5], tile_of(s)).start()

        dc[chip] = zo[chip]

    def hand_on(dp, de, sem):
        return to_tile(dp, de.at[core], sem.at[6], sem.at[7], partner)

    def divide(za, zp, dc, dp, de, sem):
        wait_all(dc, sem.at[5], CHIPS)

        @pl.loop(0, CHIPS)
        def _(l):
            (s1, _r1, p1, _h1), (_s2, r2, p2, h2) = tile_maps(za, zp, l)
            d1, e2 = dc[l, 0:16, :], dc[l, 16:32, :]
            d2 = p1 * d1 + s1
            e1 = p2 * e2 + (r2 + h2 * d2)
            de[core, l, 0:16, :] = jnp.where(core == 0, d1, d2)
            de[core, l, 16:32, :] = jnp.where(core == 0, e1, e2)
            dp[l, 0:16, :] = jnp.where(core == 0, d2, d1)
            dp[l, 16:32, :] = jnp.where(core == 0, e2, e1)

        hand_on(dp, de, sem).start()

    def carries_sent(za, zp, zc, zo, dp, de, sem):
        to_partner(za, zp, sem).wait_send()
        wait_all(zc, sem.at[2], CHIPS)
        wait_all(zo, sem.at[4], CHIPS)
        hand_on(dp, de, sem).wait_send()

    sources(lambda l, half: (alpha_of(l, half),), za, 0, LEVELS // 2)
    to_partner(za, zp, z_sem).start()

    lane1 = lax.broadcasted_iota(jnp.int32, (1, 128), 1)
    lane = lax.broadcasted_iota(jnp.int32, (SLOTS, 128), 1)
    lgroup = lane >> 5
    slot_id = lax.broadcasted_iota(jnp.int32, (SLOTS, 128), 0)
    r16 = lax.broadcasted_iota(jnp.int32, (16, 128), 0) - (
        lax.broadcasted_iota(jnp.int32, (16, 128), 1) >> 5
    )
    sub96 = lax.broadcasted_iota(jnp.int32, (QROWS, 128), 0)
    sub384 = lax.broadcasted_iota(jnp.int32, (DROWS, 128), 0)

    def one_hot(condition):
        return jnp.where(condition, 1.0, 0.0).astype(BF16)

    def source_row(s):
        return jnp.where(lane1 < pc_ref[t, s], src_v[pl.ds(s, 1), :], -1)

    def target_row(s):
        return dst_v[pl.ds(s, 1), :]

    def spread_out(x):
        x = x + pltpu.roll(x, 64, 1)
        return x + pltpu.roll(x, 32, 1)

    def weight_pair(s, i):
        return jnp.concatenate(
            [
                w_v[s, 16 * (i + half) : 16 * (i + half) + 16].reshape(16 * BLK, 128)
                for half in range(2)
            ],
            axis=1,
        )

    def back_terms(tiles):
        srows = [source_row(s) for s in tiles]
        scols = [scol_v[s] for s in tiles]
        dcols = [dcol_v[s] for s in tiles]
        pick = jnp.concatenate(
            [
                jnp.concatenate([one_hot(lane + 128 * k == dcol) for k in range(3)], axis=1)
                for dcol in dcols
            ],
            axis=0,
        )
        grad = dot(pick, cot_v[...]).astype(BF16)
        results = []
        for n, s in enumerate(tiles):
            parts = []
            for i in range(0, 8, 2):
                first = SLOTS * n + 16 * i
                zero = jnp.zeros((16, 128), BF16)
                pair = jnp.concatenate(
                    [
                        jnp.concatenate([grad[first : first + 16], zero], axis=1),
                        jnp.concatenate([zero, grad[first + 16 : first + 32]], axis=1),
                    ],
                    axis=0,
                )
                o = dot_nt(pair, weight_pair(s, i))
                for half in range(2):
                    parts.append(
                        sum(
                            jnp.where(
                                r16 == 4 * j,
                                o[16 * half : 16 * half + 16, 128 * j : 128 * j + 128],
                                0.0,
                            )
                            for j in range(4)
                        )
                    )
            terms = spread_out(jnp.concatenate(parts, axis=0))
            terms = jnp.where(lgroup == (scols[n] & 3), terms, 0.0)
            put = one_hot(sub96 == (srows[n] >> 2))
            both = dot(put, jnp.concatenate(split(terms), axis=1))
            results.append(both[:, 0:128] + both[:, 128:256])
        return results

    def forward_terms(tiles):
        puts, sums = [], []
        for s in tiles:
            scol = scol_v[s]
            picked = dot(one_hot(lane == (scol >> 2)), low[s])
            picked = spread_out(jnp.where(lgroup == (scol & 3), picked, 0.0))
            parts = []
            for i in range(0, 8, 2):
                xs = []
                for half in range(2):
                    x = picked[16 * (i + half) : 16 * (i + half) + 16]
                    xs.append(
                        jnp.concatenate([jnp.where(r16 == 4 * j, x, 0.0) for j in range(4)], axis=1)
                    )
                both = dot(jnp.concatenate(xs, axis=0).astype(BF16), weight_pair(s, i))
                parts.append(both[0:16, 0:128])
                parts.append(both[16:32, 128:256])
            sums.append(jnp.concatenate(split(jnp.concatenate(parts, axis=0)), axis=1))
            puts.append(one_hot(sub384 == target_row(s)))
        both = dot(jnp.concatenate(puts, axis=1), jnp.concatenate(sums, axis=0))
        return both[:, 0:128] + both[:, 128:256]

    loads[2].wait()
    loads[3].wait()
    turned = jnp.transpose(
        jnp.concatenate([src_v[...], dst_v[...], jnp.zeros((96, SLOTS), jnp.int32)], axis=0).astype(F32)
    ).astype(jnp.int32)
    for s in range(TILES):
        scol = jnp.broadcast_to(turned[:, s : s + 1], (SLOTS, 128))
        scol_v[s] = jnp.where(slot_id < pc_ref[t, s], scol, -1)
        dcol_v[s] = jnp.broadcast_to(turned[:, TILES + s : TILES + s + 1], (SLOTS, 128))

    def off_chip(ch):
        return to_tile(ss.at[ch], sr.at[chip], ss_s, ss_r, tile_of(ch))

    def core_pair(ch):
        return to_tile(sf.at[0, ch], sp.at[ch], sp_s, sp_r.at[ch], partner)

    steps = TILES // GROUP

    @pl.loop(0, steps)
    def _(j):
        late = j // (steps // 2)
        chips = [chip_peer(GROUP * (j - steps // 2 * late) + 1 + i) for i in range(GROUP)]
        tiles = [2 * ch + 1 - core + late * (2 * core - 1) for ch in chips]
        for s in tiles:
            w_load(s).wait()
        for ch, r in zip(chips, back_terms(tiles)):
            sf[late, ch] = r

        @pl.when(late == 0)
        def _():
            for ch in chips:
                core_pair(ch).start()

        @pl.when(late == 1)
        def _():
            for ch in chips:
                core_pair(ch).wait_recv()
                ss[ch] = sf[1, ch] + sp[ch]

                @pl.when(ch != chip)
                def _():
                    off_chip(ch).start()

        @pl.when(j == steps // 4 - 1)
        def _():
            compose(za, zp, zc, zr, z_sem)

        @pl.when(j == steps // 2 - 1)
        def _():
            recursion(zr, zo, dc, z_sem)

        @pl.when(j == steps - 1)
        def _():
            divide(za, zp, dc, dp, de, z_sem)

    sr[chip] = ss[chip]

    ax = dx_ref[...]
    posx = lax.broadcasted_iota(jnp.int32, (8, COLS), 1)
    lx, hx = scans(ax, posx, COLS, COLS)
    cx = coefficient(ax)
    gx = cx * hx
    edge1 = jnp.broadcast_to(lx[:, 127:128], (8, COLS))
    edge2 = jnp.broadcast_to(lx[:, 255:256], (8, COLS))
    xt[:, 0, :] = lx
    xt[:, 1, :] = cx
    xt[:, 2, :] = gx
    xt[:, 3, :] = gx * jnp.exp(jnp.minimum(lx - jnp.where(posx < 256, edge1, edge2), 0.0))
    xt[:, 4, :] = cx * jnp.exp(jnp.minimum(edge1 - lx, 0.0))
    xt[:, 5, :] = cx * jnp.exp(jnp.minimum(edge2 - lx, 0.0))
    xt[:, 6:8, :] = jnp.zeros((LEVELS, 2, COLS), F32)
    lowx = lax.broadcasted_iota(jnp.int32, (128, 128), 0) >= (
        lax.broadcasted_iota(jnp.int32, (128, 128), 1)
    )

    @pl.loop(0, LEVELS)
    def _(l):
        rows = xt[l]
        cols = columns(rows)
        for ib in range(3):
            for jb in range(3):
                r = rows[:, 128 * jb : 128 * jb + 128]

                def xcol(f):
                    return cols[128 * ib : 128 * ib + 128, f : f + 1]

                if ib == jb:
                    e = jnp.exp(-jnp.abs(xcol(0) - r[0:1]))
                    m = e * jnp.where(lowx, xcol(2) * r[1:2], xcol(1) * r[2:3])
                elif ib > jb:
                    m = xcol(3) * r[3 + ib : 4 + ib]
                else:
                    m = xcol(3 + jb) * r[3:4]
                mh, ml = split(m)
                kk[l, 128 * ib : 128 * ib + 128, 128 * jb : 128 * jb + 128] = mh
                at = COLS + 128 * ib
                kk[l, at : at + 128, 128 * jb : 128 * jb + 128] = ml

    exports = [
        pltpu.make_async_copy(x, y, out_sem.at[i])
        for i, (x, y) in enumerate(
            [
                (mt, mt_hbm), (pb, pb_hbm), (qb, qb_hbm), (kk.at[:, pl.ds(0, COLS), :], kk_hbm),
                (back, back_hbm), (de2, de_hbm), (inc_v, inc_hbm),
            ]
        )
    ]
    for x in exports[:4]:
        x.start()

    wait_all(sr, ss_r, CHIPS)
    acc = sr[0]
    for s in range(1, CHIPS):
        acc = acc + sr[s]
    bq[...] = acc
    for j in range(3):
        back[g, :, 128 * j : 128 * j + 128] = bq[pl.ds(j, ROWS, stride=3), :].astype(BF16)

    @pl.loop(1, LEVELS)
    def _(k):
        l = mem_peer(k)
        to_mem(back.at[g], back.at[g], bk_s, bk_r, l).start()

    loads[4].wait()
    hand_on(dp, de, z_sem).wait_recv()

    def partial(l):
        y = smooth(
            [(alpha_of(l, half),) for half in range(2)], (de[0, l], de[1, l]),
            mt[l], pb[l], qb[l], kk[l, 0:COLS], kk[l, COLS : 2 * COLS],
        )
        acc = jnp.zeros((ROWS, COLS), F32)
        for m in range(2 * HALF):
            acc = acc + (live[m] * pert_v[m, l].astype(F32)) * y[ROWS * m : ROWS * m + ROWS]
        return acc

    @pl.loop(1, LEVELS + 1)
    def _(k):
        l = mem_peer(k)
        ps[l] = partial(l)

        @pl.when(l != g)
        def _():
            to_mem(ps.at[l], pr.at[g], rs_s, rs_r, l).start()

    pr[g] = ps[g]

    wait_all(back, bk_r, LEVELS)
    exports[4].start()

    def weighted(l, half):
        x = pert_v[HALF * half : HALF * half + HALF, l].astype(F32) * back[l].astype(F32)[None]
        return split(x.reshape(PACK, COLS))

    sources(weighted, za2, 0, 2)

    wait_all(pr, rs_r, LEVELS)
    acc = pr[0]
    for s in range(1, LEVELS):
        acc = acc + pr[s]
    acc = acc * scale
    for j in range(3):
        lq[pl.ds(j, ROWS, stride=3), :] = acc[:, 128 * j : 128 * j + 128]
    lows[...] = lq[...].astype(BF16)

    def low_rows(s):
        return low.at[s, pl.ds(0, QROWS), :]

    def low_to(s):
        return to_tile(lows, low_rows(t), lo_s, lo_r.at[t], s)

    def low_on(s):
        return to_tile(low_rows(s), low_rows(s), lo_f, lo_r.at[s], partner)

    @pl.loop(1, CHIPS)
    def _(k):
        low_to(tile_of(chip_peer(k))).start()

    low_to(partner).start()

    low[t, 0:QROWS, :] = lows[...]

    sources(weighted, za2, 2, 4)
    to_partner(za2, zp2, z2_sem).start()

    inc_v[...] = jnp.zeros((DROWS, 128), F32)

    @pl.loop(0, steps)
    def _(j):
        tiles = []
        for i in range(GROUP):
            n = GROUP * j + i
            afar = (n + TILES - 2) // TILES
            late = n // (CHIPS + 1)
            ch = chip_back(afar * (n - 1 - (CHIPS - 1) * late))
            s = 2 * ch + core + (late + (1 - afar) * lax.rem(n, 2)) * (1 - 2 * core)
            tiles.append(s)

            @pl.when(n > 0)
            def _():
                low_on(s).wait_recv()

            @pl.when((afar == 1) & (late == 0))
            def _():
                low_on(s).start()

        inc_v[...] += forward_terms(tiles)

        @pl.when(j == steps // 4 - 1)
        def _():
            compose(za2, zp2, zc2, zr2, z2_sem)

        @pl.when(j == steps // 2 - 1)
        def _():
            recursion(zr2, zo2, dc2, z2_sem)

        @pl.when(j == 3 * steps // 4 - 1)
        def _():
            divide(za2, zp2, dc2, dp2, de2, z2_sem)

    hand_on(dp2, de2, z2_sem).wait_recv()
    exports[5].start()
    exports[6].start()

    carries_sent(za, zp, zc, zo, dp, de, z_sem)
    carries_sent(za2, zp2, zc2, zo2, dp2, de2, z2_sem)
    pltpu.make_async_copy(sp, sp, sp_s).wait()
    wait_all(ss, ss_s, CHIPS)
    lows8 = low.at[pl.ds(0, CHIPS), pl.ds(0, QROWS), :]
    pltpu.make_async_copy(lows8, lows8, lo_s).wait()
    lows7 = low.at[pl.ds(0, CHIPS - 1), pl.ds(0, QROWS), :]
    pltpu.make_async_copy(lows7, lows7, lo_f).wait()
    wait_all(ps, rs_s, LEVELS)
    wait_all(back, bk_s, LEVELS)
    for x in exports:
        x.wait()


def shards(
    alpha, perturbation, cotangent, decay_y, decay_x, group_members, interp_weight,
    pair_count, src_index, dst_index,
):
    any_spec = pl.BlockSpec(memory_space=pl.ANY)
    vmem = pl.BlockSpec(memory_space=pltpu.VMEM)
    smem = pl.BlockSpec(memory_space=pltpu.SMEM)
    dma = pltpu.SemaphoreType.DMA
    V = pltpu.VMEM
    zbuf = V((CHIPS, 32, 128), F32)
    zpair = V((2, CHIPS, 32, 128), F32)
    zall = [zpair, *[zbuf] * 6, zpair]
    scratch = [
        V((2 * HALF, LEVELS, ROWS, COLS), BF16),
        V((2 * HALF, LEVELS, ROWS, COLS), BF16),
        V((1, DROWS * 128), BF16),
        V((DROWS, 128), BF16),
        V((TILES, SLOTS, BLK, 128), BF16),
        V((TILES, SLOTS), jnp.int32),
        V((TILES, SLOTS), jnp.int32),
        V((8, 512), F32),
        V((LEVELS, 8, 512), F32),
        V((LEVELS, 2, COLS), F32),
        V((LEVELS, 8, COLS), F32),
        V((LEVELS, PACK, 512), BF16),
        V((LEVELS, 32, PACK), BF16),
        V((LEVELS, ROWS, 128), F32),
        V((LEVELS, ROWS, 128), F32),
        V((LEVELS, 2 * COLS, COLS), BF16),
        *zall,
        *zall,
        V((2, CHIPS, QROWS, 128), F32),
        V((CHIPS, QROWS, 128), F32),
        V((CHIPS, QROWS, 128), F32),
        V((CHIPS, QROWS, 128), F32),
        V((QROWS, 128), F32),
        V((LEVELS, ROWS, COLS), BF16),
        V((LEVELS, ROWS, COLS), F32),
        V((LEVELS, ROWS, COLS), F32),
        V((QROWS, 128), F32),
        V((TILES, 128, 128), BF16),
        V((QROWS, 128), BF16),
        V((DROWS, 128), F32),
        V((TILES, SLOTS, 128), jnp.int32),
        V((TILES, SLOTS, 128), jnp.int32),
        dma((5,)),
        dma((TILES,)),
        dma((7,)),
        dma((8,)),
        dma((8,)),
        dma,
        dma((CHIPS,)),
        *[dma] * 6,
        dma((TILES,)),
        dma,
        dma,
    ]
    shape = jax.ShapeDtypeStruct
    inc, *rest = pl.pallas_call(
        kernel,
        out_shape=(
            shape((DROWS, 128), F32),
            shape((LEVELS, ROWS, COLS), BF16),
            shape((2, CHIPS, 32, 128), F32),
            shape((LEVELS, PACK, 512), BF16),
            shape((LEVELS, ROWS, 128), F32),
            shape((LEVELS, ROWS, 128), F32),
            shape((LEVELS, COLS, COLS), BF16),
        ),
        in_specs=[any_spec, any_spec, any_spec, vmem, vmem, smem, any_spec, smem, any_spec, any_spec],
        out_specs=(any_spec,) * 7,
        scratch_shapes=scratch,
        compiler_params=pltpu.CompilerParams(
            collective_id=0, has_side_effects=True, vmem_limit_bytes=60 * 1024 * 1024
        ),
        cost_estimate=pl.CostEstimate(
            flops=9_000_000_000, bytes_accessed=29_000_000, transcendentals=700_000
        ),
    )(
        alpha, perturbation, cotangent, decay_y, decay_x, group_members,
        interp_weight, pair_count, src_index, dst_index,
    )

    members_shape = (2 * HALF, LEVELS, ROWS, COLS)
    return pl.pallas_call(
        grad_kernel,
        out_shape=(shape((1, DROWS * 128), F32), shape(alpha.shape, F32)),
        in_specs=[smem, *[any_spec] * 7, vmem],
        out_specs=(vmem, any_spec),
        scratch_shapes=[
            V(members_shape, BF16),
            V((LEVELS, ROWS, COLS), BF16),
            V((2, CHIPS, 32, 128), F32),
            V((LEVELS, PACK, 512), BF16),
            V((LEVELS, ROWS, 128), F32),
            V((LEVELS, ROWS, 128), F32),
            V((LEVELS, COLS, COLS), BF16),
            V(members_shape, F32),
            dma((7, LEVELS)),
            dma((LEVELS,)),
        ],
        compiler_params=pltpu.CompilerParams(vmem_limit_bytes=60 * 1024 * 1024),
        cost_estimate=pl.CostEstimate(
            flops=3_500_000_000, bytes_accessed=11_000_000, transcendentals=0
        ),
    )(group_members, perturbation, *rest, inc)


def solution(mesh):
    in_specs = (
        P("mem", None, "tile", None),
        P("mem", None, "tile", None),
        P("mem", "tile"),
        P(None, "tile"),
        P(),
        P(),
        P("tile", None, None, None, None),
        P(),
        P(),
        P(),
    )
    out_specs = (P("mem", "tile"), P("mem", None, "tile", None))
    return jax.shard_map(shards, mesh=mesh, in_specs=in_specs, out_specs=out_specs, check_vma=False)
```

```python
import jax
import jax.numpy as jnp
from jax import lax
from jax.experimental import pallas as pl
from jax.experimental.pallas import tpu as pltpu
from jax.sharding import PartitionSpec as P

MESH = pl.DeviceIdType.MESH
F32 = jnp.float32
BF16 = jnp.bfloat16

LEVELS = 8
TILES = 16
CHIPS = 8
ROWS = 32
COLS = 384
HALF = 5
PACK = HALF * ROWS
SLOTS = 128
BLK = 32
QROWS = ROWS * COLS // 128
DROWS = 384
GROUP = 2


def dot(a, b):
    return lax.dot_general(a, b, (((1,), (0,)), ((), ())), preferred_element_type=F32)


def dot_nt(a, b):
    return lax.dot_general(a, b, (((1,), (1,)), ((), ())), preferred_element_type=F32)


def split(x):
    high = x.astype(BF16)
    return high, (x - high.astype(F32)).astype(BF16)


def coefficient(a):
    t = 1.0 - a * a
    ratio = (t * t * t) / (1.0 + a * a)
    return jnp.where(ratio > 0.0, jnp.sqrt(jnp.sqrt(jnp.maximum(ratio, 1e-37))), 0.0)


def scans(a, pos, width, segment):
    logs = jnp.log(a)
    steps = [1 << b for b in range(16) if (1 << b) < segment]
    for k in steps:
        logs = logs + jnp.where(pos >= k, pltpu.roll(logs, k, 1), 0.0)
    rate = jnp.where(pos < segment - 1, pltpu.roll(a * a, width - 1, 1), 0.0)
    h = jnp.ones_like(a)
    for k in steps:
        h = h + rate * pltpu.roll(h, width - k, 1)
        rate = rate * pltpu.roll(rate, width - k, 1)
    return logs, h


def carry_row(carry, first):
    rows = [carry[first + HALF * j : first + HALF * j + 1, :] for j in range(3)]
    return jnp.concatenate(rows, axis=1)


def smooth(fields, carries, mt, pb, qb, upper, lower=None):
    p3 = jnp.concatenate([pb] * 3, axis=1)
    q3 = jnp.concatenate([qb] * 3, axis=1)
    rows = []
    for field, carry in zip(fields, carries):
        hi, *lo = field
        stack = jnp.concatenate([hi, hi, *lo], axis=0)
        y = dot(mt[:, 0 : stack.shape[0]], stack)
        for m in range(HALF):
            rows.append(
                y[ROWS * m : ROWS * m + ROWS]
                + p3 * carry_row(carry, m)
                + q3 * carry_row(carry, 16 + m)
            )
    yh, yl = split(jnp.concatenate(rows, axis=0))
    if lower is None:
        return dot(jnp.concatenate([yh, yl], axis=1), jnp.concatenate([upper] * 2, axis=0))
    return dot(
        jnp.concatenate([yh, yl, yh], axis=1), jnp.concatenate([upper, upper, lower], axis=0)
    )


def members(gm_ref):
    own = gm_ref[lax.axis_index("mem")]
    total = gm_ref[0]
    for i in range(1, LEVELS):
        total = total + gm_ref[i]
    scale = 1.0 / jnp.sqrt(jnp.full((1, COLS), total.astype(F32) - 1.0, F32))
    return scale, [jnp.where(m < own, 1.0, 0.0).astype(F32) for m in range(2 * HALF)]


def grad_kernel(
    gm_ref, pert_hbm, back_hbm, de_hbm, mt_hbm, pb_hbm, qb_hbm, kk_hbm, inc_ref,
    inc_out, grad_hbm,
    pert_v, back_v, de_v, mt_v, pb_v, qb_v, kk_v, out_v, whole_sem, in_sem, out_sem,
):
    whole = [
        pltpu.make_async_copy(a, b, whole_sem.at[i])
        for i, (a, b) in enumerate(
            [(back_hbm, back_v), (de_hbm, de_v), (pb_hbm, pb_v), (qb_hbm, qb_v), (mt_hbm, mt_v)]
        )
    ]

    def loads(l):
        return [
            pltpu.make_async_copy(pert_hbm.at[:, l], pert_v.at[:, l], in_sem.at[0, l]),
            pltpu.make_async_copy(kk_hbm.at[l], kk_v.at[l], in_sem.at[1, l]),
        ]

    def store(l):
        return pltpu.make_async_copy(out_v.at[:, l], grad_hbm.at[:, l], out_sem.at[l])

    for x in whole:
        x.start()

    @pl.loop(0, LEVELS)
    def _(l):
        for x in loads(l):
            x.start()

    scale, live = members(gm_ref)

    @pl.loop(0, DROWS // 8)
    def _(i):
        x = inc_ref[pl.ds(pl.multiple_of(8 * i, 8), 8), :]
        for r in range(8):
            inc_out[0:1, pl.ds(pl.multiple_of(1024 * i + 128 * r, 128), 128)] = x[r : r + 1, :]

    for x in whole:
        x.wait()

    @pl.loop(0, LEVELS)
    def _(l):
        for x in loads(l):
            x.wait()
        fields = []
        for half in range(2):
            x = pert_v[HALF * half : HALF * half + HALF, l].astype(F32) * back_v[l].astype(F32)[None]
            fields.append(split(x.reshape(PACK, COLS)))
        y = smooth(fields, (de_v[0, l], de_v[1, l]), mt_v[l], pb_v[l], qb_v[l], kk_v[l])
        for m in range(2 * HALF):
            out_v[m, l] = y[ROWS * m : ROWS * m + ROWS] * (scale * live[m])
        store(l).start()

    @pl.loop(0, LEVELS)
    def _(l):
        store(l).wait()


def kernel(
    alpha_hbm, pert_hbm, cot_hbm, dy_ref, dx_ref, gm_ref, w_hbm, pc_ref, src_hbm, dst_hbm,
    inc_hbm, back_hbm, de_hbm, mt_hbm, pb_hbm, qb_hbm, kk_hbm,
    alpha_v, pert_v, cot_raw, cot_v, w_v, src_v, dst_v,
    rep_v, yt, ytail, xt, mt, zf, pb, qb, kk,
    za, zr, zo, de, za2, zr2, zo2, de2,
    sf, sp, ss, sr, bq, back, ps, pr, lq, low, lows, inc_v, scol_v, dcol_v,
    in_sem, w_sem, out_sem, z_sem, z2_sem,
    sp_s, sp_r, ss_s, ss_r, rs_s, rs_r, lo_s, lo_f, lo_r, bk_s, bk_r,
):
    g = lax.axis_index("mem")
    t = lax.axis_index("tile")

    chip = t // 2
    core = lax.rem(t, 2)
    partner = t + 1 - 2 * core

    def chip_peer(k):
        return lax.rem(chip + k, CHIPS)

    def chip_back(k):
        return lax.rem(chip + CHIPS - k, CHIPS)

    def tile_of(ch):
        return 2 * ch + core

    def mem_peer(k):
        return lax.rem(g + k, LEVELS)

    def to_tile(src, dst, ssem, rsem, s):
        return pltpu.make_async_remote_copy(
            src_ref=src, dst_ref=dst, send_sem=ssem, recv_sem=rsem,
            device_id={"tile": s}, device_id_type=MESH,
        )

    def to_mem(src, dst, ssem, rsem, s):
        return pltpu.make_async_remote_copy(
            src_ref=src, dst_ref=dst, send_sem=ssem, recv_sem=rsem,
            device_id={"mem": s}, device_id_type=MESH,
        )

    loads = [
        pltpu.make_async_copy(alpha_hbm, alpha_v, in_sem.at[0]),
        pltpu.make_async_copy(cot_hbm, cot_raw, in_sem.at[1]),
        pltpu.make_async_copy(src_hbm.at[t], src_v, in_sem.at[2]),
        pltpu.make_async_copy(dst_hbm.at[t], dst_v, in_sem.at[3]),
        pltpu.make_async_copy(pert_hbm, pert_v, in_sem.at[4]),
    ]

    def wait_all(buf, sem, count):
        part = buf.at[pl.ds(0, count - 1)]
        pltpu.make_async_copy(part, part, sem).wait()

    def w_load(s):
        return pltpu.make_async_copy(w_hbm.at[0, s], w_v.at[s], w_sem.at[s])

    for c in loads:
        c.start()

    @pl.loop(0, TILES)
    def _(i):
        late = i // CHIPS
        w_load(2 * chip_peer(i - CHIPS * late + 1) + 1 - core + late * (2 * core - 1)).start()

    barrier = pltpu.get_barrier_semaphore()

    @pl.loop(1, TILES)
    def _(k):
        pl.semaphore_signal(
            barrier, inc=1, device_id={"tile": lax.rem(t + k, TILES)}, device_id_type=MESH
        )

    @pl.loop(1, LEVELS)
    def _(k):
        pl.semaphore_signal(barrier, inc=1, device_id={"mem": mem_peer(k)}, device_id_type=MESH)

    scale, live = members(gm_ref)

    for k in range(16):
        rep_v[:, 32 * k : 32 * k + 32] = dy_ref[...]
    a = rep_v[...]
    pos = lax.broadcasted_iota(jnp.int32, (8, 512), 1) & 31
    logs, h = scans(a, pos, 512, ROWS)
    c = coefficient(a)
    ltot = jnp.broadcast_to(logs[:, 31:32], (8, 512))
    lane512 = lax.broadcasted_iota(jnp.int32, (8, 512), 1)
    hsum = jnp.sum(jnp.where(lane512 < 32, jnp.exp(2.0 * logs), 0.0), axis=1, keepdims=True)
    for f, x in enumerate(
        (logs, c, c * h, c * h * jnp.exp(logs), c * jnp.exp(ltot - logs))
    ):
        yt[:, f, :] = x
    yt[:, 5:8, :] = jnp.zeros((LEVELS, 3, 512), F32)
    ytail[:, 0, :] = jnp.broadcast_to(jnp.exp(ltot[:, 0:1]), (LEVELS, COLS))
    ytail[:, 1, :] = jnp.broadcast_to(hsum, (LEVELS, COLS))
    lane_y = lax.broadcasted_iota(jnp.int32, (ROWS, 512), 1)
    lower = lax.broadcasted_iota(jnp.int32, (ROWS, 512), 0) >= (lane_y & 31)
    zr_i = lax.broadcasted_iota(jnp.int32, (16, 256), 0)
    zc_i = lax.broadcasted_iota(jnp.int32, (16, 256), 1) >> 5

    def columns(rows):
        width = rows.shape[1]
        return jnp.transpose(jnp.concatenate([rows, jnp.zeros((120, width), F32)], axis=0))

    @pl.loop(0, LEVELS)
    def _(l):
        rows = yt[l]
        cols = columns(rows[:, 0:128])[0:ROWS]

        def col(f):
            return cols[:, f : f + 1]

        e = jnp.exp(-jnp.abs(col(0) - rows[0:1]))
        m = e * jnp.where(lower, col(2) * rows[1:2], col(1) * rows[2:3])
        part = lane_y >> 5
        mh, ml = split(m)
        m = jnp.where((part >= HALF) & (part < 2 * HALF), ml.astype(F32), mh.astype(F32))
        part = jnp.where(part < 3 * HALF, part % HALF, -1)
        for i in range(HALF):
            mt[l, ROWS * i : ROWS * i + ROWS, :] = jnp.where(part == i, m, 0.0).astype(BF16)
        z = jnp.where(zr_i == zc_i, rows[4:5, 0:256], 0.0) + jnp.where(zr_i == zc_i + 8, rows[3:4, 0:256], 0.0)
        z = jnp.where(zc_i < HALF, z, 0.0)
        zh, zl = split(z)
        zf[l, 0:16, :] = zh[:, 0:PACK]
        zf[l, 16:32, :] = zl[:, 0:PACK]
        pb[l] = jnp.broadcast_to(col(3), (ROWS, 128))
        qb[l] = jnp.broadcast_to(col(4), (ROWS, 128))

    low[:, QROWS:128, :] = jnp.zeros((TILES, 128 - QROWS, 128), BF16)

    loads[1].wait()

    @pl.loop(0, DROWS // 16)
    def _(i):
        rows = [
            cot_raw[:, pl.ds(pl.multiple_of(2048 * i + 128 * r, 128), 128)].astype(F32)
            for r in range(16)
        ]
        cot_v[pl.ds(pl.multiple_of(16 * i, 16), 16), :] = jnp.concatenate(rows, axis=0).astype(BF16)

    loads[0].wait()
    pl.semaphore_wait(barrier, TILES - 1 + LEVELS - 1)

    def alpha_of(l, half):
        return alpha_v[HALF * half : HALF * half + HALF, l].reshape(PACK, COLS)

    def source(l, hi, lo=None):
        r = dot(zf[l], hi)
        z = r[0:16] + r[16:32]
        if lo is not None:
            z = z + dot(zf[l, 0:16, :], lo)
        return z

    def sources(field, za, zr, sem, first, last):
        @pl.loop(first, last)
        def _(k):
            found = []
            for i in range(2):
                l = lax.rem(chip + 2 * k + i + 1, LEVELS)
                for half in range(2):
                    found.append((half, l, source(l, *field(l, half))))
            for half, l, z in found:
                for j in range(3):
                    part = z[:, 128 * j : 128 * j + 128]
                    za[half, l, HALF * j : HALF * j + HALF, :] = part[0:HALF]
                    za[half, l, 16 + HALF * j : 16 + HALF * j + HALF, :] = part[8 : 8 + HALF]
                za[half, l, 15:16, :] = ytail[l, 0:1, 0:128]
                za[half, l, 31:32, :] = ytail[l, 1:2, 0:128]
            for half, l, _z in found:

                @pl.when(2 * l + half != t)
                def _():
                    to_tile(za.at[half, l], zr.at[t], sem.at[0], sem.at[1], 2 * l + half).start()

        if last == LEVELS // 2:
            zr[t] = za[core, chip]

    def recursion(zr, zo, de, sem):
        wait_all(zr, sem.at[1], TILES)
        d = jnp.zeros((16, 128), F32)
        downs = []
        for s in range(TILES):
            downs.append(d)
            zo[s, 0:16, :] = d
            d = zr[s, 15:16, :] * d + zr[s, 0:16, :]
        e = jnp.zeros((16, 128), F32)
        for s in reversed(range(TILES)):
            zo[s, 16:32, :] = e
            e = zr[s, 15:16, :] * e + (zr[s, 16:32, :] + zr[s, 31:32, :] * downs[s])

        @pl.loop(1, TILES)
        def _(k):
            s = lax.rem(t + k, TILES)
            to_tile(zo.at[s], de.at[core, chip], sem.at[2], sem.at[3], s).start()

        de[core, chip] = zo[t]

    def carries_in(zo, sem):
        wait_all(zo, sem.at[3], TILES)

    def carries_sent(zo, sem):
        wait_all(zo, sem.at[0], TILES)
        wait_all(zo, sem.at[2], TILES)

    sources(lambda l, half: (alpha_of(l, half),), za, zr, z_sem, 0, LEVELS // 2)

    lane1 = lax.broadcasted_iota(jnp.int32, (1, 128), 1)
    lane = lax.broadcasted_iota(jnp.int32, (SLOTS, 128), 1)
    lgroup = lane >> 5
    slot_id = lax.broadcasted_iota(jnp.int32, (SLOTS, 128), 0)
    r16 = lax.broadcasted_iota(jnp.int32, (16, 128), 0) - (
        lax.broadcasted_iota(jnp.int32, (16, 128), 1) >> 5
    )
    sub96 = lax.broadcasted_iota(jnp.int32, (QROWS, 128), 0)
    sub384 = lax.broadcasted_iota(jnp.int32, (DROWS, 128), 0)

    def one_hot(condition):
        return jnp.where(condition, 1.0, 0.0).astype(BF16)

    def source_row(s):
        return jnp.where(lane1 < pc_ref[t, s], src_v[pl.ds(s, 1), :], -1)

    def target_row(s):
        return dst_v[pl.ds(s, 1), :]

    def spread_out(x):
        x = x + pltpu.roll(x, 64, 1)
        return x + pltpu.roll(x, 32, 1)

    def weight_pair(s, i):
        return jnp.concatenate(
            [
                w_v[s, 16 * (i + half) : 16 * (i + half) + 16].reshape(16 * BLK, 128)
                for half in range(2)
            ],
            axis=1,
        )

    def back_terms(tiles):
        srows = [source_row(s) for s in tiles]
        scols = [scol_v[s] for s in tiles]
        dcols = [dcol_v[s] for s in tiles]
        pick = jnp.concatenate(
            [
                jnp.concatenate([one_hot(lane + 128 * k == dcol) for k in range(3)], axis=1)
                for dcol in dcols
            ],
            axis=0,
        )
        grad = dot(pick, cot_v[...]).astype(BF16)
        results = []
        for n, s in enumerate(tiles):
            parts = []
            for i in range(0, 8, 2):
                first = SLOTS * n + 16 * i
                zero = jnp.zeros((16, 128), BF16)
                pair = jnp.concatenate(
                    [
                        jnp.concatenate([grad[first : first + 16], zero], axis=1),
                        jnp.concatenate([zero, grad[first + 16 : first + 32]], axis=1),
                    ],
                    axis=0,
                )
                o = dot_nt(pair, weight_pair(s, i))
                for half in range(2):
                    parts.append(
                        sum(
                            jnp.where(
                                r16 == 4 * j,
                                o[16 * half : 16 * half + 16, 128 * j : 128 * j + 128],
                                0.0,
                            )
                            for j in range(4)
                        )
                    )
            terms = spread_out(jnp.concatenate(parts, axis=0))
            terms = jnp.where(lgroup == (scols[n] & 3), terms, 0.0)
            put = one_hot(sub96 == (srows[n] >> 2))
            both = dot(put, jnp.concatenate(split(terms), axis=1))
            results.append(both[:, 0:128] + both[:, 128:256])
        return results

    def forward_terms(tiles):
        puts, sums = [], []
        for s in tiles:
            scol = scol_v[s]
            picked = dot(one_hot(lane == (scol >> 2)), low[s])
            picked = spread_out(jnp.where(lgroup == (scol & 3), picked, 0.0))
            parts = []
            for i in range(0, 8, 2):
                xs = []
                for half in range(2):
                    x = picked[16 * (i + half) : 16 * (i + half) + 16]
                    xs.append(
                        jnp.concatenate([jnp.where(r16 == 4 * j, x, 0.0) for j in range(4)], axis=1)
                    )
                both = dot(jnp.concatenate(xs, axis=0).astype(BF16), weight_pair(s, i))
                parts.append(both[0:16, 0:128])
                parts.append(both[16:32, 128:256])
            sums.append(jnp.concatenate(split(jnp.concatenate(parts, axis=0)), axis=1))
            puts.append(one_hot(sub384 == target_row(s)))
        both = dot(jnp.concatenate(puts, axis=1), jnp.concatenate(sums, axis=0))
        return both[:, 0:128] + both[:, 128:256]

    loads[2].wait()
    loads[3].wait()
    turned = jnp.transpose(
        jnp.concatenate([src_v[...], dst_v[...], jnp.zeros((96, SLOTS), jnp.int32)], axis=0).astype(F32)
    ).astype(jnp.int32)
    for s in range(TILES):
        scol = jnp.broadcast_to(turned[:, s : s + 1], (SLOTS, 128))
        scol_v[s] = jnp.where(slot_id < pc_ref[t, s], scol, -1)
        dcol_v[s] = jnp.broadcast_to(turned[:, TILES + s : TILES + s + 1], (SLOTS, 128))

    def off_chip(ch):
        return to_tile(ss.at[ch], sr.at[chip], ss_s, ss_r, tile_of(ch))

    def core_pair(ch):
        return to_tile(sf.at[0, ch], sp.at[ch], sp_s, sp_r.at[ch], partner)

    steps = TILES // GROUP

    @pl.loop(0, steps)
    def _(j):
        late = j // (steps // 2)
        chips = [chip_peer(GROUP * (j - steps // 2 * late) + 1 + i) for i in range(GROUP)]
        tiles = [2 * ch + 1 - core + late * (2 * core - 1) for ch in chips]
        for s in tiles:
            w_load(s).wait()
        for ch, r in zip(chips, back_terms(tiles)):
            sf[late, ch] = r

        @pl.when(late == 0)
        def _():
            for ch in chips:
                core_pair(ch).start()

        @pl.when(late == 1)
        def _():
            for ch in chips:
                core_pair(ch).wait_recv()
                ss[ch] = sf[1, ch] + sp[ch]

                @pl.when(ch != chip)
                def _():
                    off_chip(ch).start()

        @pl.when(j == steps // 2 - 1)
        def _():
            recursion(zr, zo, de, z_sem)

    sr[chip] = ss[chip]

    ax = dx_ref[...]
    posx = lax.broadcasted_iota(jnp.int32, (8, COLS), 1)
    lx, hx = scans(ax, posx, COLS, COLS)
    cx = coefficient(ax)
    gx = cx * hx
    edge1 = jnp.broadcast_to(lx[:, 127:128], (8, COLS))
    edge2 = jnp.broadcast_to(lx[:, 255:256], (8, COLS))
    xt[:, 0, :] = lx
    xt[:, 1, :] = cx
    xt[:, 2, :] = gx
    xt[:, 3, :] = gx * jnp.exp(jnp.minimum(lx - jnp.where(posx < 256, edge1, edge2), 0.0))
    xt[:, 4, :] = cx * jnp.exp(jnp.minimum(edge1 - lx, 0.0))
    xt[:, 5, :] = cx * jnp.exp(jnp.minimum(edge2 - lx, 0.0))
    xt[:, 6:8, :] = jnp.zeros((LEVELS, 2, COLS), F32)
    lowx = lax.broadcasted_iota(jnp.int32, (128, 128), 0) >= (
        lax.broadcasted_iota(jnp.int32, (128, 128), 1)
    )

    @pl.loop(0, LEVELS)
    def _(l):
        rows = xt[l]
        cols = columns(rows)
        for ib in range(3):
            for jb in range(3):
                r = rows[:, 128 * jb : 128 * jb + 128]

                def xcol(f):
                    return cols[128 * ib : 128 * ib + 128, f : f + 1]

                if ib == jb:
                    e = jnp.exp(-jnp.abs(xcol(0) - r[0:1]))
                    m = e * jnp.where(lowx, xcol(2) * r[1:2], xcol(1) * r[2:3])
                elif ib > jb:
                    m = xcol(3) * r[3 + ib : 4 + ib]
                else:
                    m = xcol(3 + jb) * r[3:4]
                mh, ml = split(m)
                kk[l, 128 * ib : 128 * ib + 128, 128 * jb : 128 * jb + 128] = mh
                at = COLS + 128 * ib
                kk[l, at : at + 128, 128 * jb : 128 * jb + 128] = ml

    exports = [
        pltpu.make_async_copy(x, y, out_sem.at[i])
        for i, (x, y) in enumerate(
            [
                (mt, mt_hbm), (pb, pb_hbm), (qb, qb_hbm), (kk.at[:, pl.ds(0, COLS), :], kk_hbm),
                (back, back_hbm), (de2, de_hbm), (inc_v, inc_hbm),
            ]
        )
    ]
    for x in exports[:4]:
        x.start()

    wait_all(sr, ss_r, CHIPS)
    acc = sr[0]
    for s in range(1, CHIPS):
        acc = acc + sr[s]
    bq[...] = acc
    for j in range(3):
        back[g, :, 128 * j : 128 * j + 128] = bq[pl.ds(j, ROWS, stride=3), :].astype(BF16)

    @pl.loop(1, LEVELS)
    def _(k):
        l = mem_peer(k)
        to_mem(back.at[g], back.at[g], bk_s, bk_r, l).start()

    loads[4].wait()
    carries_in(zo, z_sem)

    def partial(l):
        y = smooth(
            [(alpha_of(l, half),) for half in range(2)], (de[0, l], de[1, l]),
            mt[l], pb[l], qb[l], kk[l, 0:COLS], kk[l, COLS : 2 * COLS],
        )
        acc = jnp.zeros((ROWS, COLS), F32)
        for m in range(2 * HALF):
            acc = acc + (live[m] * pert_v[m, l].astype(F32)) * y[ROWS * m : ROWS * m + ROWS]
        return acc

    @pl.loop(1, LEVELS + 1)
    def _(k):
        l = mem_peer(k)
        ps[l] = partial(l)

        @pl.when(l != g)
        def _():
            to_mem(ps.at[l], pr.at[g], rs_s, rs_r, l).start()

    pr[g] = ps[g]

    wait_all(back, bk_r, LEVELS)
    exports[4].start()

    def weighted(l, half):
        x = pert_v[HALF * half : HALF * half + HALF, l].astype(F32) * back[l].astype(F32)[None]
        return split(x.reshape(PACK, COLS))

    sources(weighted, za2, zr2, z2_sem, 0, 2)

    wait_all(pr, rs_r, LEVELS)
    acc = pr[0]
    for s in range(1, LEVELS):
        acc = acc + pr[s]
    acc = acc * scale
    for j in range(3):
        lq[pl.ds(j, ROWS, stride=3), :] = acc[:, 128 * j : 128 * j + 128]
    lows[...] = lq[...].astype(BF16)

    def low_rows(s):
        return low.at[s, pl.ds(0, QROWS), :]

    def low_to(s):
        return to_tile(lows, low_rows(t), lo_s, lo_r.at[t], s)

    def low_on(s):
        return to_tile(low_rows(s), low_rows(s), lo_f, lo_r.at[s], partner)

    @pl.loop(1, CHIPS)
    def _(k):
        low_to(tile_of(chip_peer(k))).start()

    low_to(partner).start()

    low[t, 0:QROWS, :] = lows[...]

    sources(weighted, za2, zr2, z2_sem, 2, 4)

    inc_v[...] = jnp.zeros((DROWS, 128), F32)

    @pl.loop(0, steps)
    def _(j):
        tiles = []
        for i in range(GROUP):
            n = GROUP * j + i
            afar = (n + TILES - 2) // TILES
            late = n // (CHIPS + 1)
            ch = chip_back(afar * (n - 1 - (CHIPS - 1) * late))
            s = 2 * ch + core + (late + (1 - afar) * lax.rem(n, 2)) * (1 - 2 * core)
            tiles.append(s)

            @pl.when(n > 0)
            def _():
                low_on(s).wait_recv()

            @pl.when((afar == 1) & (late == 0))
            def _():
                low_on(s).start()

        inc_v[...] += forward_terms(tiles)

        @pl.when(j == steps // 2 - 1)
        def _():
            recursion(zr2, zo2, de2, z2_sem)

    exports[6].start()
    carries_in(zo2, z2_sem)
    exports[5].start()

    carries_sent(zo, z_sem)
    carries_sent(zo2, z2_sem)
    pltpu.make_async_copy(sp, sp, sp_s).wait()
    wait_all(ss, ss_s, CHIPS)
    lows8 = low.at[pl.ds(0, CHIPS), pl.ds(0, QROWS), :]
    pltpu.make_async_copy(lows8, lows8, lo_s).wait()
    lows7 = low.at[pl.ds(0, CHIPS - 1), pl.ds(0, QROWS), :]
    pltpu.make_async_copy(lows7, lows7, lo_f).wait()
    wait_all(ps, rs_s, LEVELS)
    wait_all(back, bk_s, LEVELS)
    for x in exports:
        x.wait()


def shards(
    alpha, perturbation, cotangent, decay_y, decay_x, group_members, interp_weight,
    pair_count, src_index, dst_index,
):
    any_spec = pl.BlockSpec(memory_space=pl.ANY)
    vmem = pl.BlockSpec(memory_space=pltpu.VMEM)
    smem = pl.BlockSpec(memory_space=pltpu.SMEM)
    dma = pltpu.SemaphoreType.DMA
    V = pltpu.VMEM
    zbuf = V((TILES, 32, 128), F32)
    zpair = V((2, CHIPS, 32, 128), F32)
    zall = [zpair, zbuf, zbuf, zpair]
    scratch = [
        V((2 * HALF, LEVELS, ROWS, COLS), BF16),
        V((2 * HALF, LEVELS, ROWS, COLS), BF16),
        V((1, DROWS * 128), BF16),
        V((DROWS, 128), BF16),
        V((TILES, SLOTS, BLK, 128), BF16),
        V((TILES, SLOTS), jnp.int32),
        V((TILES, SLOTS), jnp.int32),
        V((8, 512), F32),
        V((LEVELS, 8, 512), F32),
        V((LEVELS, 2, COLS), F32),
        V((LEVELS, 8, COLS), F32),
        V((LEVELS, PACK, 512), BF16),
        V((LEVELS, 32, PACK), BF16),
        V((LEVELS, ROWS, 128), F32),
        V((LEVELS, ROWS, 128), F32),
        V((LEVELS, 2 * COLS, COLS), BF16),
        *zall,
        *zall,
        V((2, CHIPS, QROWS, 128), F32),
        V((CHIPS, QROWS, 128), F32),
        V((CHIPS, QROWS, 128), F32),
        V((CHIPS, QROWS, 128), F32),
        V((QROWS, 128), F32),
        V((LEVELS, ROWS, COLS), BF16),
        V((LEVELS, ROWS, COLS), F32),
        V((LEVELS, ROWS, COLS), F32),
        V((QROWS, 128), F32),
        V((TILES, 128, 128), BF16),
        V((QROWS, 128), BF16),
        V((DROWS, 128), F32),
        V((TILES, SLOTS, 128), jnp.int32),
        V((TILES, SLOTS, 128), jnp.int32),
        dma((5,)),
        dma((TILES,)),
        dma((7,)),
        dma((4,)),
        dma((4,)),
        dma,
        dma((CHIPS,)),
        *[dma] * 6,
        dma((TILES,)),
        dma,
        dma,
    ]
    shape = jax.ShapeDtypeStruct
    inc, *rest = pl.pallas_call(
        kernel,
        out_shape=(
            shape((DROWS, 128), F32),
            shape((LEVELS, ROWS, COLS), BF16),
            shape((2, CHIPS, 32, 128), F32),
            shape((LEVELS, PACK, 512), BF16),
            shape((LEVELS, ROWS, 128), F32),
            shape((LEVELS, ROWS, 128), F32),
            shape((LEVELS, COLS, COLS), BF16),
        ),
        in_specs=[any_spec, any_spec, any_spec, vmem, vmem, smem, any_spec, smem, any_spec, any_spec],
        out_specs=(any_spec,) * 7,
        scratch_shapes=scratch,
        compiler_params=pltpu.CompilerParams(
            collective_id=0, has_side_effects=True, vmem_limit_bytes=60 * 1024 * 1024
        ),
        cost_estimate=pl.CostEstimate(
            flops=9_000_000_000, bytes_accessed=29_000_000, transcendentals=700_000
        ),
    )(
        alpha, perturbation, cotangent, decay_y, decay_x, group_members,
        interp_weight, pair_count, src_index, dst_index,
    )

    members_shape = (2 * HALF, LEVELS, ROWS, COLS)
    return pl.pallas_call(
        grad_kernel,
        out_shape=(shape((1, DROWS * 128), F32), shape(alpha.shape, F32)),
        in_specs=[smem, *[any_spec] * 7, vmem],
        out_specs=(vmem, any_spec),
        scratch_shapes=[
            V(members_shape, BF16),
            V((LEVELS, ROWS, COLS), BF16),
            V((2, CHIPS, 32, 128), F32),
            V((LEVELS, PACK, 512), BF16),
            V((LEVELS, ROWS, 128), F32),
            V((LEVELS, ROWS, 128), F32),
            V((LEVELS, COLS, COLS), BF16),
            V(members_shape, F32),
            dma((5,)),
            dma((2, LEVELS)),
            dma((LEVELS,)),
        ],
        compiler_params=pltpu.CompilerParams(vmem_limit_bytes=60 * 1024 * 1024),
        cost_estimate=pl.CostEstimate(
            flops=3_500_000_000, bytes_accessed=11_000_000, transcendentals=0
        ),
    )(group_members, perturbation, *rest, inc)


def solution(mesh):
    in_specs = (
        P("mem", None, "tile", None),
        P("mem", None, "tile", None),
        P("mem", "tile"),
        P(None, "tile"),
        P(),
        P(),
        P("tile", None, None, None, None),
        P(),
        P(),
        P(),
    )
    out_specs = (P("mem", "tile"), P("mem", None, "tile", None))
    return jax.shard_map(shards, mesh=mesh, in_specs=in_specs, out_specs=out_specs, check_vma=False)
```

```python
import jax
import jax.numpy as jnp
from jax import lax
from jax.experimental import pallas as pl
from jax.experimental.pallas import tpu as pltpu
from jax.sharding import PartitionSpec as P

MESH = pl.DeviceIdType.MESH
F32 = jnp.float32
BF16 = jnp.bfloat16

LEVELS = 8
TILES = 16
CHIPS = 8
ROWS = 32
COLS = 384
HALF = 5
PACK = HALF * ROWS
SLOTS = 128
BLK = 32
QROWS = ROWS * COLS // 128
DROWS = 384
GROUP = 2


def dot(a, b):
    return lax.dot_general(a, b, (((1,), (0,)), ((), ())), preferred_element_type=F32)


def dot_nt(a, b):
    return lax.dot_general(a, b, (((1,), (1,)), ((), ())), preferred_element_type=F32)


def split(x):
    high = x.astype(BF16)
    return high, (x - high.astype(F32)).astype(BF16)


def coefficient(a):
    t = 1.0 - a * a
    ratio = (t * t * t) / (1.0 + a * a)
    return jnp.where(ratio > 0.0, jnp.sqrt(jnp.sqrt(jnp.maximum(ratio, 1e-37))), 0.0)


def scans(a, pos, width, segment):
    logs = jnp.log(a)
    steps = [1 << b for b in range(16) if (1 << b) < segment]
    for k in steps:
        logs = logs + jnp.where(pos >= k, pltpu.roll(logs, k, 1), 0.0)
    rate = jnp.where(pos < segment - 1, pltpu.roll(a * a, width - 1, 1), 0.0)
    h = jnp.ones_like(a)
    for k in steps:
        h = h + rate * pltpu.roll(h, width - k, 1)
        rate = rate * pltpu.roll(rate, width - k, 1)
    return logs, h


def carry_row(carry, first):
    rows = [carry[first + HALF * j : first + HALF * j + 1, :] for j in range(3)]
    return jnp.concatenate(rows, axis=1)


def smooth(fields, carries, mt, pb, qb, upper, lower=None):
    p3 = jnp.concatenate([pb] * 3, axis=1)
    q3 = jnp.concatenate([qb] * 3, axis=1)
    rows = []
    for field, carry in zip(fields, carries):
        hi, *lo = field
        stack = jnp.concatenate([hi, hi, *lo], axis=0)
        y = dot(mt[:, 0 : stack.shape[0]], stack)
        for m in range(HALF):
            rows.append(
                y[ROWS * m : ROWS * m + ROWS]
                + p3 * carry_row(carry, m)
                + q3 * carry_row(carry, 16 + m)
            )
    yh, yl = split(jnp.concatenate(rows, axis=0))
    if lower is None:
        return dot(jnp.concatenate([yh, yl], axis=1), jnp.concatenate([upper] * 2, axis=0))
    return dot(
        jnp.concatenate([yh, yl, yh], axis=1), jnp.concatenate([upper, upper, lower], axis=0)
    )


def members(gm_ref):
    own = gm_ref[lax.axis_index("mem")]
    total = gm_ref[0]
    for i in range(1, LEVELS):
        total = total + gm_ref[i]
    scale = 1.0 / jnp.sqrt(jnp.full((1, COLS), total.astype(F32) - 1.0, F32))
    return scale, [jnp.where(m < own, 1.0, 0.0).astype(F32) for m in range(2 * HALF)]


def grad_kernel(
    gm_ref, pert_hbm, back_hbm, de_hbm, mt_hbm, pb_hbm, qb_hbm, kk_hbm, inc_ref,
    inc_out, grad_hbm,
    pert_v, back_v, de_v, mt_v, pb_v, qb_v, kk_v, out_v, whole_sem, in_sem, out_sem,
):
    whole = [
        pltpu.make_async_copy(a, b, whole_sem.at[i])
        for i, (a, b) in enumerate(
            [(back_hbm, back_v), (de_hbm, de_v), (pb_hbm, pb_v), (qb_hbm, qb_v)]
        )
    ]

    def loads(l):
        return [
            pltpu.make_async_copy(pert_hbm.at[:, l], pert_v.at[:, l], in_sem.at[0, l]),
            pltpu.make_async_copy(kk_hbm.at[l], kk_v.at[l], in_sem.at[1, l]),
            pltpu.make_async_copy(mt_hbm.at[l], mt_v.at[l], in_sem.at[2, l]),
        ]

    def store(l):
        return pltpu.make_async_copy(out_v.at[:, l], grad_hbm.at[:, l], out_sem.at[l])

    for x in whole:
        x.start()

    @pl.loop(0, LEVELS)
    def _(l):
        for x in loads(l):
            x.start()

    scale, live = members(gm_ref)

    @pl.loop(0, DROWS // 8)
    def _(i):
        x = inc_ref[pl.ds(pl.multiple_of(8 * i, 8), 8), :]
        for r in range(8):
            inc_out[0:1, pl.ds(pl.multiple_of(1024 * i + 128 * r, 128), 128)] = x[r : r + 1, :]

    for x in whole:
        x.wait()

    @pl.loop(0, LEVELS)
    def _(l):
        for x in loads(l):
            x.wait()
        fields = []
        for half in range(2):
            x = pert_v[HALF * half : HALF * half + HALF, l].astype(F32) * back_v[l].astype(F32)[None]
            fields.append(split(x.reshape(PACK, COLS)))
        y = smooth(fields, (de_v[0, l], de_v[1, l]), mt_v[l], pb_v[l], qb_v[l], kk_v[l])
        for m in range(2 * HALF):
            out_v[m, l] = y[ROWS * m : ROWS * m + ROWS] * (scale * live[m])
        store(l).start()

    @pl.loop(0, LEVELS)
    def _(l):
        store(l).wait()


def kernel(
    alpha_hbm, pert_hbm, cot_hbm, dy_ref, dx_ref, gm_ref, w_hbm, pc_ref, src_hbm, dst_hbm,
    inc_hbm, back_hbm, de_hbm, mt_hbm, pb_hbm, qb_hbm, kk_hbm,
    alpha_v, pert_v, cot_raw, cot_v, w_v, src_v, dst_v,
    rep_v, yt, ytail, xt, mt, zf, pb, qb, kk,
    za, zr, zo, de, za2, zr2, zo2, de2,
    sf, sp, ss, sr, bq, back, ps, pr, lq, low, lows, inc_v, scol_v, dcol_v,
    in_sem, w_sem, out_sem, z_sem, z2_sem,
    sp_s, sp_r, ss_s, ss_r, rs_s, rs_r, lo_s, lo_f, lo_r, bk_s, bk_r,
):
    g = lax.axis_index("mem")
    t = lax.axis_index("tile")

    chip = t // 2
    core = lax.rem(t, 2)
    partner = t + 1 - 2 * core

    def chip_peer(k):
        return lax.rem(chip + k, CHIPS)

    def chip_back(k):
        return lax.rem(chip + CHIPS - k, CHIPS)

    def tile_of(ch):
        return 2 * ch + core

    def mem_peer(k):
        return lax.rem(g + k, LEVELS)

    def to_tile(src, dst, ssem, rsem, s):
        return pltpu.make_async_remote_copy(
            src_ref=src, dst_ref=dst, send_sem=ssem, recv_sem=rsem,
            device_id={"tile": s}, device_id_type=MESH,
        )

    def to_mem(src, dst, ssem, rsem, s):
        return pltpu.make_async_remote_copy(
            src_ref=src, dst_ref=dst, send_sem=ssem, recv_sem=rsem,
            device_id={"mem": s}, device_id_type=MESH,
        )

    loads = [
        pltpu.make_async_copy(alpha_hbm, alpha_v, in_sem.at[0]),
        pltpu.make_async_copy(cot_hbm, cot_raw, in_sem.at[1]),
        pltpu.make_async_copy(src_hbm.at[t], src_v, in_sem.at[2]),
        pltpu.make_async_copy(dst_hbm.at[t], dst_v, in_sem.at[3]),
        pltpu.make_async_copy(pert_hbm, pert_v, in_sem.at[4]),
    ]

    def wait_all(buf, sem, count):
        part = buf.at[pl.ds(0, count - 1)]
        pltpu.make_async_copy(part, part, sem).wait()

    def w_load(s):
        return pltpu.make_async_copy(w_hbm.at[0, s], w_v.at[s], w_sem.at[s])

    for c in loads[:4]:
        c.start()

    @pl.loop(0, TILES)
    def _(i):
        late = i // CHIPS
        w_load(2 * chip_peer(i - CHIPS * late + 1) + 1 - core + late * (2 * core - 1)).start()

    loads[4].start()

    barrier = pltpu.get_barrier_semaphore()

    @pl.loop(1, TILES)
    def _(k):
        pl.semaphore_signal(
            barrier, inc=1, device_id={"tile": lax.rem(t + k, TILES)}, device_id_type=MESH
        )

    @pl.loop(1, LEVELS)
    def _(k):
        pl.semaphore_signal(barrier, inc=1, device_id={"mem": mem_peer(k)}, device_id_type=MESH)

    scale, live = members(gm_ref)

    for k in range(16):
        rep_v[:, 32 * k : 32 * k + 32] = dy_ref[...]
    a = rep_v[...]
    pos = lax.broadcasted_iota(jnp.int32, (8, 512), 1) & 31
    logs, h = scans(a, pos, 512, ROWS)
    c = coefficient(a)
    ltot = jnp.broadcast_to(logs[:, 31:32], (8, 512))
    lane512 = lax.broadcasted_iota(jnp.int32, (8, 512), 1)
    hsum = jnp.sum(jnp.where(lane512 < 32, jnp.exp(2.0 * logs), 0.0), axis=1, keepdims=True)
    for f, x in enumerate(
        (logs, c, c * h, c * h * jnp.exp(logs), c * jnp.exp(ltot - logs))
    ):
        yt[:, f, :] = x
    yt[:, 5:8, :] = jnp.zeros((LEVELS, 3, 512), F32)
    ytail[:, 0, :] = jnp.broadcast_to(jnp.exp(ltot[:, 0:1]), (LEVELS, COLS))
    ytail[:, 1, :] = jnp.broadcast_to(hsum, (LEVELS, COLS))
    lane_y = lax.broadcasted_iota(jnp.int32, (ROWS, 512), 1)
    lower = lax.broadcasted_iota(jnp.int32, (ROWS, 512), 0) >= (lane_y & 31)
    zr_i = lax.broadcasted_iota(jnp.int32, (16, 256), 0)
    zc_i = lax.broadcasted_iota(jnp.int32, (16, 256), 1) >> 5

    def columns(rows):
        width = rows.shape[1]
        return jnp.transpose(jnp.concatenate([rows, jnp.zeros((120, width), F32)], axis=0))

    @pl.loop(0, LEVELS)
    def _(l):
        rows = yt[l]
        cols = columns(rows[:, 0:128])[0:ROWS]

        def col(f):
            return cols[:, f : f + 1]

        e = jnp.exp(-jnp.abs(col(0) - rows[0:1]))
        m = e * jnp.where(lower, col(2) * rows[1:2], col(1) * rows[2:3])
        part = lane_y >> 5
        mh, ml = split(m)
        m = jnp.where((part >= HALF) & (part < 2 * HALF), ml.astype(F32), mh.astype(F32))
        part = jnp.where(part < 3 * HALF, part % HALF, -1)
        for i in range(HALF):
            mt[l, ROWS * i : ROWS * i + ROWS, :] = jnp.where(part == i, m, 0.0).astype(BF16)
        z = jnp.where(zr_i == zc_i, rows[4:5, 0:256], 0.0) + jnp.where(zr_i == zc_i + 8, rows[3:4, 0:256], 0.0)
        z = jnp.where(zc_i < HALF, z, 0.0)
        zh, zl = split(z)
        zf[l, 0:16, :] = zh[:, 0:PACK]
        zf[l, 16:32, :] = zl[:, 0:PACK]
        pb[l] = jnp.broadcast_to(col(3), (ROWS, 128))
        qb[l] = jnp.broadcast_to(col(4), (ROWS, 128))

    loads[0].wait()
    pl.semaphore_wait(barrier, TILES - 1 + LEVELS - 1)

    def alpha_of(l, half):
        return alpha_v[HALF * half : HALF * half + HALF, l].reshape(PACK, COLS)

    def source(l, hi, lo=None):
        r = dot(zf[l], hi)
        z = r[0:16] + r[16:32]
        if lo is not None:
            z = z + dot(zf[l, 0:16, :], lo)
        return z

    def sources(field, za, zr, sem, first, last):
        @pl.loop(first, last)
        def _(k):
            found = []
            for i in range(2):
                l = lax.rem(chip + 2 * k + i + 1, LEVELS)
                for half in range(2):
                    found.append((half, l, source(l, *field(l, half))))
            for half, l, z in found:
                for j in range(3):
                    part = z[:, 128 * j : 128 * j + 128]
                    za[half, l, HALF * j : HALF * j + HALF, :] = part[0:HALF]
                    za[half, l, 16 + HALF * j : 16 + HALF * j + HALF, :] = part[8 : 8 + HALF]
                za[half, l, 15:16, :] = ytail[l, 0:1, 0:128]
                za[half, l, 31:32, :] = ytail[l, 1:2, 0:128]
            for half, l, _z in found:

                @pl.when(2 * l + half != t)
                def _():
                    to_tile(za.at[half, l], zr.at[t], sem.at[0], sem.at[1], 2 * l + half).start()

        if last == LEVELS // 2:
            zr[t] = za[core, chip]

    def recursion(zr, zo, de, sem):
        wait_all(zr, sem.at[1], TILES)
        d = jnp.zeros((16, 128), F32)
        downs = []
        for s in range(TILES):
            downs.append(d)
            zo[s, 0:16, :] = d
            d = zr[s, 15:16, :] * d + zr[s, 0:16, :]
        e = jnp.zeros((16, 128), F32)
        for s in reversed(range(TILES)):
            zo[s, 16:32, :] = e
            e = zr[s, 15:16, :] * e + (zr[s, 16:32, :] + zr[s, 31:32, :] * downs[s])

        @pl.loop(1, TILES)
        def _(k):
            s = lax.rem(t + k, TILES)
            to_tile(zo.at[s], de.at[core, chip], sem.at[2], sem.at[3], s).start()

        de[core, chip] = zo[t]

    def carries_in(zo, sem):
        wait_all(zo, sem.at[3], TILES)

    def carries_sent(zo, sem):
        wait_all(zo, sem.at[0], TILES)
        wait_all(zo, sem.at[2], TILES)

    sources(lambda l, half: (alpha_of(l, half),), za, zr, z_sem, 0, LEVELS // 2)

    low[:, QROWS:128, :] = jnp.zeros((TILES, 128 - QROWS, 128), BF16)

    loads[1].wait()

    @pl.loop(0, DROWS // 16)
    def _(i):
        rows = [
            cot_raw[:, pl.ds(pl.multiple_of(2048 * i + 128 * r, 128), 128)].astype(F32)
            for r in range(16)
        ]
        cot_v[pl.ds(pl.multiple_of(16 * i, 16), 16), :] = jnp.concatenate(rows, axis=0).astype(BF16)

    lane1 = lax.broadcasted_iota(jnp.int32, (1, 128), 1)
    lane = lax.broadcasted_iota(jnp.int32, (SLOTS, 128), 1)
    lgroup = lane >> 5
    slot_id = lax.broadcasted_iota(jnp.int32, (SLOTS, 128), 0)
    r16 = lax.broadcasted_iota(jnp.int32, (16, 128), 0) - (
        lax.broadcasted_iota(jnp.int32, (16, 128), 1) >> 5
    )
    sub96 = lax.broadcasted_iota(jnp.int32, (QROWS, 128), 0)
    sub384 = lax.broadcasted_iota(jnp.int32, (DROWS, 128), 0)

    def one_hot(condition):
        return jnp.where(condition, 1.0, 0.0).astype(BF16)

    def source_row(s):
        return jnp.where(lane1 < pc_ref[t, s], src_v[pl.ds(s, 1), :], -1)

    def target_row(s):
        return dst_v[pl.ds(s, 1), :]

    def spread_out(x):
        x = x + pltpu.roll(x, 64, 1)
        return x + pltpu.roll(x, 32, 1)

    def weight_pair(s, i):
        return jnp.concatenate(
            [
                w_v[s, 16 * (i + half) : 16 * (i + half) + 16].reshape(16 * BLK, 128)
                for half in range(2)
            ],
            axis=1,
        )

    def back_terms(tiles):
        srows = [source_row(s) for s in tiles]
        scols = [scol_v[s] for s in tiles]
        dcols = [dcol_v[s] for s in tiles]
        pick = jnp.concatenate(
            [
                jnp.concatenate([one_hot(lane + 128 * k == dcol) for k in range(3)], axis=1)
                for dcol in dcols
            ],
            axis=0,
        )
        grad = dot(pick, cot_v[...]).astype(BF16)
        results = []
        for n, s in enumerate(tiles):
            parts = []
            for i in range(0, 8, 2):
                first = SLOTS * n + 16 * i
                zero = jnp.zeros((16, 128), BF16)
                pair = jnp.concatenate(
                    [
                        jnp.concatenate([grad[first : first + 16], zero], axis=1),
                        jnp.concatenate([zero, grad[first + 16 : first + 32]], axis=1),
                    ],
                    axis=0,
                )
                o = dot_nt(pair, weight_pair(s, i))
                for half in range(2):
                    parts.append(
                        sum(
                            jnp.where(
                                r16 == 4 * j,
                                o[16 * half : 16 * half + 16, 128 * j : 128 * j + 128],
                                0.0,
                            )
                            for j in range(4)
                        )
                    )
            terms = spread_out(jnp.concatenate(parts, axis=0))
            terms = jnp.where(lgroup == (scols[n] & 3), terms, 0.0)
            put = one_hot(sub96 == (srows[n] >> 2))
            both = dot(put, jnp.concatenate(split(terms), axis=1))
            results.append(both[:, 0:128] + both[:, 128:256])
        return results

    def forward_terms(tiles):
        puts, sums = [], []
        for s in tiles:
            scol = scol_v[s]
            picked = dot(one_hot(lane == (scol >> 2)), low[s])
            picked = spread_out(jnp.where(lgroup == (scol & 3), picked, 0.0))
            parts = []
            for i in range(0, 8, 2):
                xs = []
                for half in range(2):
                    x = picked[16 * (i + half) : 16 * (i + half) + 16]
                    xs.append(
                        jnp.concatenate([jnp.where(r16 == 4 * j, x, 0.0) for j in range(4)], axis=1)
                    )
                both = dot(jnp.concatenate(xs, axis=0).astype(BF16), weight_pair(s, i))
                parts.append(both[0:16, 0:128])
                parts.append(both[16:32, 128:256])
            sums.append(jnp.concatenate(split(jnp.concatenate(parts, axis=0)), axis=1))
            puts.append(one_hot(sub384 == target_row(s)))
        both = dot(jnp.concatenate(puts, axis=1), jnp.concatenate(sums, axis=0))
        return both[:, 0:128] + both[:, 128:256]

    loads[2].wait()
    loads[3].wait()
    turned = jnp.transpose(
        jnp.concatenate([src_v[...], dst_v[...], jnp.zeros((96, SLOTS), jnp.int32)], axis=0).astype(F32)
    ).astype(jnp.int32)
    for s in range(TILES):
        scol = jnp.broadcast_to(turned[:, s : s + 1], (SLOTS, 128))
        scol_v[s] = jnp.where(slot_id < pc_ref[t, s], scol, -1)
        dcol_v[s] = jnp.broadcast_to(turned[:, TILES + s : TILES + s + 1], (SLOTS, 128))

    def off_chip(ch):
        return to_tile(ss.at[ch], sr.at[chip], ss_s, ss_r, tile_of(ch))

    def core_pair(ch):
        return to_tile(sf.at[0, ch], sp.at[ch], sp_s, sp_r.at[ch], partner)

    steps = TILES // GROUP

    @pl.loop(0, steps)
    def _(j):
        late = j // (steps // 2)
        chips = [chip_peer(GROUP * (j - steps // 2 * late) + 1 + i) for i in range(GROUP)]
        tiles = [2 * ch + 1 - core + late * (2 * core - 1) for ch in chips]
        for s in tiles:
            w_load(s).wait()
        for ch, r in zip(chips, back_terms(tiles)):
            sf[late, ch] = r

        @pl.when(late == 0)
        def _():
            for ch in chips:
                core_pair(ch).start()

        @pl.when(late == 1)
        def _():
            for ch in chips:
                core_pair(ch).wait_recv()
                ss[ch] = sf[1, ch] + sp[ch]

                @pl.when(ch != chip)
                def _():
                    off_chip(ch).start()

        @pl.when(j == steps // 2)
        def _():
            recursion(zr, zo, de, z_sem)

    sr[chip] = ss[chip]

    ax = dx_ref[...]
    posx = lax.broadcasted_iota(jnp.int32, (8, COLS), 1)
    lx, hx = scans(ax, posx, COLS, COLS)
    cx = coefficient(ax)
    gx = cx * hx
    edge1 = jnp.broadcast_to(lx[:, 127:128], (8, COLS))
    edge2 = jnp.broadcast_to(lx[:, 255:256], (8, COLS))
    xt[:, 0, :] = lx
    xt[:, 1, :] = cx
    xt[:, 2, :] = gx
    xt[:, 3, :] = gx * jnp.exp(jnp.minimum(lx - jnp.where(posx < 256, edge1, edge2), 0.0))
    xt[:, 4, :] = cx * jnp.exp(jnp.minimum(edge1 - lx, 0.0))
    xt[:, 5, :] = cx * jnp.exp(jnp.minimum(edge2 - lx, 0.0))
    xt[:, 6:8, :] = jnp.zeros((LEVELS, 2, COLS), F32)
    lowx = lax.broadcasted_iota(jnp.int32, (128, 128), 0) >= (
        lax.broadcasted_iota(jnp.int32, (128, 128), 1)
    )

    @pl.loop(0, LEVELS)
    def _(l):
        rows = xt[l]
        cols = columns(rows)
        for ib in range(3):
            for jb in range(3):
                r = rows[:, 128 * jb : 128 * jb + 128]

                def xcol(f):
                    return cols[128 * ib : 128 * ib + 128, f : f + 1]

                if ib == jb:
                    e = jnp.exp(-jnp.abs(xcol(0) - r[0:1]))
                    m = e * jnp.where(lowx, xcol(2) * r[1:2], xcol(1) * r[2:3])
                elif ib > jb:
                    m = xcol(3) * r[3 + ib : 4 + ib]
                else:
                    m = xcol(3 + jb) * r[3:4]
                mh, ml = split(m)
                kk[l, 128 * ib : 128 * ib + 128, 128 * jb : 128 * jb + 128] = mh
                at = COLS + 128 * ib
                kk[l, at : at + 128, 128 * jb : 128 * jb + 128] = ml

    exports = [
        pltpu.make_async_copy(x, y, out_sem.at[i])
        for i, (x, y) in enumerate(
            [
                (mt, mt_hbm), (pb, pb_hbm), (qb, qb_hbm), (kk.at[:, pl.ds(0, COLS), :], kk_hbm),
                (back, back_hbm), (de2, de_hbm), (inc_v, inc_hbm),
            ]
        )
    ]
    for x in exports[:4]:
        x.start()

    wait_all(sr, ss_r, CHIPS)
    acc = sr[0]
    for s in range(1, CHIPS):
        acc = acc + sr[s]
    bq[...] = acc
    for j in range(3):
        back[g, :, 128 * j : 128 * j + 128] = bq[pl.ds(j, ROWS, stride=3), :].astype(BF16)

    @pl.loop(1, LEVELS)
    def _(k):
        l = mem_peer(k)
        to_mem(back.at[g], back.at[g], bk_s, bk_r, l).start()

    loads[4].wait()
    carries_in(zo, z_sem)

    def partial(l):
        y = smooth(
            [(alpha_of(l, half),) for half in range(2)], (de[0, l], de[1, l]),
            mt[l], pb[l], qb[l], kk[l, 0:COLS], kk[l, COLS : 2 * COLS],
        )
        acc = jnp.zeros((ROWS, COLS), F32)
        for m in range(2 * HALF):
            acc = acc + (live[m] * pert_v[m, l].astype(F32)) * y[ROWS * m : ROWS * m + ROWS]
        return acc

    @pl.loop(1, LEVELS + 1)
    def _(k):
        l = mem_peer(k)
        ps[l] = partial(l)

        @pl.when(l != g)
        def _():
            to_mem(ps.at[l], pr.at[g], rs_s, rs_r, l).start()

    pr[g] = ps[g]

    wait_all(back, bk_r, LEVELS)
    exports[4].start()

    def weighted(l, half):
        x = pert_v[HALF * half : HALF * half + HALF, l].astype(F32) * back[l].astype(F32)[None]
        return split(x.reshape(PACK, COLS))

    sources(weighted, za2, zr2, z2_sem, 0, 2)

    wait_all(pr, rs_r, LEVELS)
    acc = pr[0]
    for s in range(1, LEVELS):
        acc = acc + pr[s]
    acc = acc * scale
    for j in range(3):
        lq[pl.ds(j, ROWS, stride=3), :] = acc[:, 128 * j : 128 * j + 128]
    lows[...] = lq[...].astype(BF16)

    def low_rows(s):
        return low.at[s, pl.ds(0, QROWS), :]

    def low_to(s):
        return to_tile(lows, low_rows(t), lo_s, lo_r.at[t], s)

    def low_on(s):
        return to_tile(low_rows(s), low_rows(s), lo_f, lo_r.at[s], partner)

    @pl.loop(1, CHIPS)
    def _(k):
        low_to(tile_of(chip_peer(k))).start()

    low_to(partner).start()

    low[t, 0:QROWS, :] = lows[...]

    sources(weighted, za2, zr2, z2_sem, 2, 4)

    inc_v[...] = jnp.zeros((DROWS, 128), F32)

    @pl.loop(0, steps)
    def _(j):
        tiles = []
        for i in range(GROUP):
            n = GROUP * j + i
            afar = (n + TILES - 2) // TILES
            late = n // (CHIPS + 1)
            ch = chip_back(afar * (n - 1 - (CHIPS - 1) * late))
            s = 2 * ch + core + (late + (1 - afar) * lax.rem(n, 2)) * (1 - 2 * core)
            tiles.append(s)

            @pl.when(n > 0)
            def _():
                low_on(s).wait_recv()

            @pl.when((afar == 1) & (late == 0))
            def _():
                low_on(s).start()

        inc_v[...] += forward_terms(tiles)

        @pl.when(j == steps // 2 - 1)
        def _():
            recursion(zr2, zo2, de2, z2_sem)

    exports[6].start()
    carries_in(zo2, z2_sem)
    exports[5].start()

    carries_sent(zo, z_sem)
    carries_sent(zo2, z2_sem)
    pltpu.make_async_copy(sp, sp, sp_s).wait()
    wait_all(ss, ss_s, CHIPS)
    lows8 = low.at[pl.ds(0, CHIPS), pl.ds(0, QROWS), :]
    pltpu.make_async_copy(lows8, lows8, lo_s).wait()
    lows7 = low.at[pl.ds(0, CHIPS - 1), pl.ds(0, QROWS), :]
    pltpu.make_async_copy(lows7, lows7, lo_f).wait()
    wait_all(ps, rs_s, LEVELS)
    wait_all(back, bk_s, LEVELS)
    for x in exports:
        x.wait()


def shards(
    alpha, perturbation, cotangent, decay_y, decay_x, group_members, interp_weight,
    pair_count, src_index, dst_index,
):
    any_spec = pl.BlockSpec(memory_space=pl.ANY)
    vmem = pl.BlockSpec(memory_space=pltpu.VMEM)
    smem = pl.BlockSpec(memory_space=pltpu.SMEM)
    dma = pltpu.SemaphoreType.DMA
    V = pltpu.VMEM
    zbuf = V((TILES, 32, 128), F32)
    zpair = V((2, CHIPS, 32, 128), F32)
    zall = [zpair, zbuf, zbuf, zpair]
    scratch = [
        V((2 * HALF, LEVELS, ROWS, COLS), BF16),
        V((2 * HALF, LEVELS, ROWS, COLS), BF16),
        V((1, DROWS * 128), BF16),
        V((DROWS, 128), BF16),
        V((TILES, SLOTS, BLK, 128), BF16),
        V((TILES, SLOTS), jnp.int32),
        V((TILES, SLOTS), jnp.int32),
        V((8, 512), F32),
        V((LEVELS, 8, 512), F32),
        V((LEVELS, 2, COLS), F32),
        V((LEVELS, 8, COLS), F32),
        V((LEVELS, PACK, 512), BF16),
        V((LEVELS, 32, PACK), BF16),
        V((LEVELS, ROWS, 128), F32),
        V((LEVELS, ROWS, 128), F32),
        V((LEVELS, 2 * COLS, COLS), BF16),
        *zall,
        *zall,
        V((2, CHIPS, QROWS, 128), F32),
        V((CHIPS, QROWS, 128), F32),
        V((CHIPS, QROWS, 128), F32),
        V((CHIPS, QROWS, 128), F32),
        V((QROWS, 128), F32),
        V((LEVELS, ROWS, COLS), BF16),
        V((LEVELS, ROWS, COLS), F32),
        V((LEVELS, ROWS, COLS), F32),
        V((QROWS, 128), F32),
        V((TILES, 128, 128), BF16),
        V((QROWS, 128), BF16),
        V((DROWS, 128), F32),
        V((TILES, SLOTS, 128), jnp.int32),
        V((TILES, SLOTS, 128), jnp.int32),
        dma((5,)),
        dma((TILES,)),
        dma((7,)),
        dma((4,)),
        dma((4,)),
        dma,
        dma((CHIPS,)),
        *[dma] * 6,
        dma((TILES,)),
        dma,
        dma,
    ]
    shape = jax.ShapeDtypeStruct
    inc, *rest = pl.pallas_call(
        kernel,
        out_shape=(
            shape((DROWS, 128), F32),
            shape((LEVELS, ROWS, COLS), BF16),
            shape((2, CHIPS, 32, 128), F32),
            shape((LEVELS, PACK, 512), BF16),
            shape((LEVELS, ROWS, 128), F32),
            shape((LEVELS, ROWS, 128), F32),
            shape((LEVELS, COLS, COLS), BF16),
        ),
        in_specs=[any_spec, any_spec, any_spec, vmem, vmem, smem, any_spec, smem, any_spec, any_spec],
        out_specs=(any_spec,) * 7,
        scratch_shapes=scratch,
        compiler_params=pltpu.CompilerParams(
            collective_id=0, has_side_effects=True, vmem_limit_bytes=60 * 1024 * 1024
        ),
        cost_estimate=pl.CostEstimate(
            flops=9_000_000_000, bytes_accessed=29_000_000, transcendentals=700_000
        ),
    )(
        alpha, perturbation, cotangent, decay_y, decay_x, group_members,
        interp_weight, pair_count, src_index, dst_index,
    )

    members_shape = (2 * HALF, LEVELS, ROWS, COLS)
    return pl.pallas_call(
        grad_kernel,
        out_shape=(shape((1, DROWS * 128), F32), shape(alpha.shape, F32)),
        in_specs=[smem, *[any_spec] * 7, vmem],
        out_specs=(vmem, any_spec),
        scratch_shapes=[
            V(members_shape, BF16),
            V((LEVELS, ROWS, COLS), BF16),
            V((2, CHIPS, 32, 128), F32),
            V((LEVELS, PACK, 512), BF16),
            V((LEVELS, ROWS, 128), F32),
            V((LEVELS, ROWS, 128), F32),
            V((LEVELS, COLS, COLS), BF16),
            V(members_shape, F32),
            dma((4,)),
            dma((3, LEVELS)),
            dma((LEVELS,)),
        ],
        compiler_params=pltpu.CompilerParams(vmem_limit_bytes=60 * 1024 * 1024),
        cost_estimate=pl.CostEstimate(
            flops=3_500_000_000, bytes_accessed=11_000_000, transcendentals=0
        ),
    )(group_members, perturbation, *rest, inc)


def solution(mesh):
    in_specs = (
        P("mem", None, "tile", None),
        P("mem", None, "tile", None),
        P("mem", "tile"),
        P(None, "tile"),
        P(),
        P(),
        P("tile", None, None, None, None),
        P(),
        P(),
        P(),
    )
    out_specs = (P("mem", "tile"), P("mem", None, "tile", None))
    return jax.shard_map(shards, mesh=mesh, in_specs=in_specs, out_specs=out_specs, check_vma=False)
```

```python
import jax
import jax.numpy as jnp
from jax import lax
from jax.experimental import pallas as pl
from jax.experimental.pallas import tpu as pltpu
from jax.sharding import PartitionSpec as P

MESH = pl.DeviceIdType.MESH
F32 = jnp.float32
BF16 = jnp.bfloat16

LEVELS = 8
TILES = 16
CHIPS = 8
ROWS = 32
COLS = 384
HALF = 5
PACK = HALF * ROWS
SLOTS = 128
BLK = 32
QROWS = ROWS * COLS // 128
DROWS = 384
GROUP = 2


def dot(a, b):
    return lax.dot_general(a, b, (((1,), (0,)), ((), ())), preferred_element_type=F32)


def dot_nt(a, b):
    return lax.dot_general(a, b, (((1,), (1,)), ((), ())), preferred_element_type=F32)


def split(x):
    high = x.astype(BF16)
    return high, (x - high.astype(F32)).astype(BF16)


def coefficient(a):
    t = 1.0 - a * a
    ratio = (t * t * t) / (1.0 + a * a)
    return jnp.where(ratio > 0.0, jnp.sqrt(jnp.sqrt(jnp.maximum(ratio, 1e-37))), 0.0)


def scans(a, pos, width, segment):
    logs = jnp.log(a)
    steps = [1 << b for b in range(16) if (1 << b) < segment]
    for k in steps:
        logs = logs + jnp.where(pos >= k, pltpu.roll(logs, k, 1), 0.0)
    rate = jnp.where(pos < segment - 1, pltpu.roll(a * a, width - 1, 1), 0.0)
    h = jnp.ones_like(a)
    for k in steps:
        h = h + rate * pltpu.roll(h, width - k, 1)
        rate = rate * pltpu.roll(rate, width - k, 1)
    return logs, h


def carry_row(carry, first):
    rows = [carry[first + HALF * j : first + HALF * j + 1, :] for j in range(3)]
    return jnp.concatenate(rows, axis=1)


def smooth(fields, carries, mt, pb, qb, upper, lower=None):
    p3 = jnp.concatenate([pb] * 3, axis=1)
    q3 = jnp.concatenate([qb] * 3, axis=1)
    rows = []
    for field, carry in zip(fields, carries):
        hi, *lo = field
        stack = jnp.concatenate([hi, hi, *lo], axis=0)
        y = dot(mt[:, 0 : stack.shape[0]], stack)
        for m in range(HALF):
            rows.append(
                y[ROWS * m : ROWS * m + ROWS]
                + p3 * carry_row(carry, m)
                + q3 * carry_row(carry, 16 + m)
            )
    yh, yl = split(jnp.concatenate(rows, axis=0))
    if lower is None:
        return dot(jnp.concatenate([yh, yl], axis=1), jnp.concatenate([upper] * 2, axis=0))
    return dot(
        jnp.concatenate([yh, yl, yh], axis=1), jnp.concatenate([upper, upper, lower], axis=0)
    )


def members(gm_ref):
    own = gm_ref[lax.axis_index("mem")]
    total = gm_ref[0]
    for i in range(1, LEVELS):
        total = total + gm_ref[i]
    scale = 1.0 / jnp.sqrt(jnp.full((1, COLS), total.astype(F32) - 1.0, F32))
    return scale, [jnp.where(m < own, 1.0, 0.0).astype(F32) for m in range(2 * HALF)]


def grad_kernel(
    gm_ref, pert_hbm, back_hbm, de_hbm, mt_hbm, pb_hbm, qb_hbm, kk_hbm, inc_ref,
    inc_out, grad_hbm,
    pert_v, back_v, de_v, mt_v, pb_v, qb_v, kk_v, out_v, whole_sem, in_sem, out_sem,
):
    whole = [
        pltpu.make_async_copy(a, b, whole_sem.at[i])
        for i, (a, b) in enumerate(
            [(back_hbm, back_v), (de_hbm, de_v), (pb_hbm, pb_v), (qb_hbm, qb_v)]
        )
    ]

    def loads(l):
        return [
            pltpu.make_async_copy(pert_hbm.at[:, l], pert_v.at[:, l], in_sem.at[0, l]),
            pltpu.make_async_copy(kk_hbm.at[l], kk_v.at[l], in_sem.at[1, l]),
            pltpu.make_async_copy(mt_hbm.at[l], mt_v.at[l], in_sem.at[2, l]),
        ]

    def store(l):
        return pltpu.make_async_copy(out_v.at[:, l], grad_hbm.at[:, l], out_sem.at[l])

    for x in whole:
        x.start()

    @pl.loop(0, LEVELS)
    def _(l):
        for x in loads(l):
            x.start()

    scale, live = members(gm_ref)

    @pl.loop(0, DROWS // 8)
    def _(i):
        x = inc_ref[pl.ds(pl.multiple_of(8 * i, 8), 8), :]
        for r in range(8):
            inc_out[0:1, pl.ds(pl.multiple_of(1024 * i + 128 * r, 128), 128)] = x[r : r + 1, :]

    for x in whole:
        x.wait()

    @pl.loop(0, LEVELS)
    def _(l):
        for x in loads(l):
            x.wait()
        fields = []
        for half in range(2):
            x = pert_v[HALF * half : HALF * half + HALF, l].astype(F32) * back_v[l].astype(F32)[None]
            fields.append(split(x.reshape(PACK, COLS)))
        y = smooth(fields, (de_v[0, l], de_v[1, l]), mt_v[l], pb_v[l], qb_v[l], kk_v[l])
        for m in range(2 * HALF):
            out_v[m, l] = y[ROWS * m : ROWS * m + ROWS] * (scale * live[m])
        store(l).start()

    @pl.loop(0, LEVELS)
    def _(l):
        store(l).wait()


def kernel(
    alpha_hbm, pert_hbm, cot_hbm, dy_ref, dx_ref, gm_ref, w_hbm, pc_ref, src_hbm, dst_hbm,
    inc_hbm, back_hbm, de_hbm, mt_hbm, pb_hbm, qb_hbm, kk_hbm,
    alpha_v, pert_v, cot_raw, cot_v, w_v, src_v, dst_v,
    rep_v, yt, ytail, xt, mt, zf, pb, qb, kk,
    za, zr, zo, de, za2, zr2, zo2, de2,
    sf, sp, ss, sr, bq, back, ps, pr, lq, low, lows, inc_v, scol_v, dcol_v,
    in_sem, w_sem, out_sem, z_sem, z2_sem,
    sp_s, sp_r, ss_s, ss_r, rs_s, rs_r, lo_s, lo_f, lo_r, bk_s, bk_r,
):
    g = lax.axis_index("mem")
    t = lax.axis_index("tile")

    chip = t // 2
    core = lax.rem(t, 2)
    partner = t + 1 - 2 * core

    def chip_peer(k):
        return lax.rem(chip + k, CHIPS)

    def chip_back(k):
        return lax.rem(chip + CHIPS - k, CHIPS)

    def tile_of(ch):
        return 2 * ch + core

    def mem_peer(k):
        return lax.rem(g + k, LEVELS)

    def to_tile(src, dst, ssem, rsem, s):
        return pltpu.make_async_remote_copy(
            src_ref=src, dst_ref=dst, send_sem=ssem, recv_sem=rsem,
            device_id={"tile": s}, device_id_type=MESH,
        )

    def to_mem(src, dst, ssem, rsem, s):
        return pltpu.make_async_remote_copy(
            src_ref=src, dst_ref=dst, send_sem=ssem, recv_sem=rsem,
            device_id={"mem": s}, device_id_type=MESH,
        )

    loads = [
        pltpu.make_async_copy(alpha_hbm, alpha_v, in_sem.at[0]),
        pltpu.make_async_copy(cot_hbm, cot_raw, in_sem.at[1]),
        pltpu.make_async_copy(src_hbm.at[t], src_v, in_sem.at[2]),
        pltpu.make_async_copy(dst_hbm.at[t], dst_v, in_sem.at[3]),
        pltpu.make_async_copy(pert_hbm, pert_v, in_sem.at[4]),
    ]

    def wait_all(buf, sem, count):
        part = buf.at[pl.ds(0, count - 1)]
        pltpu.make_async_copy(part, part, sem).wait()

    def w_load(s):
        return pltpu.make_async_copy(w_hbm.at[0, s], w_v.at[s], w_sem.at[s])

    for c in loads:
        c.start()

    @pl.loop(0, TILES)
    def _(i):
        late = i // CHIPS
        w_load(2 * chip_peer(i - CHIPS * late + 1) + 1 - core + late * (2 * core - 1)).start()

    barrier = pltpu.get_barrier_semaphore()

    @pl.loop(1, TILES)
    def _(k):
        pl.semaphore_signal(
            barrier, inc=1, device_id={"tile": lax.rem(t + k, TILES)}, device_id_type=MESH
        )

    @pl.loop(1, LEVELS)
    def _(k):
        pl.semaphore_signal(barrier, inc=1, device_id={"mem": mem_peer(k)}, device_id_type=MESH)

    scale, live = members(gm_ref)

    for k in range(16):
        rep_v[:, 32 * k : 32 * k + 32] = dy_ref[...]
    a = rep_v[...]
    pos = lax.broadcasted_iota(jnp.int32, (8, 512), 1) & 31
    logs, h = scans(a, pos, 512, ROWS)
    c = coefficient(a)
    ltot = jnp.broadcast_to(logs[:, 31:32], (8, 512))
    lane512 = lax.broadcasted_iota(jnp.int32, (8, 512), 1)
    hsum = jnp.sum(jnp.where(lane512 < 32, jnp.exp(2.0 * logs), 0.0), axis=1, keepdims=True)
    for f, x in enumerate(
        (logs, c, c * h, c * h * jnp.exp(logs), c * jnp.exp(ltot - logs))
    ):
        yt[:, f, :] = x
    yt[:, 5:8, :] = jnp.zeros((LEVELS, 3, 512), F32)
    ytail[:, 0, :] = jnp.broadcast_to(jnp.exp(ltot[:, 0:1]), (LEVELS, COLS))
    ytail[:, 1, :] = jnp.broadcast_to(hsum, (LEVELS, COLS))
    lane_y = lax.broadcasted_iota(jnp.int32, (ROWS, 512), 1)
    lower = lax.broadcasted_iota(jnp.int32, (ROWS, 512), 0) >= (lane_y & 31)
    zr_i = lax.broadcasted_iota(jnp.int32, (16, 256), 0)
    zc_i = lax.broadcasted_iota(jnp.int32, (16, 256), 1) >> 5

    def columns(rows):
        width = rows.shape[1]
        return jnp.transpose(jnp.concatenate([rows, jnp.zeros((120, width), F32)], axis=0))

    @pl.loop(0, LEVELS)
    def _(l):
        rows = yt[l]
        cols = columns(rows[:, 0:128])[0:ROWS]

        def col(f):
            return cols[:, f : f + 1]

        e = jnp.exp(-jnp.abs(col(0) - rows[0:1]))
        m = e * jnp.where(lower, col(2) * rows[1:2], col(1) * rows[2:3])
        part = lane_y >> 5
        mh, ml = split(m)
        m = jnp.where((part >= HALF) & (part < 2 * HALF), ml.astype(F32), mh.astype(F32))
        part = jnp.where(part < 3 * HALF, part % HALF, -1)
        for i in range(HALF):
            mt[l, ROWS * i : ROWS * i + ROWS, :] = jnp.where(part == i, m, 0.0).astype(BF16)
        z = jnp.where(zr_i == zc_i, rows[4:5, 0:256], 0.0) + jnp.where(zr_i == zc_i + 8, rows[3:4, 0:256], 0.0)
        z = jnp.where(zc_i < HALF, z, 0.0)
        zh, zl = split(z)
        zf[l, 0:16, :] = zh[:, 0:PACK]
        zf[l, 16:32, :] = zl[:, 0:PACK]
        pb[l] = jnp.broadcast_to(col(3), (ROWS, 128))
        qb[l] = jnp.broadcast_to(col(4), (ROWS, 128))

    low[:, QROWS:128, :] = jnp.zeros((TILES, 128 - QROWS, 128), BF16)

    loads[1].wait()

    @pl.loop(0, DROWS // 16)
    def _(i):
        rows = [
            cot_raw[:, pl.ds(pl.multiple_of(2048 * i + 128 * r, 128), 128)].astype(F32)
            for r in range(16)
        ]
        cot_v[pl.ds(pl.multiple_of(16 * i, 16), 16), :] = jnp.concatenate(rows, axis=0).astype(BF16)

    loads[0].wait()
    pl.semaphore_wait(barrier, TILES - 1 + LEVELS - 1)

    def alpha_of(l, half):
        return alpha_v[HALF * half : HALF * half + HALF, l].reshape(PACK, COLS)

    def source(l, hi, lo=None):
        r = dot(zf[l], hi)
        z = r[0:16] + r[16:32]
        if lo is not None:
            z = z + dot(zf[l, 0:16, :], lo)
        return z

    def sources(field, za, zr, sem, first, last):
        @pl.loop(first, last)
        def _(k):
            found = []
            for i in range(2):
                l = lax.rem(chip + 2 * k + i + 1, LEVELS)
                for half in range(2):
                    found.append((half, l, source(l, *field(l, half))))
            for half, l, z in found:
                for j in range(3):
                    part = z[:, 128 * j : 128 * j + 128]
                    za[half, l, HALF * j : HALF * j + HALF, :] = part[0:HALF]
                    za[half, l, 16 + HALF * j : 16 + HALF * j + HALF, :] = part[8 : 8 + HALF]
                za[half, l, 15:16, :] = ytail[l, 0:1, 0:128]
                za[half, l, 31:32, :] = ytail[l, 1:2, 0:128]

        if last == LEVELS // 2:

            @pl.loop(1, TILES)
            def _(k):
                s = lax.rem(t + k, TILES)
                to_tile(za.at[lax.rem(s, 2), s // 2], zr.at[t], sem.at[0], sem.at[1], s).start()

            zr[t] = za[core, chip]

    def recursion(zr, zo, de, sem):
        wait_all(zr, sem.at[1], TILES)
        d = jnp.zeros((16, 128), F32)
        downs = []
        for s in range(TILES):
            downs.append(d)
            zo[s, 0:16, :] = d
            d = zr[s, 15:16, :] * d + zr[s, 0:16, :]
        e = jnp.zeros((16, 128), F32)
        for s in reversed(range(TILES)):
            zo[s, 16:32, :] = e
            e = zr[s, 15:16, :] * e + (zr[s, 16:32, :] + zr[s, 31:32, :] * downs[s])

        @pl.loop(1, TILES)
        def _(k):
            s = lax.rem(t + k, TILES)
            to_tile(zo.at[s], de.at[core, chip], sem.at[2], sem.at[3], s).start()

        de[core, chip] = zo[t]

    def carries_in(zo, sem):
        wait_all(zo, sem.at[3], TILES)

    def carries_sent(zo, sem):
        wait_all(zo, sem.at[0], TILES)
        wait_all(zo, sem.at[2], TILES)

    sources(lambda l, half: (alpha_of(l, half),), za, zr, z_sem, 0, LEVELS // 2)

    lane1 = lax.broadcasted_iota(jnp.int32, (1, 128), 1)
    lane = lax.broadcasted_iota(jnp.int32, (SLOTS, 128), 1)
    lgroup = lane >> 5
    slot_id = lax.broadcasted_iota(jnp.int32, (SLOTS, 128), 0)
    r16 = lax.broadcasted_iota(jnp.int32, (16, 128), 0) - (
        lax.broadcasted_iota(jnp.int32, (16, 128), 1) >> 5
    )
    sub96 = lax.broadcasted_iota(jnp.int32, (QROWS, 128), 0)
    sub384 = lax.broadcasted_iota(jnp.int32, (DROWS, 128), 0)

    def one_hot(condition):
        return jnp.where(condition, 1.0, 0.0).astype(BF16)

    def source_row(s):
        return jnp.where(lane1 < pc_ref[t, s], src_v[pl.ds(s, 1), :], -1)

    def target_row(s):
        return dst_v[pl.ds(s, 1), :]

    def spread_out(x):
        x = x + pltpu.roll(x, 64, 1)
        return x + pltpu.roll(x, 32, 1)

    def weight_pair(s, i):
        return jnp.concatenate(
            [
                w_v[s, 16 * (i + half) : 16 * (i + half) + 16].reshape(16 * BLK, 128)
                for half in range(2)
            ],
            axis=1,
        )

    def back_terms(tiles):
        srows = [source_row(s) for s in tiles]
        scols = [scol_v[s] for s in tiles]
        dcols = [dcol_v[s] for s in tiles]
        pick = jnp.concatenate(
            [
                jnp.concatenate([one_hot(lane + 128 * k == dcol) for k in range(3)], axis=1)
                for dcol in dcols
            ],
            axis=0,
        )
        grad = dot(pick, cot_v[...]).astype(BF16)
        results = []
        for n, s in enumerate(tiles):
            parts = []
            for i in range(0, 8, 2):
                first = SLOTS * n + 16 * i
                zero = jnp.zeros((16, 128), BF16)
                pair = jnp.concatenate(
                    [
                        jnp.concatenate([grad[first : first + 16], zero], axis=1),
                        jnp.concatenate([zero, grad[first + 16 : first + 32]], axis=1),
                    ],
                    axis=0,
                )
                o = dot_nt(pair, weight_pair(s, i))
                for half in range(2):
                    parts.append(
                        sum(
                            jnp.where(
                                r16 == 4 * j,
                                o[16 * half : 16 * half + 16, 128 * j : 128 * j + 128],
                                0.0,
                            )
                            for j in range(4)
                        )
                    )
            terms = spread_out(jnp.concatenate(parts, axis=0))
            terms = jnp.where(lgroup == (scols[n] & 3), terms, 0.0)
            put = one_hot(sub96 == (srows[n] >> 2))
            both = dot(put, jnp.concatenate(split(terms), axis=1))
            results.append(both[:, 0:128] + both[:, 128:256])
        return results

    def forward_terms(tiles):
        puts, sums = [], []
        for s in tiles:
            scol = scol_v[s]
            picked = dot(one_hot(lane == (scol >> 2)), low[s])
            picked = spread_out(jnp.where(lgroup == (scol & 3), picked, 0.0))
            parts = []
            for i in range(0, 8, 2):
                xs = []
                for half in range(2):
                    x = picked[16 * (i + half) : 16 * (i + half) + 16]
                    xs.append(
                        jnp.concatenate([jnp.where(r16 == 4 * j, x, 0.0) for j in range(4)], axis=1)
                    )
                both = dot(jnp.concatenate(xs, axis=0).astype(BF16), weight_pair(s, i))
                parts.append(both[0:16, 0:128])
                parts.append(both[16:32, 128:256])
            sums.append(jnp.concatenate(split(jnp.concatenate(parts, axis=0)), axis=1))
            puts.append(one_hot(sub384 == target_row(s)))
        both = dot(jnp.concatenate(puts, axis=1), jnp.concatenate(sums, axis=0))
        return both[:, 0:128] + both[:, 128:256]

    loads[2].wait()
    loads[3].wait()
    turned = jnp.transpose(
        jnp.concatenate([src_v[...], dst_v[...], jnp.zeros((96, SLOTS), jnp.int32)], axis=0).astype(F32)
    ).astype(jnp.int32)
    for s in range(TILES):
        scol = jnp.broadcast_to(turned[:, s : s + 1], (SLOTS, 128))
        scol_v[s] = jnp.where(slot_id < pc_ref[t, s], scol, -1)
        dcol_v[s] = jnp.broadcast_to(turned[:, TILES + s : TILES + s + 1], (SLOTS, 128))

    def off_chip(ch):
        return to_tile(ss.at[ch], sr.at[chip], ss_s, ss_r, tile_of(ch))

    def core_pair(ch):
        return to_tile(sf.at[0, ch], sp.at[ch], sp_s, sp_r.at[ch], partner)

    steps = TILES // GROUP

    @pl.loop(0, steps)
    def _(j):
        late = j // (steps // 2)
        chips = [chip_peer(GROUP * (j - steps // 2 * late) + 1 + i) for i in range(GROUP)]
        tiles = [2 * ch + 1 - core + late * (2 * core - 1) for ch in chips]
        for s in tiles:
            w_load(s).wait()
        for ch, r in zip(chips, back_terms(tiles)):
            sf[late, ch] = r

        @pl.when(late == 0)
        def _():
            for ch in chips:
                core_pair(ch).start()

        @pl.when(late == 1)
        def _():
            for ch in chips:
                core_pair(ch).wait_recv()
                ss[ch] = sf[1, ch] + sp[ch]

                @pl.when(ch != chip)
                def _():
                    off_chip(ch).start()

        @pl.when(j == steps // 2 - 1)
        def _():
            recursion(zr, zo, de, z_sem)

    sr[chip] = ss[chip]

    ax = dx_ref[...]
    posx = lax.broadcasted_iota(jnp.int32, (8, COLS), 1)
    lx, hx = scans(ax, posx, COLS, COLS)
    cx = coefficient(ax)
    gx = cx * hx
    edge1 = jnp.broadcast_to(lx[:, 127:128], (8, COLS))
    edge2 = jnp.broadcast_to(lx[:, 255:256], (8, COLS))
    xt[:, 0, :] = lx
    xt[:, 1, :] = cx
    xt[:, 2, :] = gx
    xt[:, 3, :] = gx * jnp.exp(jnp.minimum(lx - jnp.where(posx < 256, edge1, edge2), 0.0))
    xt[:, 4, :] = cx * jnp.exp(jnp.minimum(edge1 - lx, 0.0))
    xt[:, 5, :] = cx * jnp.exp(jnp.minimum(edge2 - lx, 0.0))
    xt[:, 6:8, :] = jnp.zeros((LEVELS, 2, COLS), F32)
    lowx = lax.broadcasted_iota(jnp.int32, (128, 128), 0) >= (
        lax.broadcasted_iota(jnp.int32, (128, 128), 1)
    )

    @pl.loop(0, LEVELS)
    def _(l):
        rows = xt[l]
        cols = columns(rows)
        for ib in range(3):
            for jb in range(3):
                r = rows[:, 128 * jb : 128 * jb + 128]

                def xcol(f):
                    return cols[128 * ib : 128 * ib + 128, f : f + 1]

                if ib == jb:
                    e = jnp.exp(-jnp.abs(xcol(0) - r[0:1]))
                    m = e * jnp.where(lowx, xcol(2) * r[1:2], xcol(1) * r[2:3])
                elif ib > jb:
                    m = xcol(3) * r[3 + ib : 4 + ib]
                else:
                    m = xcol(3 + jb) * r[3:4]
                mh, ml = split(m)
                kk[l, 128 * ib : 128 * ib + 128, 128 * jb : 128 * jb + 128] = mh
                at = COLS + 128 * ib
                kk[l, at : at + 128, 128 * jb : 128 * jb + 128] = ml

    exports = [
        pltpu.make_async_copy(x, y, out_sem.at[i])
        for i, (x, y) in enumerate(
            [
                (mt, mt_hbm), (pb, pb_hbm), (qb, qb_hbm), (kk.at[:, pl.ds(0, COLS), :], kk_hbm),
                (back, back_hbm), (de2, de_hbm), (inc_v, inc_hbm),
            ]
        )
    ]
    for x in exports[:4]:
        x.start()

    wait_all(sr, ss_r, CHIPS)
    acc = sr[0]
    for s in range(1, CHIPS):
        acc = acc + sr[s]
    bq[...] = acc
    for j in range(3):
        back[g, :, 128 * j : 128 * j + 128] = bq[pl.ds(j, ROWS, stride=3), :].astype(BF16)

    @pl.loop(1, LEVELS)
    def _(k):
        l = mem_peer(k)
        to_mem(back.at[g], back.at[g], bk_s, bk_r, l).start()

    loads[4].wait()
    carries_in(zo, z_sem)

    def partial(l):
        y = smooth(
            [(alpha_of(l, half),) for half in range(2)], (de[0, l], de[1, l]),
            mt[l], pb[l], qb[l], kk[l, 0:COLS], kk[l, COLS : 2 * COLS],
        )
        acc = jnp.zeros((ROWS, COLS), F32)
        for m in range(2 * HALF):
            acc = acc + (live[m] * pert_v[m, l].astype(F32)) * y[ROWS * m : ROWS * m + ROWS]
        return acc

    @pl.loop(1, LEVELS + 1)
    def _(k):
        l = mem_peer(k)
        ps[l] = partial(l)

        @pl.when(l != g)
        def _():
            to_mem(ps.at[l], pr.at[g], rs_s, rs_r, l).start()

    pr[g] = ps[g]

    wait_all(back, bk_r, LEVELS)
    exports[4].start()

    def weighted(l, half):
        x = pert_v[HALF * half : HALF * half + HALF, l].astype(F32) * back[l].astype(F32)[None]
        return split(x.reshape(PACK, COLS))

    sources(weighted, za2, zr2, z2_sem, 0, 2)

    wait_all(pr, rs_r, LEVELS)
    acc = pr[0]
    for s in range(1, LEVELS):
        acc = acc + pr[s]
    acc = acc * scale
    for j in range(3):
        lq[pl.ds(j, ROWS, stride=3), :] = acc[:, 128 * j : 128 * j + 128]
    lows[...] = lq[...].astype(BF16)

    def low_rows(s):
        return low.at[s, pl.ds(0, QROWS), :]

    def low_to(s):
        return to_tile(lows, low_rows(t), lo_s, lo_r.at[t], s)

    def low_on(s):
        return to_tile(low_rows(s), low_rows(s), lo_f, lo_r.at[s], partner)

    @pl.loop(1, CHIPS)
    def _(k):
        low_to(tile_of(chip_peer(k))).start()

    low_to(partner).start()

    low[t, 0:QROWS, :] = lows[...]

    sources(weighted, za2, zr2, z2_sem, 2, 4)

    inc_v[...] = jnp.zeros((DROWS, 128), F32)

    @pl.loop(0, steps)
    def _(j):
        tiles = []
        for i in range(GROUP):
            n = GROUP * j + i
            afar = (n + TILES - 2) // TILES
            late = n // (CHIPS + 1)
            ch = chip_back(afar * (n - 1 - (CHIPS - 1) * late))
            s = 2 * ch + core + (late + (1 - afar) * lax.rem(n, 2)) * (1 - 2 * core)
            tiles.append(s)

            @pl.when(n > 0)
            def _():
                low_on(s).wait_recv()

            @pl.when((afar == 1) & (late == 0))
            def _():
                low_on(s).start()

        inc_v[...] += forward_terms(tiles)

        @pl.when(j == steps // 2 - 1)
        def _():
            recursion(zr2, zo2, de2, z2_sem)

    exports[6].start()
    carries_in(zo2, z2_sem)
    exports[5].start()

    carries_sent(zo, z_sem)
    carries_sent(zo2, z2_sem)
    pltpu.make_async_copy(sp, sp, sp_s).wait()
    wait_all(ss, ss_s, CHIPS)
    lows8 = low.at[pl.ds(0, CHIPS), pl.ds(0, QROWS), :]
    pltpu.make_async_copy(lows8, lows8, lo_s).wait()
    lows7 = low.at[pl.ds(0, CHIPS - 1), pl.ds(0, QROWS), :]
    pltpu.make_async_copy(lows7, lows7, lo_f).wait()
    wait_all(ps, rs_s, LEVELS)
    wait_all(back, bk_s, LEVELS)
    for x in exports:
        x.wait()


def shards(
    alpha, perturbation, cotangent, decay_y, decay_x, group_members, interp_weight,
    pair_count, src_index, dst_index,
):
    any_spec = pl.BlockSpec(memory_space=pl.ANY)
    vmem = pl.BlockSpec(memory_space=pltpu.VMEM)
    smem = pl.BlockSpec(memory_space=pltpu.SMEM)
    dma = pltpu.SemaphoreType.DMA
    V = pltpu.VMEM
    zbuf = V((TILES, 32, 128), F32)
    zpair = V((2, CHIPS, 32, 128), F32)
    zall = [zpair, zbuf, zbuf, zpair]
    scratch = [
        V((2 * HALF, LEVELS, ROWS, COLS), BF16),
        V((2 * HALF, LEVELS, ROWS, COLS), BF16),
        V((1, DROWS * 128), BF16),
        V((DROWS, 128), BF16),
        V((TILES, SLOTS, BLK, 128), BF16),
        V((TILES, SLOTS), jnp.int32),
        V((TILES, SLOTS), jnp.int32),
        V((8, 512), F32),
        V((LEVELS, 8, 512), F32),
        V((LEVELS, 2, COLS), F32),
        V((LEVELS, 8, COLS), F32),
        V((LEVELS, PACK, 512), BF16),
        V((LEVELS, 32, PACK), BF16),
        V((LEVELS, ROWS, 128), F32),
        V((LEVELS, ROWS, 128), F32),
        V((LEVELS, 2 * COLS, COLS), BF16),
        *zall,
        *zall,
        V((2, CHIPS, QROWS, 128), F32),
        V((CHIPS, QROWS, 128), F32),
        V((CHIPS, QROWS, 128), F32),
        V((CHIPS, QROWS, 128), F32),
        V((QROWS, 128), F32),
        V((LEVELS, ROWS, COLS), BF16),
        V((LEVELS, ROWS, COLS), F32),
        V((LEVELS, ROWS, COLS), F32),
        V((QROWS, 128), F32),
        V((TILES, 128, 128), BF16),
        V((QROWS, 128), BF16),
        V((DROWS, 128), F32),
        V((TILES, SLOTS, 128), jnp.int32),
        V((TILES, SLOTS, 128), jnp.int32),
        dma((5,)),
        dma((TILES,)),
        dma((7,)),
        dma((4,)),
        dma((4,)),
        dma,
        dma((CHIPS,)),
        *[dma] * 6,
        dma((TILES,)),
        dma,
        dma,
    ]
    shape = jax.ShapeDtypeStruct
    inc, *rest = pl.pallas_call(
        kernel,
        out_shape=(
            shape((DROWS, 128), F32),
            shape((LEVELS, ROWS, COLS), BF16),
            shape((2, CHIPS, 32, 128), F32),
            shape((LEVELS, PACK, 512), BF16),
            shape((LEVELS, ROWS, 128), F32),
            shape((LEVELS, ROWS, 128), F32),
            shape((LEVELS, COLS, COLS), BF16),
        ),
        in_specs=[any_spec, any_spec, any_spec, vmem, vmem, smem, any_spec, smem, any_spec, any_spec],
        out_specs=(any_spec,) * 7,
        scratch_shapes=scratch,
        compiler_params=pltpu.CompilerParams(
            collective_id=0, has_side_effects=True, vmem_limit_bytes=60 * 1024 * 1024
        ),
        cost_estimate=pl.CostEstimate(
            flops=9_000_000_000, bytes_accessed=29_000_000, transcendentals=700_000
        ),
    )(
        alpha, perturbation, cotangent, decay_y, decay_x, group_members,
        interp_weight, pair_count, src_index, dst_index,
    )

    members_shape = (2 * HALF, LEVELS, ROWS, COLS)
    return pl.pallas_call(
        grad_kernel,
        out_shape=(shape((1, DROWS * 128), F32), shape(alpha.shape, F32)),
        in_specs=[smem, *[any_spec] * 7, vmem],
        out_specs=(vmem, any_spec),
        scratch_shapes=[
            V(members_shape, BF16),
            V((LEVELS, ROWS, COLS), BF16),
            V((2, CHIPS, 32, 128), F32),
            V((LEVELS, PACK, 512), BF16),
            V((LEVELS, ROWS, 128), F32),
            V((LEVELS, ROWS, 128), F32),
            V((LEVELS, COLS, COLS), BF16),
            V(members_shape, F32),
            dma((4,)),
            dma((3, LEVELS)),
            dma((LEVELS,)),
        ],
        compiler_params=pltpu.CompilerParams(vmem_limit_bytes=60 * 1024 * 1024),
        cost_estimate=pl.CostEstimate(
            flops=3_500_000_000, bytes_accessed=11_000_000, transcendentals=0
        ),
    )(group_members, perturbation, *rest, inc)


def solution(mesh):
    in_specs = (
        P("mem", None, "tile", None),
        P("mem", None, "tile", None),
        P("mem", "tile"),
        P(None, "tile"),
        P(),
        P(),
        P("tile", None, None, None, None),
        P(),
        P(),
        P(),
    )
    out_specs = (P("mem", "tile"), P("mem", None, "tile", None))
    return jax.shard_map(shards, mesh=mesh, in_specs=in_specs, out_specs=out_specs, check_vma=False)
```

```python
import jax
import jax.numpy as jnp
from jax import lax
from jax.experimental import pallas as pl
from jax.experimental.pallas import tpu as pltpu
from jax.sharding import PartitionSpec as P

MESH = pl.DeviceIdType.MESH
F32 = jnp.float32
BF16 = jnp.bfloat16

LEVELS = 8
TILES = 16
CHIPS = 8
ROWS = 32
COLS = 384
HALF = 5
PACK = HALF * ROWS
SLOTS = 128
BLK = 32
QROWS = ROWS * COLS // 128
DROWS = 384
GROUP = 2


def dot(a, b):
    return lax.dot_general(a, b, (((1,), (0,)), ((), ())), preferred_element_type=F32)


def dot_nt(a, b):
    return lax.dot_general(a, b, (((1,), (1,)), ((), ())), preferred_element_type=F32)


def split(x):
    high = x.astype(BF16)
    return high, (x - high.astype(F32)).astype(BF16)


def coefficient(a):
    t = 1.0 - a * a
    ratio = (t * t * t) / (1.0 + a * a)
    return jnp.where(ratio > 0.0, jnp.sqrt(jnp.sqrt(jnp.maximum(ratio, 1e-37))), 0.0)


def scans(a, pos, width, segment):
    logs = jnp.log(a)
    steps = [1 << b for b in range(16) if (1 << b) < segment]
    for k in steps:
        logs = logs + jnp.where(pos >= k, pltpu.roll(logs, k, 1), 0.0)
    rate = jnp.where(pos < segment - 1, pltpu.roll(a * a, width - 1, 1), 0.0)
    h = jnp.ones_like(a)
    for k in steps:
        h = h + rate * pltpu.roll(h, width - k, 1)
        rate = rate * pltpu.roll(rate, width - k, 1)
    return logs, h


def carry_row(carry, first):
    rows = [carry[first + HALF * j : first + HALF * j + 1, :] for j in range(3)]
    return jnp.concatenate(rows, axis=1)


def smooth(fields, carries, mt, pb, qb, upper, lower=None):
    p3 = jnp.concatenate([pb] * 3, axis=1)
    q3 = jnp.concatenate([qb] * 3, axis=1)
    rows = []
    for field, carry in zip(fields, carries):
        hi, *lo = field
        stack = jnp.concatenate([hi, hi, *lo], axis=0)
        y = dot(mt[:, 0 : stack.shape[0]], stack)
        for m in range(HALF):
            rows.append(
                y[ROWS * m : ROWS * m + ROWS]
                + p3 * carry_row(carry, m)
                + q3 * carry_row(carry, 16 + m)
            )
    yh, yl = split(jnp.concatenate(rows, axis=0))
    if lower is None:
        return dot(jnp.concatenate([yh, yl], axis=1), jnp.concatenate([upper] * 2, axis=0))
    return dot(
        jnp.concatenate([yh, yl, yh], axis=1), jnp.concatenate([upper, upper, lower], axis=0)
    )


def members(gm_ref):
    own = gm_ref[lax.axis_index("mem")]
    total = gm_ref[0]
    for i in range(1, LEVELS):
        total = total + gm_ref[i]
    scale = 1.0 / jnp.sqrt(jnp.full((1, COLS), total.astype(F32) - 1.0, F32))
    return scale, [jnp.where(m < own, 1.0, 0.0).astype(F32) for m in range(2 * HALF)]


def grad_kernel(
    gm_ref, pert_hbm, back_hbm, de_hbm, mt_hbm, pb_hbm, qb_hbm, kk_hbm, inc_ref,
    inc_out, grad_hbm,
    pert_v, back_v, de_v, mt_v, pb_v, qb_v, kk_v, out_v, whole_sem, in_sem, out_sem,
):
    whole = [
        pltpu.make_async_copy(a, b, whole_sem.at[i])
        for i, (a, b) in enumerate(
            [(back_hbm, back_v), (de_hbm, de_v), (pb_hbm, pb_v), (qb_hbm, qb_v)]
        )
    ]

    def loads(l):
        return [
            pltpu.make_async_copy(pert_hbm.at[:, l], pert_v.at[:, l], in_sem.at[0, l]),
            pltpu.make_async_copy(kk_hbm.at[l], kk_v.at[l], in_sem.at[1, l]),
            pltpu.make_async_copy(mt_hbm.at[l], mt_v.at[l], in_sem.at[2, l]),
        ]

    def store(l):
        return pltpu.make_async_copy(out_v.at[:, l], grad_hbm.at[:, l], out_sem.at[l])

    for x in whole:
        x.start()

    @pl.loop(0, LEVELS)
    def _(l):
        for x in loads(l):
            x.start()

    scale, live = members(gm_ref)

    @pl.loop(0, DROWS // 8)
    def _(i):
        x = inc_ref[pl.ds(pl.multiple_of(8 * i, 8), 8), :]
        for r in range(8):
            inc_out[0:1, pl.ds(pl.multiple_of(1024 * i + 128 * r, 128), 128)] = x[r : r + 1, :]

    for x in whole:
        x.wait()

    @pl.loop(0, LEVELS)
    def _(l):
        for x in loads(l):
            x.wait()
        fields = []
        for half in range(2):
            x = pert_v[HALF * half : HALF * half + HALF, l].astype(F32) * back_v[l].astype(F32)[None]
            fields.append(split(x.reshape(PACK, COLS)))
        y = smooth(fields, (de_v[0, l], de_v[1, l]), mt_v[l], pb_v[l], qb_v[l], kk_v[l])
        for m in range(2 * HALF):
            out_v[m, l] = y[ROWS * m : ROWS * m + ROWS] * (scale * live[m])
        store(l).start()

    @pl.loop(0, LEVELS)
    def _(l):
        store(l).wait()


def kernel(
    alpha_hbm, pert_hbm, cot_hbm, dy_ref, dx_ref, gm_ref, w_hbm, pc_ref, src_hbm, dst_hbm,
    inc_hbm, back_hbm, de_hbm, mt_hbm, pb_hbm, qb_hbm, kk_hbm,
    alpha_v, pert_v, cot_raw, cot_v, w_v, src_v, dst_v,
    rep_v, yt, ytail, xt, mt, zf, pb, qb, kk,
    za, zr, zo, de, za2, zr2, zo2, de2,
    sf, sp, ss, sr, bq, back, ps, pr, lq, low, lows, inc_v, scol_v, dcol_v,
    in_sem, w_sem, out_sem, z_sem, z2_sem,
    sp_s, sp_r, ss_s, ss_r, rs_s, rs_r, lo_s, lo_f, lo_r, bk_s, bk_r,
):
    g = lax.axis_index("mem")
    t = lax.axis_index("tile")

    chip = t // 2
    core = lax.rem(t, 2)
    partner = t + 1 - 2 * core

    def chip_peer(k):
        return lax.rem(chip + k, CHIPS)

    def chip_back(k):
        return lax.rem(chip + CHIPS - k, CHIPS)

    def tile_of(ch):
        return 2 * ch + core

    def mem_peer(k):
        return lax.rem(g + k, LEVELS)

    def to_tile(src, dst, ssem, rsem, s):
        return pltpu.make_async_remote_copy(
            src_ref=src, dst_ref=dst, send_sem=ssem, recv_sem=rsem,
            device_id={"tile": s}, device_id_type=MESH,
        )

    def to_mem(src, dst, ssem, rsem, s):
        return pltpu.make_async_remote_copy(
            src_ref=src, dst_ref=dst, send_sem=ssem, recv_sem=rsem,
            device_id={"mem": s}, device_id_type=MESH,
        )

    loads = [
        pltpu.make_async_copy(alpha_hbm, alpha_v, in_sem.at[0]),
        pltpu.make_async_copy(cot_hbm, cot_raw, in_sem.at[1]),
        pltpu.make_async_copy(src_hbm.at[t], src_v, in_sem.at[2]),
        pltpu.make_async_copy(dst_hbm.at[t], dst_v, in_sem.at[3]),
        pltpu.make_async_copy(pert_hbm, pert_v, in_sem.at[4]),
    ]

    def wait_all(buf, sem, count):
        part = buf.at[pl.ds(0, count - 1)]
        pltpu.make_async_copy(part, part, sem).wait()

    def w_load(s):
        return pltpu.make_async_copy(w_hbm.at[0, s], w_v.at[s], w_sem.at[s])

    def w_tile(i):
        late = i // CHIPS
        return 2 * chip_peer(i - CHIPS * late + 1) + 1 - core + late * (2 * core - 1)

    for c in loads[:4]:
        c.start()

    @pl.loop(0, CHIPS // 2)
    def _(i):
        w_load(w_tile(i)).start()

    barrier = pltpu.get_barrier_semaphore()

    @pl.loop(1, TILES)
    def _(k):
        pl.semaphore_signal(
            barrier, inc=1, device_id={"tile": lax.rem(t + k, TILES)}, device_id_type=MESH
        )

    @pl.loop(1, LEVELS)
    def _(k):
        pl.semaphore_signal(barrier, inc=1, device_id={"mem": mem_peer(k)}, device_id_type=MESH)

    scale, live = members(gm_ref)

    for k in range(16):
        rep_v[:, 32 * k : 32 * k + 32] = dy_ref[...]
    a = rep_v[...]
    pos = lax.broadcasted_iota(jnp.int32, (8, 512), 1) & 31
    logs, h = scans(a, pos, 512, ROWS)
    c = coefficient(a)
    ltot = jnp.broadcast_to(logs[:, 31:32], (8, 512))
    lane512 = lax.broadcasted_iota(jnp.int32, (8, 512), 1)
    hsum = jnp.sum(jnp.where(lane512 < 32, jnp.exp(2.0 * logs), 0.0), axis=1, keepdims=True)
    for f, x in enumerate(
        (logs, c, c * h, c * h * jnp.exp(logs), c * jnp.exp(ltot - logs))
    ):
        yt[:, f, :] = x
    yt[:, 5:8, :] = jnp.zeros((LEVELS, 3, 512), F32)
    ytail[:, 0, :] = jnp.broadcast_to(jnp.exp(ltot[:, 0:1]), (LEVELS, COLS))
    ytail[:, 1, :] = jnp.broadcast_to(hsum, (LEVELS, COLS))
    lane_y = lax.broadcasted_iota(jnp.int32, (ROWS, 512), 1)
    lower = lax.broadcasted_iota(jnp.int32, (ROWS, 512), 0) >= (lane_y & 31)
    zr_i = lax.broadcasted_iota(jnp.int32, (16, 256), 0)
    zc_i = lax.broadcasted_iota(jnp.int32, (16, 256), 1) >> 5

    def columns(rows):
        width = rows.shape[1]
        return jnp.transpose(jnp.concatenate([rows, jnp.zeros((120, width), F32)], axis=0))

    @pl.loop(0, LEVELS)
    def _(l):
        rows = yt[l]
        cols = columns(rows[:, 0:128])[0:ROWS]

        def col(f):
            return cols[:, f : f + 1]

        e = jnp.exp(-jnp.abs(col(0) - rows[0:1]))
        m = e * jnp.where(lower, col(2) * rows[1:2], col(1) * rows[2:3])
        part = lane_y >> 5
        mh, ml = split(m)
        m = jnp.where((part >= HALF) & (part < 2 * HALF), ml.astype(F32), mh.astype(F32))
        part = jnp.where(part < 3 * HALF, part % HALF, -1)
        for i in range(HALF):
            mt[l, ROWS * i : ROWS * i + ROWS, :] = jnp.where(part == i, m, 0.0).astype(BF16)
        z = jnp.where(zr_i == zc_i, rows[4:5, 0:256], 0.0) + jnp.where(zr_i == zc_i + 8, rows[3:4, 0:256], 0.0)
        z = jnp.where(zc_i < HALF, z, 0.0)
        zh, zl = split(z)
        zf[l, 0:16, :] = zh[:, 0:PACK]
        zf[l, 16:32, :] = zl[:, 0:PACK]
        pb[l] = jnp.broadcast_to(col(3), (ROWS, 128))
        qb[l] = jnp.broadcast_to(col(4), (ROWS, 128))

    low[:, QROWS:128, :] = jnp.zeros((TILES, 128 - QROWS, 128), BF16)

    loads[1].wait()

    @pl.loop(0, DROWS // 16)
    def _(i):
        rows = [
            cot_raw[:, pl.ds(pl.multiple_of(2048 * i + 128 * r, 128), 128)].astype(F32)
            for r in range(16)
        ]
        cot_v[pl.ds(pl.multiple_of(16 * i, 16), 16), :] = jnp.concatenate(rows, axis=0).astype(BF16)

    loads[0].wait()

    @pl.loop(CHIPS // 2, CHIPS)
    def _(i):
        w_load(w_tile(i)).start()

    pl.semaphore_wait(barrier, TILES - 1 + LEVELS - 1)

    def alpha_of(l, half):
        return alpha_v[HALF * half : HALF * half + HALF, l].reshape(PACK, COLS)

    def source(l, hi, lo=None):
        r = dot(zf[l], hi)
        z = r[0:16] + r[16:32]
        if lo is not None:
            z = z + dot(zf[l, 0:16, :], lo)
        return z

    def sources(field, za, zr, sem, first, last):
        @pl.loop(first, last)
        def _(k):
            found = []
            for i in range(2):
                l = lax.rem(chip + 2 * k + i + 1, LEVELS)
                for half in range(2):
                    found.append((half, l, source(l, *field(l, half))))
            for half, l, z in found:
                for j in range(3):
                    part = z[:, 128 * j : 128 * j + 128]
                    za[half, l, HALF * j : HALF * j + HALF, :] = part[0:HALF]
                    za[half, l, 16 + HALF * j : 16 + HALF * j + HALF, :] = part[8 : 8 + HALF]
                za[half, l, 15:16, :] = ytail[l, 0:1, 0:128]
                za[half, l, 31:32, :] = ytail[l, 1:2, 0:128]

        if last == LEVELS // 2:

            @pl.loop(1, TILES)
            def _(k):
                s = lax.rem(t + k, TILES)
                to_tile(za.at[lax.rem(s, 2), s // 2], zr.at[t], sem.at[0], sem.at[1], s).start()

            zr[t] = za[core, chip]

    def recursion(zr, zo, de, sem):
        wait_all(zr, sem.at[1], TILES)
        d = jnp.zeros((16, 128), F32)
        downs = []
        for s in range(TILES):
            downs.append(d)
            zo[s, 0:16, :] = d
            d = zr[s, 15:16, :] * d + zr[s, 0:16, :]
        e = jnp.zeros((16, 128), F32)
        for s in reversed(range(TILES)):
            zo[s, 16:32, :] = e
            e = zr[s, 15:16, :] * e + (zr[s, 16:32, :] + zr[s, 31:32, :] * downs[s])

        @pl.loop(1, TILES)
        def _(k):
            s = lax.rem(t + k, TILES)
            to_tile(zo.at[s], de.at[core, chip], sem.at[2], sem.at[3], s).start()

        de[core, chip] = zo[t]

    def carries_in(zo, sem):
        wait_all(zo, sem.at[3], TILES)

    def carries_sent(zo, sem):
        wait_all(zo, sem.at[0], TILES)
        wait_all(zo, sem.at[2], TILES)

    sources(lambda l, half: (alpha_of(l, half),), za, zr, z_sem, 0, LEVELS // 2)

    lane1 = lax.broadcasted_iota(jnp.int32, (1, 128), 1)
    lane = lax.broadcasted_iota(jnp.int32, (SLOTS, 128), 1)
    lgroup = lane >> 5
    slot_id = lax.broadcasted_iota(jnp.int32, (SLOTS, 128), 0)
    r16 = lax.broadcasted_iota(jnp.int32, (16, 128), 0) - (
        lax.broadcasted_iota(jnp.int32, (16, 128), 1) >> 5
    )
    sub96 = lax.broadcasted_iota(jnp.int32, (QROWS, 128), 0)
    sub384 = lax.broadcasted_iota(jnp.int32, (DROWS, 128), 0)

    def one_hot(condition):
        return jnp.where(condition, 1.0, 0.0).astype(BF16)

    def source_row(s):
        return jnp.where(lane1 < pc_ref[t, s], src_v[pl.ds(s, 1), :], -1)

    def target_row(s):
        return dst_v[pl.ds(s, 1), :]

    def spread_out(x):
        x = x + pltpu.roll(x, 64, 1)
        return x + pltpu.roll(x, 32, 1)

    def weight_pair(s, i):
        return jnp.concatenate(
            [
                w_v[s, 16 * (i + half) : 16 * (i + half) + 16].reshape(16 * BLK, 128)
                for half in range(2)
            ],
            axis=1,
        )

    def back_terms(tiles):
        srows = [source_row(s) for s in tiles]
        scols = [scol_v[s] for s in tiles]
        dcols = [dcol_v[s] for s in tiles]
        pick = jnp.concatenate(
            [
                jnp.concatenate([one_hot(lane + 128 * k == dcol) for k in range(3)], axis=1)
                for dcol in dcols
            ],
            axis=0,
        )
        grad = dot(pick, cot_v[...]).astype(BF16)
        results = []
        for n, s in enumerate(tiles):
            parts = []
            for i in range(0, 8, 2):
                first = SLOTS * n + 16 * i
                zero = jnp.zeros((16, 128), BF16)
                pair = jnp.concatenate(
                    [
                        jnp.concatenate([grad[first : first + 16], zero], axis=1),
                        jnp.concatenate([zero, grad[first + 16 : first + 32]], axis=1),
                    ],
                    axis=0,
                )
                o = dot_nt(pair, weight_pair(s, i))
                for half in range(2):
                    parts.append(
                        sum(
                            jnp.where(
                                r16 == 4 * j,
                                o[16 * half : 16 * half + 16, 128 * j : 128 * j + 128],
                                0.0,
                            )
                            for j in range(4)
                        )
                    )
            terms = spread_out(jnp.concatenate(parts, axis=0))
            terms = jnp.where(lgroup == (scols[n] & 3), terms, 0.0)
            put = one_hot(sub96 == (srows[n] >> 2))
            both = dot(put, jnp.concatenate(split(terms), axis=1))
            results.append(both[:, 0:128] + both[:, 128:256])
        return results

    def forward_terms(tiles):
        puts, sums = [], []
        for s in tiles:
            scol = scol_v[s]
            picked = dot(one_hot(lane == (scol >> 2)), low[s])
            picked = spread_out(jnp.where(lgroup == (scol & 3), picked, 0.0))
            parts = []
            for i in range(0, 8, 2):
                xs = []
                for half in range(2):
                    x = picked[16 * (i + half) : 16 * (i + half) + 16]
                    xs.append(
                        jnp.concatenate([jnp.where(r16 == 4 * j, x, 0.0) for j in range(4)], axis=1)
                    )
                both = dot(jnp.concatenate(xs, axis=0).astype(BF16), weight_pair(s, i))
                parts.append(both[0:16, 0:128])
                parts.append(both[16:32, 128:256])
            sums.append(jnp.concatenate(split(jnp.concatenate(parts, axis=0)), axis=1))
            puts.append(one_hot(sub384 == target_row(s)))
        both = dot(jnp.concatenate(puts, axis=1), jnp.concatenate(sums, axis=0))
        return both[:, 0:128] + both[:, 128:256]

    loads[2].wait()
    loads[3].wait()
    turned = jnp.transpose(
        jnp.concatenate([src_v[...], dst_v[...], jnp.zeros((96, SLOTS), jnp.int32)], axis=0).astype(F32)
    ).astype(jnp.int32)
    for s in range(TILES):
        scol = jnp.broadcast_to(turned[:, s : s + 1], (SLOTS, 128))
        scol_v[s] = jnp.where(slot_id < pc_ref[t, s], scol, -1)
        dcol_v[s] = jnp.broadcast_to(turned[:, TILES + s : TILES + s + 1], (SLOTS, 128))

    def off_chip(ch):
        return to_tile(ss.at[ch], sr.at[chip], ss_s, ss_r, tile_of(ch))

    def core_pair(ch):
        return to_tile(sf.at[0, ch], sp.at[ch], sp_s, sp_r.at[ch], partner)

    steps = TILES // GROUP

    @pl.loop(0, steps)
    def _(j):
        late = j // (steps // 2)
        chips = [chip_peer(GROUP * (j - steps // 2 * late) + 1 + i) for i in range(GROUP)]
        tiles = [2 * ch + 1 - core + late * (2 * core - 1) for ch in chips]
        for s in tiles:
            w_load(s).wait()

        @pl.when(late == 0)
        def _():
            for i in range(GROUP):
                w_load(w_tile(CHIPS + GROUP * j + i)).start()

        @pl.when(j == steps // 2)
        def _():
            loads[4].start()

        for ch, r in zip(chips, back_terms(tiles)):
            sf[late, ch] = r

        @pl.when(late == 0)
        def _():
            for ch in chips:
                core_pair(ch).start()

        @pl.when(late == 1)
        def _():
            for ch in chips:
                core_pair(ch).wait_recv()
                ss[ch] = sf[1, ch] + sp[ch]

                @pl.when(ch != chip)
                def _():
                    off_chip(ch).start()

        @pl.when(j == steps // 2 - 1)
        def _():
            recursion(zr, zo, de, z_sem)

    sr[chip] = ss[chip]

    ax = dx_ref[...]
    posx = lax.broadcasted_iota(jnp.int32, (8, COLS), 1)
    lx, hx = scans(ax, posx, COLS, COLS)
    cx = coefficient(ax)
    gx = cx * hx
    edge1 = jnp.broadcast_to(lx[:, 127:128], (8, COLS))
    edge2 = jnp.broadcast_to(lx[:, 255:256], (8, COLS))
    xt[:, 0, :] = lx
    xt[:, 1, :] = cx
    xt[:, 2, :] = gx
    xt[:, 3, :] = gx * jnp.exp(jnp.minimum(lx - jnp.where(posx < 256, edge1, edge2), 0.0))
    xt[:, 4, :] = cx * jnp.exp(jnp.minimum(edge1 - lx, 0.0))
    xt[:, 5, :] = cx * jnp.exp(jnp.minimum(edge2 - lx, 0.0))
    xt[:, 6:8, :] = jnp.zeros((LEVELS, 2, COLS), F32)
    lowx = lax.broadcasted_iota(jnp.int32, (128, 128), 0) >= (
        lax.broadcasted_iota(jnp.int32, (128, 128), 1)
    )

    @pl.loop(0, LEVELS)
    def _(l):
        rows = xt[l]
        cols = columns(rows)
        for ib in range(3):
            for jb in range(3):
                r = rows[:, 128 * jb : 128 * jb + 128]

                def xcol(f):
                    return cols[128 * ib : 128 * ib + 128, f : f + 1]

                if ib == jb:
                    e = jnp.exp(-jnp.abs(xcol(0) - r[0:1]))
                    m = e * jnp.where(lowx, xcol(2) * r[1:2], xcol(1) * r[2:3])
                elif ib > jb:
                    m = xcol(3) * r[3 + ib : 4 + ib]
                else:
                    m = xcol(3 + jb) * r[3:4]
                mh, ml = split(m)
                kk[l, 128 * ib : 128 * ib + 128, 128 * jb : 128 * jb + 128] = mh
                at = COLS + 128 * ib
                kk[l, at : at + 128, 128 * jb : 128 * jb + 128] = ml

    exports = [
        pltpu.make_async_copy(x, y, out_sem.at[i])
        for i, (x, y) in enumerate(
            [
                (mt, mt_hbm), (pb, pb_hbm), (qb, qb_hbm), (kk.at[:, pl.ds(0, COLS), :], kk_hbm),
                (back, back_hbm), (de2, de_hbm), (inc_v, inc_hbm),
            ]
        )
    ]
    for x in exports[:4]:
        x.start()

    wait_all(sr, ss_r, CHIPS)
    acc = sr[0]
    for s in range(1, CHIPS):
        acc = acc + sr[s]
    bq[...] = acc
    for j in range(3):
        back[g, :, 128 * j : 128 * j + 128] = bq[pl.ds(j, ROWS, stride=3), :].astype(BF16)

    @pl.loop(1, LEVELS)
    def _(k):
        l = mem_peer(k)
        to_mem(back.at[g], back.at[g], bk_s, bk_r, l).start()

    loads[4].wait()
    carries_in(zo, z_sem)

    def partial(l):
        y = smooth(
            [(alpha_of(l, half),) for half in range(2)], (de[0, l], de[1, l]),
            mt[l], pb[l], qb[l], kk[l, 0:COLS], kk[l, COLS : 2 * COLS],
        )
        acc = jnp.zeros((ROWS, COLS), F32)
        for m in range(2 * HALF):
            acc = acc + (live[m] * pert_v[m, l].astype(F32)) * y[ROWS * m : ROWS * m + ROWS]
        return acc

    @pl.loop(1, LEVELS + 1)
    def _(k):
        l = mem_peer(k)
        ps[l] = partial(l)

        @pl.when(l != g)
        def _():
            to_mem(ps.at[l], pr.at[g], rs_s, rs_r, l).start()

    pr[g] = ps[g]

    wait_all(back, bk_r, LEVELS)
    exports[4].start()

    def weighted(l, half):
        x = pert_v[HALF * half : HALF * half + HALF, l].astype(F32) * back[l].astype(F32)[None]
        return split(x.reshape(PACK, COLS))

    sources(weighted, za2, zr2, z2_sem, 0, 2)

    wait_all(pr, rs_r, LEVELS)
    acc = pr[0]
    for s in range(1, LEVELS):
        acc = acc + pr[s]
    acc = acc * scale
    for j in range(3):
        lq[pl.ds(j, ROWS, stride=3), :] = acc[:, 128 * j : 128 * j + 128]
    lows[...] = lq[...].astype(BF16)

    def low_rows(s):
        return low.at[s, pl.ds(0, QROWS), :]

    def low_to(s):
        return to_tile(lows, low_rows(t), lo_s, lo_r.at[t], s)

    def low_on(s):
        return to_tile(low_rows(s), low_rows(s), lo_f, lo_r.at[s], partner)

    @pl.loop(1, CHIPS)
    def _(k):
        low_to(tile_of(chip_peer(k))).start()

    low_to(partner).start()

    low[t, 0:QROWS, :] = lows[...]

    sources(weighted, za2, zr2, z2_sem, 2, 4)

    inc_v[...] = jnp.zeros((DROWS, 128), F32)

    @pl.loop(0, steps)
    def _(j):
        tiles = []
        for i in range(GROUP):
            n = GROUP * j + i
            afar = (n + TILES - 2) // TILES
            late = n // (CHIPS + 1)
            ch = chip_back(afar * (n - 1 - (CHIPS - 1) * late))
            s = 2 * ch + core + (late + (1 - afar) * lax.rem(n, 2)) * (1 - 2 * core)
            tiles.append(s)

            @pl.when(n > 0)
            def _():
                low_on(s).wait_recv()

            @pl.when((afar == 1) & (late == 0))
            def _():
                low_on(s).start()

        inc_v[...] += forward_terms(tiles)

        @pl.when(j == steps // 2 - 1)
        def _():
            recursion(zr2, zo2, de2, z2_sem)

    exports[6].start()
    carries_in(zo2, z2_sem)
    exports[5].start()

    carries_sent(zo, z_sem)
    carries_sent(zo2, z2_sem)
    pltpu.make_async_copy(sp, sp, sp_s).wait()
    wait_all(ss, ss_s, CHIPS)
    lows8 = low.at[pl.ds(0, CHIPS), pl.ds(0, QROWS), :]
    pltpu.make_async_copy(lows8, lows8, lo_s).wait()
    lows7 = low.at[pl.ds(0, CHIPS - 1), pl.ds(0, QROWS), :]
    pltpu.make_async_copy(lows7, lows7, lo_f).wait()
    wait_all(ps, rs_s, LEVELS)
    wait_all(back, bk_s, LEVELS)
    for x in exports:
        x.wait()


def shards(
    alpha, perturbation, cotangent, decay_y, decay_x, group_members, interp_weight,
    pair_count, src_index, dst_index,
):
    any_spec = pl.BlockSpec(memory_space=pl.ANY)
    vmem = pl.BlockSpec(memory_space=pltpu.VMEM)
    smem = pl.BlockSpec(memory_space=pltpu.SMEM)
    dma = pltpu.SemaphoreType.DMA
    V = pltpu.VMEM
    zbuf = V((TILES, 32, 128), F32)
    zpair = V((2, CHIPS, 32, 128), F32)
    zall = [zpair, zbuf, zbuf, zpair]
    scratch = [
        V((2 * HALF, LEVELS, ROWS, COLS), BF16),
        V((2 * HALF, LEVELS, ROWS, COLS), BF16),
        V((1, DROWS * 128), BF16),
        V((DROWS, 128), BF16),
        V((TILES, SLOTS, BLK, 128), BF16),
        V((TILES, SLOTS), jnp.int32),
        V((TILES, SLOTS), jnp.int32),
        V((8, 512), F32),
        V((LEVELS, 8, 512), F32),
        V((LEVELS, 2, COLS), F32),
        V((LEVELS, 8, COLS), F32),
        V((LEVELS, PACK, 512), BF16),
        V((LEVELS, 32, PACK), BF16),
        V((LEVELS, ROWS, 128), F32),
        V((LEVELS, ROWS, 128), F32),
        V((LEVELS, 2 * COLS, COLS), BF16),
        *zall,
        *zall,
        V((2, CHIPS, QROWS, 128), F32),
        V((CHIPS, QROWS, 128), F32),
        V((CHIPS, QROWS, 128), F32),
        V((CHIPS, QROWS, 128), F32),
        V((QROWS, 128), F32),
        V((LEVELS, ROWS, COLS), BF16),
        V((LEVELS, ROWS, COLS), F32),
        V((LEVELS, ROWS, COLS), F32),
        V((QROWS, 128), F32),
        V((TILES, 128, 128), BF16),
        V((QROWS, 128), BF16),
        V((DROWS, 128), F32),
        V((TILES, SLOTS, 128), jnp.int32),
        V((TILES, SLOTS, 128), jnp.int32),
        dma((5,)),
        dma((TILES,)),
        dma((7,)),
        dma((4,)),
        dma((4,)),
        dma,
        dma((CHIPS,)),
        *[dma] * 6,
        dma((TILES,)),
        dma,
        dma,
    ]
    shape = jax.ShapeDtypeStruct
    inc, *rest = pl.pallas_call(
        kernel,
        out_shape=(
            shape((DROWS, 128), F32),
            shape((LEVELS, ROWS, COLS), BF16),
            shape((2, CHIPS, 32, 128), F32),
            shape((LEVELS, PACK, 512), BF16),
            shape((LEVELS, ROWS, 128), F32),
            shape((LEVELS, ROWS, 128), F32),
            shape((LEVELS, COLS, COLS), BF16),
        ),
        in_specs=[any_spec, any_spec, any_spec, vmem, vmem, smem, any_spec, smem, any_spec, any_spec],
        out_specs=(any_spec,) * 7,
        scratch_shapes=scratch,
        compiler_params=pltpu.CompilerParams(
            collective_id=0, has_side_effects=True, vmem_limit_bytes=60 * 1024 * 1024
        ),
        cost_estimate=pl.CostEstimate(
            flops=9_000_000_000, bytes_accessed=29_000_000, transcendentals=700_000
        ),
    )(
        alpha, perturbation, cotangent, decay_y, decay_x, group_members,
        interp_weight, pair_count, src_index, dst_index,
    )

    members_shape = (2 * HALF, LEVELS, ROWS, COLS)
    return pl.pallas_call(
        grad_kernel,
        out_shape=(shape((1, DROWS * 128), F32), shape(alpha.shape, F32)),
        in_specs=[smem, *[any_spec] * 7, vmem],
        out_specs=(vmem, any_spec),
        scratch_shapes=[
            V(members_shape, BF16),
            V((LEVELS, ROWS, COLS), BF16),
            V((2, CHIPS, 32, 128), F32),
            V((LEVELS, PACK, 512), BF16),
            V((LEVELS, ROWS, 128), F32),
            V((LEVELS, ROWS, 128), F32),
            V((LEVELS, COLS, COLS), BF16),
            V(members_shape, F32),
            dma((4,)),
            dma((3, LEVELS)),
            dma((LEVELS,)),
        ],
        compiler_params=pltpu.CompilerParams(vmem_limit_bytes=60 * 1024 * 1024),
        cost_estimate=pl.CostEstimate(
            flops=3_500_000_000, bytes_accessed=11_000_000, transcendentals=0
        ),
    )(group_members, perturbation, *rest, inc)


def solution(mesh):
    in_specs = (
        P("mem", None, "tile", None),
        P("mem", None, "tile", None),
        P("mem", "tile"),
        P(None, "tile"),
        P(),
        P(),
        P("tile", None, None, None, None),
        P(),
        P(),
        P(),
    )
    out_specs = (P("mem", "tile"), P("mem", None, "tile", None))
    return jax.shard_map(shards, mesh=mesh, in_specs=in_specs, out_specs=out_specs, check_vma=False)
```

```python
import jax
import jax.numpy as jnp
from jax import lax
from jax.experimental import pallas as pl
from jax.experimental.pallas import tpu as pltpu
from jax.sharding import PartitionSpec as P

MESH = pl.DeviceIdType.MESH
F32 = jnp.float32
BF16 = jnp.bfloat16

LEVELS = 8
TILES = 16
CHIPS = 8
ROWS = 32
COLS = 384
HALF = 5
PACK = HALF * ROWS
SLOTS = 128
BLK = 32
QROWS = ROWS * COLS // 128
DROWS = 384
GROUP = 2


def dot(a, b):
    return lax.dot_general(a, b, (((1,), (0,)), ((), ())), preferred_element_type=F32)


def dot_nt(a, b):
    return lax.dot_general(a, b, (((1,), (1,)), ((), ())), preferred_element_type=F32)


def split(x):
    high = x.astype(BF16)
    return high, (x - high.astype(F32)).astype(BF16)


def coefficient(a):
    t = 1.0 - a * a
    ratio = (t * t * t) / (1.0 + a * a)
    return jnp.where(ratio > 0.0, jnp.sqrt(jnp.sqrt(jnp.maximum(ratio, 1e-37))), 0.0)


def scans(a, pos, width, segment):
    logs = jnp.log(a)
    steps = [1 << b for b in range(16) if (1 << b) < segment]
    for k in steps:
        logs = logs + jnp.where(pos >= k, pltpu.roll(logs, k, 1), 0.0)
    rate = jnp.where(pos < segment - 1, pltpu.roll(a * a, width - 1, 1), 0.0)
    h = jnp.ones_like(a)
    for k in steps:
        h = h + rate * pltpu.roll(h, width - k, 1)
        rate = rate * pltpu.roll(rate, width - k, 1)
    return logs, h


def carry_row(carry, first):
    rows = [carry[first + HALF * j : first + HALF * j + 1, :] for j in range(3)]
    return jnp.concatenate(rows, axis=1)


def smooth(fields, carries, mt, pb, qb, upper, lower=None):
    p3 = jnp.concatenate([pb] * 3, axis=1)
    q3 = jnp.concatenate([qb] * 3, axis=1)
    rows = []
    for field, carry in zip(fields, carries):
        hi, *lo = field
        stack = jnp.concatenate([hi, hi, *lo], axis=0)
        y = dot(mt[:, 0 : stack.shape[0]], stack)
        for m in range(HALF):
            rows.append(
                y[ROWS * m : ROWS * m + ROWS]
                + p3 * carry_row(carry, m)
                + q3 * carry_row(carry, 16 + m)
            )
    yh, yl = split(jnp.concatenate(rows, axis=0))
    if lower is None:
        return dot(jnp.concatenate([yh, yl], axis=1), jnp.concatenate([upper] * 2, axis=0))
    return dot(
        jnp.concatenate([yh, yl, yh], axis=1), jnp.concatenate([upper, upper, lower], axis=0)
    )


def members(gm_ref):
    own = gm_ref[lax.axis_index("mem")]
    total = gm_ref[0]
    for i in range(1, LEVELS):
        total = total + gm_ref[i]
    scale = 1.0 / jnp.sqrt(jnp.full((1, COLS), total.astype(F32) - 1.0, F32))
    return scale, [jnp.where(m < own, 1.0, 0.0).astype(F32) for m in range(2 * HALF)]


def grad_kernel(
    gm_ref, pert_hbm, back_hbm, de_hbm, mt_hbm, pb_hbm, qb_hbm, kk_hbm, inc_ref,
    inc_out, grad_hbm,
    pert_v, back_v, de_v, mt_v, pb_v, qb_v, kk_v, out_v, whole_sem, in_sem, out_sem,
):
    whole = [
        pltpu.make_async_copy(a, b, whole_sem.at[i])
        for i, (a, b) in enumerate(
            [(back_hbm, back_v), (de_hbm, de_v), (pb_hbm, pb_v), (qb_hbm, qb_v)]
        )
    ]

    def loads(l):
        return [
            pltpu.make_async_copy(pert_hbm.at[:, l], pert_v.at[:, l], in_sem.at[0, l]),
            pltpu.make_async_copy(kk_hbm.at[l], kk_v.at[l], in_sem.at[1, l]),
            pltpu.make_async_copy(mt_hbm.at[l], mt_v.at[l], in_sem.at[2, l]),
        ]

    def store(l):
        return pltpu.make_async_copy(out_v.at[:, l], grad_hbm.at[:, l], out_sem.at[l])

    for x in whole:
        x.start()

    @pl.loop(0, LEVELS)
    def _(l):
        for x in loads(l):
            x.start()

    scale, live = members(gm_ref)

    @pl.loop(0, DROWS // 8)
    def _(i):
        x = inc_ref[pl.ds(pl.multiple_of(8 * i, 8), 8), :]
        for r in range(8):
            inc_out[0:1, pl.ds(pl.multiple_of(1024 * i + 128 * r, 128), 128)] = x[r : r + 1, :]

    for x in whole:
        x.wait()

    @pl.loop(0, LEVELS)
    def _(l):
        for x in loads(l):
            x.wait()
        fields = []
        for half in range(2):
            x = pert_v[HALF * half : HALF * half + HALF, l].astype(F32) * back_v[l].astype(F32)[None]
            fields.append(split(x.reshape(PACK, COLS)))
        y = smooth(fields, (de_v[0, l], de_v[1, l]), mt_v[l], pb_v[l], qb_v[l], kk_v[l])
        for m in range(2 * HALF):
            out_v[m, l] = y[ROWS * m : ROWS * m + ROWS] * (scale * live[m])
        store(l).start()

    @pl.loop(0, LEVELS)
    def _(l):
        store(l).wait()


def kernel(
    alpha_hbm, pert_hbm, cot_hbm, dy_ref, dx_ref, gm_ref, w_hbm, pc_ref, src_hbm, dst_hbm,
    inc_hbm, back_hbm, de_hbm, mt_hbm, pb_hbm, qb_hbm, kk_hbm,
    alpha_v, pert_v, cot_raw, cot_v, w_v, src_v, dst_v,
    rep_v, yt, ytail, xt, mt, zf, pb, qb, kk,
    za, zr, zo, de, za2, zr2, zo2, de2,
    sf, sp, ss, sr, bq, back, ps, pr, lq, low, lows, inc_v, scol_v, dcol_v,
    in_sem, w_sem, out_sem, z_sem, z2_sem,
    sp_s, sp_r, ss_s, ss_r, rs_s, rs_r, lo_s, lo_f, lo_r, bk_s, bk_r,
):
    g = lax.axis_index("mem")
    t = lax.axis_index("tile")

    chip = t // 2
    core = lax.rem(t, 2)
    partner = t + 1 - 2 * core

    def chip_peer(k):
        return lax.rem(chip + k, CHIPS)

    def chip_back(k):
        return lax.rem(chip + CHIPS - k, CHIPS)

    def tile_of(ch):
        return 2 * ch + core

    def mem_peer(k):
        return lax.rem(g + k, LEVELS)

    def to_tile(src, dst, ssem, rsem, s):
        return pltpu.make_async_remote_copy(
            src_ref=src, dst_ref=dst, send_sem=ssem, recv_sem=rsem,
            device_id={"tile": s}, device_id_type=MESH,
        )

    def to_mem(src, dst, ssem, rsem, s):
        return pltpu.make_async_remote_copy(
            src_ref=src, dst_ref=dst, send_sem=ssem, recv_sem=rsem,
            device_id={"mem": s}, device_id_type=MESH,
        )

    loads = [
        pltpu.make_async_copy(alpha_hbm, alpha_v, in_sem.at[0]),
        pltpu.make_async_copy(cot_hbm, cot_raw, in_sem.at[1]),
        pltpu.make_async_copy(src_hbm.at[t], src_v, in_sem.at[2]),
        pltpu.make_async_copy(dst_hbm.at[t], dst_v, in_sem.at[3]),
        pltpu.make_async_copy(pert_hbm, pert_v, in_sem.at[4]),
    ]

    def wait_all(buf, sem, count):
        part = buf.at[pl.ds(0, count - 1)]
        pltpu.make_async_copy(part, part, sem).wait()

    def w_load(s):
        return pltpu.make_async_copy(w_hbm.at[0, s], w_v.at[s], w_sem.at[s])

    def w_tile(i):
        late = i // CHIPS
        return 2 * chip_peer(i - CHIPS * late + 1) + 1 - core + late * (2 * core - 1)

    for c in loads[:4]:
        c.start()

    @pl.loop(0, CHIPS // 2)
    def _(i):
        w_load(w_tile(i)).start()

    barrier = pltpu.get_barrier_semaphore()

    @pl.loop(1, TILES)
    def _(k):
        pl.semaphore_signal(
            barrier, inc=1, device_id={"tile": lax.rem(t + k, TILES)}, device_id_type=MESH
        )

    @pl.loop(1, LEVELS)
    def _(k):
        pl.semaphore_signal(barrier, inc=1, device_id={"mem": mem_peer(k)}, device_id_type=MESH)

    scale, live = members(gm_ref)

    for k in range(16):
        rep_v[:, 32 * k : 32 * k + 32] = dy_ref[...]
    a = rep_v[...]
    pos = lax.broadcasted_iota(jnp.int32, (8, 512), 1) & 31
    logs, h = scans(a, pos, 512, ROWS)
    c = coefficient(a)
    ltot = jnp.broadcast_to(logs[:, 31:32], (8, 512))
    lane512 = lax.broadcasted_iota(jnp.int32, (8, 512), 1)
    hsum = jnp.sum(jnp.where(lane512 < 32, jnp.exp(2.0 * logs), 0.0), axis=1, keepdims=True)
    for f, x in enumerate(
        (logs, c, c * h, c * h * jnp.exp(logs), c * jnp.exp(ltot - logs))
    ):
        yt[:, f, :] = x
    yt[:, 5:8, :] = jnp.zeros((LEVELS, 3, 512), F32)
    ytail[:, 0, :] = jnp.broadcast_to(jnp.exp(ltot[:, 0:1]), (LEVELS, COLS))
    ytail[:, 1, :] = jnp.broadcast_to(hsum, (LEVELS, COLS))
    lane_y = lax.broadcasted_iota(jnp.int32, (ROWS, 512), 1)
    lower = lax.broadcasted_iota(jnp.int32, (ROWS, 512), 0) >= (lane_y & 31)
    zr_i = lax.broadcasted_iota(jnp.int32, (16, 256), 0)
    zc_i = lax.broadcasted_iota(jnp.int32, (16, 256), 1) >> 5

    def columns(rows):
        width = rows.shape[1]
        return jnp.transpose(jnp.concatenate([rows, jnp.zeros((120, width), F32)], axis=0))

    @pl.loop(0, LEVELS)
    def _(l):
        rows = yt[l]
        cols = columns(rows[:, 0:128])[0:ROWS]

        def col(f):
            return cols[:, f : f + 1]

        e = jnp.exp(-jnp.abs(col(0) - rows[0:1]))
        m = e * jnp.where(lower, col(2) * rows[1:2], col(1) * rows[2:3])
        part = lane_y >> 5
        mh, ml = split(m)
        m = jnp.where((part >= HALF) & (part < 2 * HALF), ml.astype(F32), mh.astype(F32))
        part = jnp.where(part < 3 * HALF, part % HALF, -1)
        for i in range(HALF):
            mt[l, ROWS * i : ROWS * i + ROWS, :] = jnp.where(part == i, m, 0.0).astype(BF16)
        z = jnp.where(zr_i == zc_i, rows[4:5, 0:256], 0.0) + jnp.where(zr_i == zc_i + 8, rows[3:4, 0:256], 0.0)
        z = jnp.where(zc_i < HALF, z, 0.0)
        zh, zl = split(z)
        zf[l, 0:16, :] = zh[:, 0:PACK]
        zf[l, 16:32, :] = zl[:, 0:PACK]
        pb[l] = jnp.broadcast_to(col(3), (ROWS, 128))
        qb[l] = jnp.broadcast_to(col(4), (ROWS, 128))

    low[:, QROWS:128, :] = jnp.zeros((TILES, 128 - QROWS, 128), BF16)

    loads[1].wait()

    @pl.loop(0, DROWS // 16)
    def _(i):
        rows = [
            cot_raw[:, pl.ds(pl.multiple_of(2048 * i + 128 * r, 128), 128)].astype(F32)
            for r in range(16)
        ]
        cot_v[pl.ds(pl.multiple_of(16 * i, 16), 16), :] = jnp.concatenate(rows, axis=0).astype(BF16)

    slot_id = lax.broadcasted_iota(jnp.int32, (SLOTS, 128), 0)
    loads[2].wait()
    loads[3].wait()
    turned = jnp.transpose(
        jnp.concatenate([src_v[...], dst_v[...], jnp.zeros((96, SLOTS), jnp.int32)], axis=0).astype(F32)
    ).astype(jnp.int32)
    for s in range(TILES):
        scol = jnp.broadcast_to(turned[:, s : s + 1], (SLOTS, 128))
        scol_v[s] = jnp.where(slot_id < pc_ref[t, s], scol, -1)
        dcol_v[s] = jnp.broadcast_to(turned[:, TILES + s : TILES + s + 1], (SLOTS, 128))

    loads[0].wait()

    @pl.loop(CHIPS // 2, CHIPS)
    def _(i):
        w_load(w_tile(i)).start()

    pl.semaphore_wait(barrier, TILES - 1 + LEVELS - 1)

    def alpha_of(l, half):
        return alpha_v[HALF * half : HALF * half + HALF, l].reshape(PACK, COLS)

    def source(l, hi, lo=None):
        r = dot(zf[l], hi)
        z = r[0:16] + r[16:32]
        if lo is not None:
            z = z + dot(zf[l, 0:16, :], lo)
        return z

    def sources(field, za, zr, sem, first, last):
        @pl.loop(first, last)
        def _(k):
            found = []
            for i in range(2):
                l = lax.rem(chip + 2 * k + i + 1, LEVELS)
                for half in range(2):
                    found.append((half, l, source(l, *field(l, half))))
            for half, l, z in found:
                for j in range(3):
                    part = z[:, 128 * j : 128 * j + 128]
                    za[half, l, HALF * j : HALF * j + HALF, :] = part[0:HALF]
                    za[half, l, 16 + HALF * j : 16 + HALF * j + HALF, :] = part[8 : 8 + HALF]
                za[half, l, 15:16, :] = ytail[l, 0:1, 0:128]
                za[half, l, 31:32, :] = ytail[l, 1:2, 0:128]

        if last == LEVELS // 2:

            @pl.loop(1, TILES)
            def _(k):
                s = lax.rem(t + k, TILES)
                to_tile(za.at[lax.rem(s, 2), s // 2], zr.at[t], sem.at[0], sem.at[1], s).start()

            zr[t] = za[core, chip]

    def recursion(zr, zo, de, sem):
        wait_all(zr, sem.at[1], TILES)
        d = jnp.zeros((16, 128), F32)
        downs = []
        for s in range(TILES):
            downs.append(d)
            zo[s, 0:16, :] = d
            d = zr[s, 15:16, :] * d + zr[s, 0:16, :]
        e = jnp.zeros((16, 128), F32)
        for s in reversed(range(TILES)):
            zo[s, 16:32, :] = e
            e = zr[s, 15:16, :] * e + (zr[s, 16:32, :] + zr[s, 31:32, :] * downs[s])

        @pl.loop(1, TILES)
        def _(k):
            s = lax.rem(t + k, TILES)
            to_tile(zo.at[s], de.at[core, chip], sem.at[2], sem.at[3], s).start()

        de[core, chip] = zo[t]

    def carries_in(zo, sem):
        wait_all(zo, sem.at[3], TILES)

    def carries_sent(zo, sem):
        wait_all(zo, sem.at[0], TILES)
        wait_all(zo, sem.at[2], TILES)

    sources(lambda l, half: (alpha_of(l, half),), za, zr, z_sem, 0, LEVELS // 2)

    lane1 = lax.broadcasted_iota(jnp.int32, (1, 128), 1)
    lane = lax.broadcasted_iota(jnp.int32, (SLOTS, 128), 1)
    lgroup = lane >> 5
    r16 = lax.broadcasted_iota(jnp.int32, (16, 128), 0) - (
        lax.broadcasted_iota(jnp.int32, (16, 128), 1) >> 5
    )
    sub96 = lax.broadcasted_iota(jnp.int32, (QROWS, 128), 0)
    sub384 = lax.broadcasted_iota(jnp.int32, (DROWS, 128), 0)

    def one_hot(condition):
        return jnp.where(condition, 1.0, 0.0).astype(BF16)

    def source_row(s):
        return jnp.where(lane1 < pc_ref[t, s], src_v[pl.ds(s, 1), :], -1)

    def target_row(s):
        return dst_v[pl.ds(s, 1), :]

    def spread_out(x):
        x = x + pltpu.roll(x, 64, 1)
        return x + pltpu.roll(x, 32, 1)

    def weight_pair(s, i):
        return jnp.concatenate(
            [
                w_v[s, 16 * (i + half) : 16 * (i + half) + 16].reshape(16 * BLK, 128)
                for half in range(2)
            ],
            axis=1,
        )

    def back_terms(tiles):
        srows = [source_row(s) for s in tiles]
        scols = [scol_v[s] for s in tiles]
        dcols = [dcol_v[s] for s in tiles]
        pick = jnp.concatenate(
            [
                jnp.concatenate([one_hot(lane + 128 * k == dcol) for k in range(3)], axis=1)
                for dcol in dcols
            ],
            axis=0,
        )
        grad = dot(pick, cot_v[...]).astype(BF16)
        results = []
        for n, s in enumerate(tiles):
            parts = []
            for i in range(0, 8, 2):
                first = SLOTS * n + 16 * i
                zero = jnp.zeros((16, 128), BF16)
                pair = jnp.concatenate(
                    [
                        jnp.concatenate([grad[first : first + 16], zero], axis=1),
                        jnp.concatenate([zero, grad[first + 16 : first + 32]], axis=1),
                    ],
                    axis=0,
                )
                o = dot_nt(pair, weight_pair(s, i))
                for half in range(2):
                    parts.append(
                        sum(
                            jnp.where(
                                r16 == 4 * j,
                                o[16 * half : 16 * half + 16, 128 * j : 128 * j + 128],
                                0.0,
                            )
                            for j in range(4)
                        )
                    )
            terms = spread_out(jnp.concatenate(parts, axis=0))
            terms = jnp.where(lgroup == (scols[n] & 3), terms, 0.0)
            put = one_hot(sub96 == (srows[n] >> 2))
            both = dot(put, jnp.concatenate(split(terms), axis=1))
            results.append(both[:, 0:128] + both[:, 128:256])
        return results

    def forward_terms(tiles):
        puts, sums = [], []
        for s in tiles:
            scol = scol_v[s]
            picked = dot(one_hot(lane == (scol >> 2)), low[s])
            picked = spread_out(jnp.where(lgroup == (scol & 3), picked, 0.0))
            parts = []
            for i in range(0, 8, 2):
                xs = []
                for half in range(2):
                    x = picked[16 * (i + half) : 16 * (i + half) + 16]
                    xs.append(
                        jnp.concatenate([jnp.where(r16 == 4 * j, x, 0.0) for j in range(4)], axis=1)
                    )
                both = dot(jnp.concatenate(xs, axis=0).astype(BF16), weight_pair(s, i))
                parts.append(both[0:16, 0:128])
                parts.append(both[16:32, 128:256])
            sums.append(jnp.concatenate(split(jnp.concatenate(parts, axis=0)), axis=1))
            puts.append(one_hot(sub384 == target_row(s)))
        both = dot(jnp.concatenate(puts, axis=1), jnp.concatenate(sums, axis=0))
        return both[:, 0:128] + both[:, 128:256]

    def off_chip(ch):
        return to_tile(ss.at[ch], sr.at[chip], ss_s, ss_r, tile_of(ch))

    def core_pair(ch):
        return to_tile(sf.at[0, ch], sp.at[ch], sp_s, sp_r.at[ch], partner)

    steps = TILES // GROUP

    @pl.loop(0, steps)
    def _(j):
        late = j // (steps // 2)
        chips = [chip_peer(GROUP * (j - steps // 2 * late) + 1 + i) for i in range(GROUP)]
        tiles = [2 * ch + 1 - core + late * (2 * core - 1) for ch in chips]
        for s in tiles:
            w_load(s).wait()

        @pl.when(late == 0)
        def _():
            for i in range(GROUP):
                w_load(w_tile(CHIPS + GROUP * j + i)).start()

        @pl.when(j == steps // 2)
        def _():
            loads[4].start()

        for ch, r in zip(chips, back_terms(tiles)):
            sf[late, ch] = r

        @pl.when(late == 0)
        def _():
            for ch in chips:
                core_pair(ch).start()

        @pl.when(late == 1)
        def _():
            for ch in chips:
                core_pair(ch).wait_recv()
                ss[ch] = sf[1, ch] + sp[ch]

                @pl.when(ch != chip)
                def _():
                    off_chip(ch).start()

        @pl.when(j == steps // 2 - 1)
        def _():
            recursion(zr, zo, de, z_sem)

    sr[chip] = ss[chip]

    ax = dx_ref[...]
    posx = lax.broadcasted_iota(jnp.int32, (8, COLS), 1)
    lx, hx = scans(ax, posx, COLS, COLS)
    cx = coefficient(ax)
    gx = cx * hx
    edge1 = jnp.broadcast_to(lx[:, 127:128], (8, COLS))
    edge2 = jnp.broadcast_to(lx[:, 255:256], (8, COLS))
    xt[:, 0, :] = lx
    xt[:, 1, :] = cx
    xt[:, 2, :] = gx
    xt[:, 3, :] = gx * jnp.exp(jnp.minimum(lx - jnp.where(posx < 256, edge1, edge2), 0.0))
    xt[:, 4, :] = cx * jnp.exp(jnp.minimum(edge1 - lx, 0.0))
    xt[:, 5, :] = cx * jnp.exp(jnp.minimum(edge2 - lx, 0.0))
    xt[:, 6:8, :] = jnp.zeros((LEVELS, 2, COLS), F32)
    lowx = lax.broadcasted_iota(jnp.int32, (128, 128), 0) >= (
        lax.broadcasted_iota(jnp.int32, (128, 128), 1)
    )

    @pl.loop(0, LEVELS)
    def _(l):
        rows = xt[l]
        cols = columns(rows)
        for ib in range(3):
            for jb in range(3):
                r = rows[:, 128 * jb : 128 * jb + 128]

                def xcol(f):
                    return cols[128 * ib : 128 * ib + 128, f : f + 1]

                if ib == jb:
                    e = jnp.exp(-jnp.abs(xcol(0) - r[0:1]))
                    m = e * jnp.where(lowx, xcol(2) * r[1:2], xcol(1) * r[2:3])
                elif ib > jb:
                    m = xcol(3) * r[3 + ib : 4 + ib]
                else:
                    m = xcol(3 + jb) * r[3:4]
                mh, ml = split(m)
                kk[l, 128 * ib : 128 * ib + 128, 128 * jb : 128 * jb + 128] = mh
                at = COLS + 128 * ib
                kk[l, at : at + 128, 128 * jb : 128 * jb + 128] = ml

    exports = [
        pltpu.make_async_copy(x, y, out_sem.at[i])
        for i, (x, y) in enumerate(
            [
                (mt, mt_hbm), (pb, pb_hbm), (qb, qb_hbm), (kk.at[:, pl.ds(0, COLS), :], kk_hbm),
                (back, back_hbm), (de2, de_hbm), (inc_v, inc_hbm),
            ]
        )
    ]
    for x in exports[:4]:
        x.start()

    wait_all(sr, ss_r, CHIPS)
    acc = sr[0]
    for s in range(1, CHIPS):
        acc = acc + sr[s]
    bq[...] = acc
    for j in range(3):
        back[g, :, 128 * j : 128 * j + 128] = bq[pl.ds(j, ROWS, stride=3), :].astype(BF16)

    @pl.loop(1, LEVELS)
    def _(k):
        l = mem_peer(k)
        to_mem(back.at[g], back.at[g], bk_s, bk_r, l).start()

    loads[4].wait()
    carries_in(zo, z_sem)

    def partial(l):
        y = smooth(
            [(alpha_of(l, half),) for half in range(2)], (de[0, l], de[1, l]),
            mt[l], pb[l], qb[l], kk[l, 0:COLS], kk[l, COLS : 2 * COLS],
        )
        acc = jnp.zeros((ROWS, COLS), F32)
        for m in range(2 * HALF):
            acc = acc + (live[m] * pert_v[m, l].astype(F32)) * y[ROWS * m : ROWS * m + ROWS]
        return acc

    @pl.loop(1, LEVELS + 1)
    def _(k):
        l = mem_peer(k)
        ps[l] = partial(l)

        @pl.when(l != g)
        def _():
            to_mem(ps.at[l], pr.at[g], rs_s, rs_r, l).start()

    pr[g] = ps[g]

    wait_all(back, bk_r, LEVELS)
    exports[4].start()

    def weighted(l, half):
        x = pert_v[HALF * half : HALF * half + HALF, l].astype(F32) * back[l].astype(F32)[None]
        return split(x.reshape(PACK, COLS))

    sources(weighted, za2, zr2, z2_sem, 0, 2)

    wait_all(pr, rs_r, LEVELS)
    acc = pr[0]
    for s in range(1, LEVELS):
        acc = acc + pr[s]
    acc = acc * scale
    for j in range(3):
        lq[pl.ds(j, ROWS, stride=3), :] = acc[:, 128 * j : 128 * j + 128]
    lows[...] = lq[...].astype(BF16)

    def low_rows(s):
        return low.at[s, pl.ds(0, QROWS), :]

    def low_to(s):
        return to_tile(lows, low_rows(t), lo_s, lo_r.at[t], s)

    def low_on(s):
        return to_tile(low_rows(s), low_rows(s), lo_f, lo_r.at[s], partner)

    @pl.loop(1, CHIPS)
    def _(k):
        low_to(tile_of(chip_peer(k))).start()

    low_to(partner).start()

    low[t, 0:QROWS, :] = lows[...]

    sources(weighted, za2, zr2, z2_sem, 2, 4)

    inc_v[...] = jnp.zeros((DROWS, 128), F32)

    @pl.loop(0, steps)
    def _(j):
        tiles = []
        for i in range(GROUP):
            n = GROUP * j + i
            afar = (n + TILES - 2) // TILES
            late = n // (CHIPS + 1)
            ch = chip_back(afar * (n - 1 - (CHIPS - 1) * late))
            s = 2 * ch + core + (late + (1 - afar) * lax.rem(n, 2)) * (1 - 2 * core)
            tiles.append(s)

            @pl.when(n > 0)
            def _():
                low_on(s).wait_recv()

            @pl.when((afar == 1) & (late == 0))
            def _():
                low_on(s).start()

        inc_v[...] += forward_terms(tiles)

        @pl.when(j == steps // 2 - 1)
        def _():
            recursion(zr2, zo2, de2, z2_sem)

    exports[6].start()
    carries_in(zo2, z2_sem)
    exports[5].start()

    carries_sent(zo, z_sem)
    carries_sent(zo2, z2_sem)
    pltpu.make_async_copy(sp, sp, sp_s).wait()
    wait_all(ss, ss_s, CHIPS)
    lows8 = low.at[pl.ds(0, CHIPS), pl.ds(0, QROWS), :]
    pltpu.make_async_copy(lows8, lows8, lo_s).wait()
    lows7 = low.at[pl.ds(0, CHIPS - 1), pl.ds(0, QROWS), :]
    pltpu.make_async_copy(lows7, lows7, lo_f).wait()
    wait_all(ps, rs_s, LEVELS)
    wait_all(back, bk_s, LEVELS)
    for x in exports:
        x.wait()


def shards(
    alpha, perturbation, cotangent, decay_y, decay_x, group_members, interp_weight,
    pair_count, src_index, dst_index,
):
    any_spec = pl.BlockSpec(memory_space=pl.ANY)
    vmem = pl.BlockSpec(memory_space=pltpu.VMEM)
    smem = pl.BlockSpec(memory_space=pltpu.SMEM)
    dma = pltpu.SemaphoreType.DMA
    V = pltpu.VMEM
    zbuf = V((TILES, 32, 128), F32)
    zpair = V((2, CHIPS, 32, 128), F32)
    zall = [zpair, zbuf, zbuf, zpair]
    scratch = [
        V((2 * HALF, LEVELS, ROWS, COLS), BF16),
        V((2 * HALF, LEVELS, ROWS, COLS), BF16),
        V((1, DROWS * 128), BF16),
        V((DROWS, 128), BF16),
        V((TILES, SLOTS, BLK, 128), BF16),
        V((TILES, SLOTS), jnp.int32),
        V((TILES, SLOTS), jnp.int32),
        V((8, 512), F32),
        V((LEVELS, 8, 512), F32),
        V((LEVELS, 2, COLS), F32),
        V((LEVELS, 8, COLS), F32),
        V((LEVELS, PACK, 512), BF16),
        V((LEVELS, 32, PACK), BF16),
        V((LEVELS, ROWS, 128), F32),
        V((LEVELS, ROWS, 128), F32),
        V((LEVELS, 2 * COLS, COLS), BF16),
        *zall,
        *zall,
        V((2, CHIPS, QROWS, 128), F32),
        V((CHIPS, QROWS, 128), F32),
        V((CHIPS, QROWS, 128), F32),
        V((CHIPS, QROWS, 128), F32),
        V((QROWS, 128), F32),
        V((LEVELS, ROWS, COLS), BF16),
        V((LEVELS, ROWS, COLS), F32),
        V((LEVELS, ROWS, COLS), F32),
        V((QROWS, 128), F32),
        V((TILES, 128, 128), BF16),
        V((QROWS, 128), BF16),
        V((DROWS, 128), F32),
        V((TILES, SLOTS, 128), jnp.int32),
        V((TILES, SLOTS, 128), jnp.int32),
        dma((5,)),
        dma((TILES,)),
        dma((7,)),
        dma((4,)),
        dma((4,)),
        dma,
        dma((CHIPS,)),
        *[dma] * 6,
        dma((TILES,)),
        dma,
        dma,
    ]
    shape = jax.ShapeDtypeStruct
    inc, *rest = pl.pallas_call(
        kernel,
        out_shape=(
            shape((DROWS, 128), F32),
            shape((LEVELS, ROWS, COLS), BF16),
            shape((2, CHIPS, 32, 128), F32),
            shape((LEVELS, PACK, 512), BF16),
            shape((LEVELS, ROWS, 128), F32),
            shape((LEVELS, ROWS, 128), F32),
            shape((LEVELS, COLS, COLS), BF16),
        ),
        in_specs=[any_spec, any_spec, any_spec, vmem, vmem, smem, any_spec, smem, any_spec, any_spec],
        out_specs=(any_spec,) * 7,
        scratch_shapes=scratch,
        compiler_params=pltpu.CompilerParams(
            collective_id=0, has_side_effects=True, vmem_limit_bytes=60 * 1024 * 1024
        ),
        cost_estimate=pl.CostEstimate(
            flops=9_000_000_000, bytes_accessed=29_000_000, transcendentals=700_000
        ),
    )(
        alpha, perturbation, cotangent, decay_y, decay_x, group_members,
        interp_weight, pair_count, src_index, dst_index,
    )

    members_shape = (2 * HALF, LEVELS, ROWS, COLS)
    return pl.pallas_call(
        grad_kernel,
        out_shape=(shape((1, DROWS * 128), F32), shape(alpha.shape, F32)),
        in_specs=[smem, *[any_spec] * 7, vmem],
        out_specs=(vmem, any_spec),
        scratch_shapes=[
            V(members_shape, BF16),
            V((LEVELS, ROWS, COLS), BF16),
            V((2, CHIPS, 32, 128), F32),
            V((LEVELS, PACK, 512), BF16),
            V((LEVELS, ROWS, 128), F32),
            V((LEVELS, ROWS, 128), F32),
            V((LEVELS, COLS, COLS), BF16),
            V(members_shape, F32),
            dma((4,)),
            dma((3, LEVELS)),
            dma((LEVELS,)),
        ],
        compiler_params=pltpu.CompilerParams(vmem_limit_bytes=60 * 1024 * 1024),
        cost_estimate=pl.CostEstimate(
            flops=3_500_000_000, bytes_accessed=11_000_000, transcendentals=0
        ),
    )(group_members, perturbation, *rest, inc)


def solution(mesh):
    in_specs = (
        P("mem", None, "tile", None),
        P("mem", None, "tile", None),
        P("mem", "tile"),
        P(None, "tile"),
        P(),
        P(),
        P("tile", None, None, None, None),
        P(),
        P(),
        P(),
    )
    out_specs = (P("mem", "tile"), P("mem", None, "tile", None))
    return jax.shard_map(shards, mesh=mesh, in_specs=in_specs, out_specs=out_specs, check_vma=False)
```
